32 devices in a mesh: dp: 8 (over y, x, core), tensor: 4 (over z).
Axes of the slice: x: 2, y: 2, z: 4, core: 2. Of those that a mesh axis runs over, the one named last changes fastest.
Arguments:
- tokens: bfloat16 [8192, 2048], P(('dp', 'tensor')), may hold values from -6 to 6
- segment_ids: int32 [8, 1024], P('dp'), may hold values from 0 to 3, never falling along the last dimension, each value on 1 to 512 neighbouring positions
- attn_gain: bfloat16 [2048], P('dp'), may hold values from 0.5 to 1.5
- w_query: bfloat16 [2048, 2048], P('dp', 'tensor'), may hold values from -0.125 to 0.125
- w_key: bfloat16 [2048, 2048], P('dp', 'tensor'), may hold values from -0.125 to 0.125
- w_value: bfloat16 [2048, 4096], P('dp', 'tensor'), may hold values from -0.125 to 0.125
- w_gate: bfloat16 [2048, 4096], P('dp', 'tensor'), may hold values from -0.125 to 0.125
- w_out: bfloat16 [2048, 4096], P('dp', 'tensor'), may hold values from -0.09375 to 0.09375
- mlp_gain: bfloat16 [2048], P('dp'), may hold values from 0.5 to 1.5
- w_mlp_gate: bfloat16 [2048, 4096], P('dp', 'tensor'), may hold values from -0.125 to 0.125
- w_mlp_up: bfloat16 [2048, 4096], P('dp', 'tensor'), may hold values from -0.125 to 0.125
- w_down: bfloat16 [2048, 4096], P('dp', 'tensor'), may hold values from -0.09375 to 0.09375
- cotangent: bfloat16 [8192, 2048], P(('dp', 'tensor')), may hold values from -6 to 6
Outputs:
- output: bfloat16 [8192, 2048], P(('dp', 'tensor'))
- tokens_grad: bfloat16 [8192, 2048], P(('dp', 'tensor'))
- attn_gain_grad: float32 [2048], P('dp')
- w_query_grad: float32 [2048, 2048], P('dp', 'tensor')
- w_key_grad: float32 [2048, 2048], P('dp', 'tensor')
- w_value_grad: float32 [2048, 4096], P('dp', 'tensor')
- w_gate_grad: float32 [2048, 4096], P('dp', 'tensor')
- w_out_grad: float32 [2048, 4096], P('dp', 'tensor')
- mlp_gain_grad: float32 [2048], P('dp')
- w_mlp_gate_grad: float32 [2048, 4096], P('dp', 'tensor')
- w_mlp_up_grad: float32 [2048, 4096], P('dp', 'tensor')
- w_down_grad: float32 [2048, 4096], P('dp', 'tensor')
The draws below stay inside these ranges and needn't reach their ends.
Inputs may be any that keep to these rules, and one draw needn't show every extreme that they name: `segment_ids`: along each sequence the document numbers never fall; a run of equal numbers is one document of at most 512 tokens, and one document of each sequence has exactly that length.
All inputs are finite; a program needn't handle non-finite values.
Results may differ from the reference program's by a relative error of at most 0.015.
Values may be sent and summed in bfloat16 or wider, within the bound.
A program may use at most 256 MiB of HBM per device.

```python
import math
import jax
import jax.numpy as jnp
import numpy as np
from jax import lax

D = 2048
HEADS = 8
KD = 256
VD = 512
FF = 4096
BLOCK = 512
DOCS = 4
SEQ_LEN = 1024
SEQS = 8
TOKENS = 8192


def with_spikes(drawn, key, source, target, parts, factor):
    def block_of(dim):
        return (jnp.arange(drawn.shape[dim]) // (drawn.shape[dim] // parts)).reshape((-1,) + (1,) * (drawn.ndim - 1 - dim))

    one_side = jax.random.permutation(key, parts)[block_of(target)]
    second = (block_of(target) + parts // 2) % parts
    return jnp.where((block_of(source) == one_side) | (block_of(source) == second), factor * drawn, drawn)


def shard_levels(own_key, shape, pieces, low, top_value):
    loudness, own = 1.0, jax.random.fold_in(own_key, 6)
    for axis_at, parts in pieces:
        steps = jnp.exp(jax.random.uniform(jax.random.fold_in(own, axis_at), (parts,), jnp.float32, low / len(pieces), top_value / len(pieces)))
        loudness = loudness * jnp.repeat(steps, shape[axis_at] // parts).reshape([-1 if axis == axis_at else 1 for axis in range(len(shape))])
    return loudness


def profile(amount, total, bound, lean):
    weights = [(1 << 20) // math.isqrt(grade ** lean) + 1 for grade in range(2, amount + 1)]
    surplus, holding = total - bound - (amount - 1), [1] * (amount - 1)
    while surplus > 0:
        free = [i for i in range(amount - 1) if holding[i] < bound]
        whole, budget = sum([weights[i] for i in free]), surplus
        for i in free:
            extra = min(bound - holding[i], max(1, budget * weights[i] // whole), surplus)
            holding[i] = holding[i] + extra
            surplus = surplus - extra
    return np.array([bound] + holding)


def ragged_sizes(rng, count, total, reach, slope):
    if count == 2:
        one = jax.random.randint(rng, (), max(1, total - reach), min(reach, total - 1) + 1)
        return jnp.stack([one, total - one])
    tallies = jnp.asarray(profile(count, total, reach, slope), jnp.int32)
    couples = (count - 1) // 2
    donor, taker = tallies[1:1 + 2 * couples:2], tallies[2:2 + 2 * couples:2]
    margin = jnp.minimum(donor - 1, reach - taker)
    passed = jax.random.randint(jax.random.fold_in(rng, 1), (couples,), 0, 1 << 20) % (margin + 1)
    tallies = tallies.at[1:1 + 2 * couples:2].set(donor - passed).at[2:2 + 2 * couples:2].set(taker + passed)
    return tallies[jax.random.permutation(jax.random.fold_in(rng, 2), count)]


def normal_values(stream_key, shape, spread, bound, pieces=(), kind=jnp.bfloat16):
    values = jax.random.normal(stream_key, shape, jnp.float32) * spread
    if len(pieces) > 0:
        values = shard_levels(stream_key, shape, pieces, -0.22, 0.18) * values
    return jnp.clip(values, min=-bound, max=bound).astype(kind)


def noise_with(rng, extent, scale, most, cuts, heavy, dtype=jnp.bfloat16):
    values = scale * jax.random.normal(rng, extent, jnp.float32)
    if cuts:
        values = values * shard_levels(rng, extent, cuts, -0.22, 0.18)
    return jnp.clip(with_spikes(values, jax.random.fold_in(rng, 3), *heavy), -most, most).astype(dtype)


def setup_inputs(seed: int = 0) -> dict:
    arg_keys = jax.random.split(jax.random.key(seed), 14)
    return {
        "tokens": noise_with(arg_keys[0], (TOKENS, D), 1.0, 6.0, ((0, 32),), (0, 1, 32, 2.75)),
        "segment_ids": jax.vmap(lambda own: jnp.searchsorted(jnp.cumsum(ragged_sizes(own, DOCS, SEQ_LEN, SEQ_LEN // 2, 0)), jnp.arange(SEQ_LEN), side="right"))(jax.random.split(arg_keys[1], SEQS)).reshape((SEQS, SEQ_LEN)).astype(jnp.int32),
        "attn_gain": jnp.clip(1.0 + 0.1 * jax.random.normal(arg_keys[2], (D,), jnp.float32), 0.5, 1.5).astype(jnp.bfloat16),
        "w_query": normal_values(arg_keys[3], (D, HEADS * KD), D ** -0.5, 0.125, ((0, 8), (1, 4))),
        "w_key": normal_values(arg_keys[4], (D, HEADS * KD), D ** -0.5, 0.125, ((0, 8), (1, 4))),
        "w_value": normal_values(arg_keys[5], (D, HEADS * VD), D ** -0.5, 0.125, ((0, 8), (1, 4))),
        "w_gate": normal_values(arg_keys[6], (D, HEADS * VD), D ** -0.5, 0.125, ((0, 8), (1, 4))),
        "w_out": normal_values(arg_keys[7], (D, HEADS * VD), (HEADS * VD) ** -0.5, 0.09375, ((0, 8), (1, 4))),
        "mlp_gain": jnp.clip(1.0 + 0.1 * jax.random.normal(arg_keys[8], (D,), jnp.float32), 0.5, 1.5).astype(jnp.bfloat16),
        "w_mlp_gate": normal_values(arg_keys[9], (D, FF), D ** -0.5, 0.125, ((0, 8), (1, 4))),
        "w_mlp_up": normal_values(arg_keys[10], (D, FF), D ** -0.5, 0.125, ((0, 8), (1, 4))),
        "w_down": normal_values(arg_keys[11], (D, FF), FF ** -0.5, 0.09375, ((0, 8), (1, 4))),
        "cotangent": noise_with(arg_keys[12], (TOKENS, D), 1.0, 6.0, ((0, 32),), (0, 1, 32, 2.75)),
    }


EPS_NORM = 1e-06
EPS_GROUP = 1.0
HIGHEST = lax.Precision.HIGHEST

@jax.custom_vjp
def low(v):
    return lax.optimization_barrier(v.astype(jnp.bfloat16)).astype(jnp.float32)

@jax.custom_vjp
def low_back(v):
    return v

def low_keep(v):
    return (low(v), None)

def low_pass(kept, grad):
    return (grad,)

def back_keep(v):
    return (v, None)

def back_low(kept, grad):
    return (low(grad),)
low.defvjp(low_keep, low_pass)
low_back.defvjp(back_keep, back_low)

def matmul(left_side, right_side):
    return jnp.dot(left_side, right_side, precision=HIGHEST, preferred_element_type=jnp.float32)

def matmul_t(left_side, right_side):
    return lax.dot_general(left_side, right_side, (((1,), (1,)), ((), ())), precision=HIGHEST, preferred_element_type=jnp.float32)

def normalize(row_block, gain_vec):
    inverse = lax.rsqrt(lax.optimization_barrier(jnp.mean(row_block * row_block, axis=-1, keepdims=True)) + EPS_NORM)
    return row_block * inverse * gain_vec

def rotary_tables(length, channel_count):
    positions = jnp.arange(length).astype(jnp.float32)[:, None]
    frequency = 10000.0 ** (-jnp.arange(channel_count // 2).astype(jnp.float32) * (2.0 / channel_count))
    angles = positions * frequency[None, :]
    angles = jnp.concatenate([angles, angles], axis=1)
    return (jnp.cos(angles), jnp.sin(angles))

def rotate(values, cosine_table, sine_table):
    half_width = values.shape[-1] // 2
    turned = jnp.concatenate([-values[..., half_width:], values[..., :half_width]], axis=-1)
    return values * cosine_table[:, None, :] + turned * sine_table[:, None, :]

def gated_norm(heads_out, gate_pre):
    average = lax.optimization_barrier(jnp.mean(heads_out, axis=-1, keepdims=True))
    centred = heads_out - average
    variance = lax.optimization_barrier(jnp.mean(centred * centred, axis=-1, keepdims=True))
    normed = centred * lax.rsqrt(variance + EPS_GROUP)
    return jax.nn.silu(gate_pre) * normed.reshape(gate_pre.shape)

def decay_mask(seg_rows, seg_columns, start_row, logdecay):
    row_ids = start_row + jnp.arange(seg_rows.shape[0]).astype(jnp.int32)
    col_ids = jnp.arange(seg_columns.shape[0]).astype(jnp.int32)
    distance = row_ids[:, None] - col_ids[None, :]
    allowed = (distance >= 0) & (seg_rows[:, None] == seg_columns[None, :])
    spans_float = jnp.maximum(distance, 0).astype(jnp.float32)
    return jnp.where(allowed[None], jnp.exp(logdecay[:, None, None] * spans_float[None]), 0.0)

def retention(queries, keys_rot, values, segments, logdecay):
    length = queries.shape[0]
    block_count = length // BLOCK
    starts = (jnp.arange(block_count) * BLOCK).astype(jnp.int32)
    query_blocks = queries.reshape(block_count, BLOCK, HEADS, KD)

    @jax.checkpoint
    def one_block(block_item):
        query_block, start_row = block_item
        scores = low_back(jnp.einsum('bhk,mhk->hbm', query_block, keys_rot, precision=HIGHEST))
        seg_rows = lax.dynamic_slice(segments, (start_row,), (BLOCK,))
        weights = low(scores * decay_mask(seg_rows, segments, start_row, logdecay))
        return jnp.einsum('hbm,mhv->bhv', weights, values, precision=HIGHEST)
    return lax.map(one_block, (query_blocks, starts)).reshape(length, HEADS, VD)

def layer(params, tokens_seq, segments):
    attn_gain, w_query, w_key, w_value, w_gate, w_out, mlp_gain, w_mlp_gate, w_mlp_up, w_down = params
    length = tokens_seq.shape[0]
    normed_one = low(normalize(tokens_seq, attn_gain))
    query_pre = low_back(matmul(normed_one, w_query)).reshape(length, HEADS, KD)
    key_pre = low_back(matmul(normed_one, w_key)).reshape(length, HEADS, KD)
    values = low(low_back(matmul(normed_one, w_value))).reshape(length, HEADS, VD)
    gate_pre = low_back(matmul(normed_one, w_gate))
    cosine_table, sine_table = rotary_tables(length, KD)
    queries = low(rotate(query_pre, cosine_table, sine_table))
    keys_rot = low(rotate(key_pre, cosine_table, sine_table) * KD ** (-0.5))
    logdecay = jnp.log(1.0 - 2.0 ** (-5.0 - jnp.arange(HEADS).astype(jnp.float32)))
    heads_out = low_back(retention(queries, keys_rot, values, segments, logdecay))
    mixed = low(gated_norm(heads_out, gate_pre))
    residual = tokens_seq + low_back(matmul_t(mixed, w_out))
    normed_two = low(normalize(residual, mlp_gain))
    hidden_gate = low_back(matmul(normed_two, w_mlp_gate))
    hidden_up = low_back(matmul(normed_two, w_mlp_up))
    hidden = low(jax.nn.gelu(hidden_gate, approximate=True) * hidden_up)
    return residual + low_back(matmul_t(hidden, w_down))

def reference(tokens, segment_ids, attn_gain, w_query, w_key, w_value, w_gate, w_out, mlp_gain, w_mlp_gate, w_mlp_up, w_down, cotangent):
    params = tuple((weight_arr.astype(jnp.float32) for weight_arr in (attn_gain, w_query, w_key, w_value, w_gate, w_out, mlp_gain, w_mlp_gate, w_mlp_up, w_down)))
    inputs = tokens.astype(jnp.float32).reshape(SEQS, SEQ_LEN, D)
    cotangents = cotangent.astype(jnp.float32).reshape(SEQS, SEQ_LEN, D)

    def one_sequence(totals, seq_item):
        tokens_seq, segments, cot_seq = seq_item
        result, pullback = jax.vjp(lambda weight_set, rows_in: layer(weight_set, rows_in, segments), params, tokens_seq)
        weight_grads, input_grad = pullback(cot_seq)
        totals = tuple((running + increment for running, increment in zip(totals, weight_grads)))
        return (totals, (result.astype(jnp.bfloat16), input_grad.astype(jnp.bfloat16)))
    zero_grads = tuple((jnp.zeros_like(weight_arr) for weight_arr in params))
    totals, (outputs, input_grads) = lax.scan(one_sequence, zero_grads, (inputs, segment_ids, cotangents))
    return (outputs.reshape(TOKENS, D), input_grads.reshape(TOKENS, D), totals[0], totals[1], totals[2], totals[3], totals[4], totals[5], totals[6], totals[7], totals[8], totals[9])
```

```python
import functools
import jax
import jax.numpy as jnp
from jax import lax
from jax.experimental import pallas as pl
from jax.experimental.pallas import tpu as pltpu
from jax.sharding import PartitionSpec as P

AXIS = "tensor"


def line_body(n, chunks, rs, ag, middle, n_in, n_out, *refs):
    ins, outs, scratch = refs[:n_in], refs[n_in : n_in + n_out], list(refs[n_in + n_out :])
    me = lax.axis_index(AXIS)
    last = n - 1
    lag = last if rs else 0
    if rs:
        part, ins = ins[0], ins[1:]
        up_buf, dn_buf, total, up_send, up_recv, dn_send, dn_recv = scratch[:7]
        scratch = scratch[7:]
        rows = up_buf.shape[1]
    if ag:
        full, outs = outs[0], outs[1:]
        own, ag_recv, ag_up, ag_dn, ag_here = scratch[:5]
        rows = own.shape[0]
    size = rows // chunks

    def cut(c, base=0):
        return pl.ds(pl.multiple_of(base + c * size, size), size)

    def send(src, dst, send_sem, recv_sem, to):
        return pltpu.make_async_remote_copy(
            src_ref=src,
            dst_ref=dst,
            send_sem=send_sem,
            recv_sem=recv_sem,
            device_id={AXIS: to},
            device_id_type=pl.DeviceIdType.MESH,
        )

    barrier = pltpu.get_barrier_semaphore()

    @pl.when(me > 0)
    def _():
        pl.semaphore_signal(barrier, inc=1, device_id={AXIS: me - 1}, device_id_type=pl.DeviceIdType.MESH)

    @pl.when(me < last)
    def _():
        pl.semaphore_signal(barrier, inc=1, device_id={AXIS: me + 1}, device_id_type=pl.DeviceIdType.MESH)

    pl.semaphore_wait(barrier, jnp.where((me > 0) & (me < last), 2, 1))

    def sum_copy(up, d, c):
        buf, s, r, to = (up_buf, up_send, up_recv, me + 1) if up else (dn_buf, dn_send, dn_recv, me - 1)
        ref = buf.at[d, cut(c)]
        return send(ref, ref, s.at[d, c], r.at[d, c], to)

    def sum_step(up, d, c):
        buf = up_buf if up else dn_buf
        first = 0 if up else last
        mine = part[cut(c, d * rows)]

        @pl.when(me == first)
        def _():
            buf[d, cut(c)] = mine

        @pl.when(me != first)
        def _():
            sum_copy(up, d, c).wait_recv()
            buf[d, cut(c)] = (buf[d, cut(c)].astype(jnp.float32) + mine.astype(jnp.float32)).astype(buf.dtype)

        sum_copy(up, d, c).start()

    def gather_copy(up, j, c, from_own=False):
        ref = full.at[cut(c, j * rows)]
        src = own.at[cut(c)] if from_own else ref
        return send(src, ref, (ag_up if up else ag_dn).at[j, c], ag_recv.at[j, c], me + 1 if up else me - 1)

    def here_copy(c):
        return pltpu.make_async_copy(own.at[cut(c)], full.at[cut(c, me * rows)], ag_here.at[c])

    def step(s, _):
        if rs:
            for up in (True, False):
                c = s - me if up else s - (last - me)
                for d in range(last, 0, -1) if up else range(last):

                    @pl.when((c >= 0) & (c < chunks) & ((me < d) if up else (me > d)))
                    def _(up=up, c=c, d=d):
                        sum_step(up, d, c)

        c_own = s - lag

        @pl.when((c_own >= 0) & (c_own < chunks))
        def _():
            c = c_own
            if rs:
                total[...] = part[cut(c, me * rows)].astype(jnp.float32)

                @pl.when(me > 0)
                def _():
                    sum_copy(True, me, c).wait_recv()
                    total[...] += up_buf[me, cut(c)].astype(jnp.float32)

                @pl.when(me < last)
                def _():
                    sum_copy(False, me, c).wait_recv()
                    total[...] += dn_buf[me, cut(c)].astype(jnp.float32)

                result = middle(cut(c), total[...], ins, outs)
            else:
                result = middle(cut(c), None, ins, outs)
            if ag:
                own[cut(c)] = result.astype(own.dtype)
                here_copy(c).start()

                @pl.when(me < last)
                def _():
                    gather_copy(True, me, c, True).start()

                @pl.when(me > 0)
                def _():
                    gather_copy(False, me, c, True).start()

        if ag:
            for t in range(1, last):
                c = s - lag - t
                for up in (True, False):
                    j = me - t if up else me + t

                    @pl.when((c >= 0) & (c < chunks) & (((j >= 0) & (me < last)) if up else ((j <= last) & (me > 0))))
                    def _(up=up, c=c, j=j):
                        gather_copy(up, j, c).wait_recv()
                        gather_copy(up, j, c).start()

        return 0

    lax.fori_loop(0, chunks + lag + (last - 1 if ag else 0), step, 0)

    def drain(c, _):
        if rs:
            for d in range(n):

                @pl.when(me < d)
                def _(d=d):
                    sum_copy(True, d, c).wait_send()

                @pl.when(me > d)
                def _(d=d):
                    sum_copy(False, d, c).wait_send()

        if ag:
            here_copy(c).wait()
            for j in range(n):

                @pl.when(((me == last) & (j < me)) | ((me == 0) & (j > me)))
                def _(j=j):
                    gather_copy(True, j, c).wait_recv()

                @pl.when((me < last) & (j <= me))
                def _(j=j):
                    gather_copy(True, j, c).wait_send()

                @pl.when((me > 0) & (j >= me))
                def _(j=j):
                    gather_copy(False, j, c).wait_send()

        return 0

    lax.fori_loop(0, chunks, drain, 0)


def line_pass(name, part, extras, extra_outs, middle, ag, chunks, collective_id, rows, width):
    n = lax.axis_size(AXIS)
    rs = part is not None
    size = rows // chunks
    vmem = pl.BlockSpec(memory_space=pltpu.VMEM)
    scratch = []
    sems = pltpu.SemaphoreType.DMA((n, chunks))
    if rs:
        scratch += [
            pltpu.VMEM((n, rows, width), jnp.bfloat16),
            pltpu.VMEM((n, rows, width), jnp.bfloat16),
            pltpu.VMEM((size, width), jnp.float32),
            sems, sems, sems, sems,
        ]
    if ag:
        scratch += [pltpu.VMEM((rows, width), jnp.bfloat16), sems, sems, sems, pltpu.SemaphoreType.DMA((chunks,))]
    operands = ([part] if rs else []) + list(extras)
    shapes = ([jax.ShapeDtypeStruct((n * rows, width), jnp.bfloat16)] if ag else []) + [
        jax.ShapeDtypeStruct((rows, width), kind) for kind in extra_outs
    ]
    specs = ([pl.BlockSpec(memory_space=pl.ANY)] if ag else []) + [vmem] * len(extra_outs)
    moved = rows * width * 2 * (n - 1)
    return pl.pallas_call(
        functools.partial(line_body, n, chunks, rs, ag, middle, len(operands), len(shapes)),
        out_shape=shapes,
        in_specs=[vmem] * len(operands),
        out_specs=specs,
        scratch_shapes=scratch,
        compiler_params=pltpu.CompilerParams(
            collective_id=collective_id, has_side_effects=True, vmem_limit_bytes=48 * 1024 * 1024
        ),
        cost_estimate=pl.CostEstimate(
            flops=0, bytes_accessed=moved * 40, transcendentals=0, remote_bytes_transferred=moved
        ),
        name=name,
    )(*operands)


HEADS = 8
KD = 256
VD = 512
BLOCK = 512


EPS_NORM = 1e-06
EPS_GROUP = 1.0
CONTRACT_ROWS = (((0,), (0,)), ((), ()))
CONTRACT_COLUMNS = (((1,), (1,)), ((), ()))


def inverse_rms(rows):
    return lax.rsqrt(jnp.mean(rows * rows, axis=-1, keepdims=True) + EPS_NORM)


def norm_pull(unit, inverse, d_unit):
    return inverse * (d_unit - unit * jnp.mean(d_unit * unit, axis=-1, keepdims=True))


def rotary_tables(length, channel_count):
    positions = jnp.arange(length).astype(jnp.float32)[:, None]
    frequency = 10000.0 ** (
        -jnp.arange(channel_count // 2).astype(jnp.float32) * (2.0 / channel_count)
    )
    angles = positions * frequency[None, :]
    angles = jnp.concatenate([angles, angles], axis=1)
    return (jnp.cos(angles), jnp.sin(angles))


def rotate(values, cosine_table, sine_table):
    half_width = values.shape[-1] // 2
    turned = jnp.concatenate([-values[..., half_width:], values[..., :half_width]], axis=-1)
    return values * cosine_table[:, None, :] + turned * sine_table[:, None, :]


def gated_norm(heads_out, gate_pre):
    average = jnp.mean(heads_out, axis=-1, keepdims=True)
    centred = heads_out - average
    variance = jnp.mean(centred * centred, axis=-1, keepdims=True)
    normed = centred * lax.rsqrt(variance + EPS_GROUP)
    return jax.nn.silu(gate_pre) * normed.reshape(gate_pre.shape)


def decay_mask(seg_rows, seg_columns, start_row, logdecay):
    row_ids = start_row + jnp.arange(seg_rows.shape[0])
    col_ids = jnp.arange(seg_columns.shape[0])
    distance = row_ids[:, None] - col_ids[None, :]
    allowed = (distance >= 0) & (seg_rows[:, None] == seg_columns[None, :])
    spans_float = jnp.maximum(distance, 0).astype(jnp.float32)
    return jnp.where(allowed[None], jnp.exp(logdecay[:, None, None] * spans_float[None]), 0.0)


def block_terms(queries, keys_rot, start_row, logdecay, segments):
    end_row = start_row + BLOCK
    decay = decay_mask(segments[start_row:end_row], segments[:end_row], start_row, logdecay)
    scores = jnp.einsum(
        "bhk,mhk->hbm",
        queries[start_row:end_row],
        keys_rot[:end_row],
        preferred_element_type=jnp.float32,
    )
    return (decay, (scores * decay).astype(jnp.bfloat16))


def residual_step(cut, summed, ins, outs):
    residual = ins[0][cut].astype(jnp.float32) + summed
    outs[0][cut] = residual
    return residual * inverse_rms(residual)


def d_residual_step(cut, summed, ins, outs):
    residual = ins[0][cut]
    inverse = inverse_rms(residual)
    d_residual = ins[1][cut].astype(jnp.float32) + norm_pull(residual * inverse, inverse, summed)
    outs[0][cut] = d_residual
    return d_residual


def tokens_step(cut, summed, ins, outs):
    inputs = ins[0][cut].astype(jnp.float32)
    inverse = inverse_rms(inputs)
    grad = ins[1][cut] + norm_pull(inputs * inverse, inverse, summed)
    outs[0][cut] = grad.astype(outs[0].dtype)


def shards(
    tokens,
    segment_ids,
    attn_gain,
    w_query,
    w_key,
    w_value,
    w_gate,
    w_out,
    mlp_gain,
    w_mlp_gate,
    w_mlp_up,
    w_down,
    cotangent,
):
    tensor_parts = lax.axis_size("tensor")
    local_rows, width = tokens.shape
    length = local_rows * tensor_parts
    heads_dev = HEADS // tensor_parts
    key_cols = heads_dev * KD
    value_cols = heads_dev * VD
    hidden_cols = w_mlp_gate.shape[1]
    segments = segment_ids[0]
    gain_one = attn_gain.astype(jnp.float32)[:, None]
    gain_two = mlp_gain.astype(jnp.float32)[:, None]

    def gather(own):
        return lax.all_gather(own, "dp", axis=0, tiled=True)

    def scaled(gain, weight):
        return (weight.astype(jnp.float32) * gain).astype(jnp.bfloat16)

    def scatter(grad):
        return lax.psum_scatter(grad.astype(jnp.bfloat16), "dp", scatter_dimension=0, tiled=True).astype(jnp.float32)

    w_in_own = jnp.concatenate([scaled(gain_one, w) for w in (w_query, w_key, w_value, w_gate)], axis=1)
    w_pair_own = jnp.concatenate([scaled(gain_two, w) for w in (w_mlp_gate, w_mlp_up)], axis=1)
    w_in = gather(w_in_own)
    rest = gather(jnp.concatenate([w_out, w_pair_own, w_down], axis=1))
    out_full = rest[:, :value_cols]
    w_pair = rest[:, value_cols : value_cols + 2 * hidden_cols]
    down_full = rest[:, value_cols + 2 * hidden_cols :]

    inputs = tokens.astype(jnp.float32)
    unit_own = (inputs * inverse_rms(inputs)).astype(jnp.bfloat16)
    (unit_one,) = line_pass(
        "gather_one", None, [unit_own], [], lambda cut, _, ins, outs: ins[0][cut], True, 4, 0, local_rows, width
    )
    d_branch_two = lax.all_gather(cotangent, "tensor", axis=0, tiled=True)
    projected = jnp.dot(unit_one, w_in, preferred_element_type=jnp.float32)
    query_pre = projected[:, :key_cols].reshape(length, heads_dev, KD)
    key_pre = projected[:, key_cols : 2 * key_cols].reshape(length, heads_dev, KD)
    values = (
        projected[:, 2 * key_cols : 2 * key_cols + value_cols]
        .reshape(length, heads_dev, VD)
        .astype(jnp.bfloat16)
    )
    gate_pre = projected[:, 2 * key_cols + value_cols :]
    cosine_table, sine_table = rotary_tables(length, KD)

    def turn_query(query_part):
        return rotate(query_part, cosine_table, sine_table)

    def turn_key(key_part):
        return rotate(key_part, cosine_table, sine_table) * KD ** (-0.5)

    queries = turn_query(query_pre).astype(jnp.bfloat16)
    keys_rot = turn_key(key_pre).astype(jnp.bfloat16)
    head_ids = lax.axis_index("tensor") * heads_dev + jnp.arange(heads_dev)
    logdecay = jnp.log(1.0 - 2.0 ** (-5.0 - head_ids.astype(jnp.float32)))
    pieces = []
    for block_index in range(length // BLOCK):
        start_row = block_index * BLOCK
        decay, weights = block_terms(queries, keys_rot, start_row, logdecay, segments)
        pieces.append(
            jnp.einsum(
                "hbm,mhv->bhv",
                weights,
                values[: start_row + BLOCK],
                preferred_element_type=jnp.float32,
            )
        )
    heads_out = jnp.concatenate(pieces, axis=0)
    mixed = gated_norm(heads_out, gate_pre).astype(jnp.bfloat16)

    part_out = lax.dot_general(
        mixed, out_full, CONTRACT_COLUMNS, preferred_element_type=jnp.float32
    ).astype(jnp.bfloat16)
    unit_two, residual = line_pass(
        "residual", part_out, [tokens], [jnp.float32], residual_step, True, 16, 1, local_rows, width
    )
    both_hidden = jnp.dot(unit_two, w_pair, preferred_element_type=jnp.float32)
    hidden_gate = both_hidden[:, :hidden_cols]
    hidden_up = both_hidden[:, hidden_cols:]
    hidden = (jax.nn.gelu(hidden_gate, approximate=True) * hidden_up).astype(jnp.bfloat16)
    part_down = lax.dot_general(
        hidden, down_full, CONTRACT_COLUMNS, preferred_element_type=jnp.float32
    ).astype(jnp.bfloat16)
    result = residual + lax.psum_scatter(part_down, "tensor", scatter_dimension=0, tiled=True).astype(jnp.float32)

    grad_down = lax.dot_general(
        d_branch_two, hidden, CONTRACT_ROWS, preferred_element_type=jnp.float32
    )
    d_hidden = jnp.dot(d_branch_two, down_full, preferred_element_type=jnp.float32)
    _, gelu_pull = jax.vjp(
        lambda gate_part, up_part: jax.nn.gelu(gate_part, approximate=True) * up_part,
        hidden_gate,
        hidden_up,
    )
    d_gate_hidden, d_up_hidden = gelu_pull(d_hidden)
    d_pair = jnp.concatenate([d_gate_hidden, d_up_hidden], axis=1).astype(jnp.bfloat16)
    grad_pair = lax.dot_general(
        unit_two, d_pair, CONTRACT_ROWS, preferred_element_type=jnp.float32
    )
    part_pair = lax.dot_general(
        d_pair, w_pair, CONTRACT_COLUMNS, preferred_element_type=jnp.float32
    ).astype(jnp.bfloat16)
    d_branch_one, d_residual = line_pass(
        "d_residual", part_pair, [residual, cotangent], [jnp.float32], d_residual_step, True, 16, 2, local_rows, width
    )
    down_grad = scatter(grad_down)
    pair_grad = scatter(grad_pair)

    grad_out = lax.dot_general(
        d_branch_one, mixed, CONTRACT_ROWS, preferred_element_type=jnp.float32
    )
    out_grad = scatter(grad_out)
    d_mixed = jnp.dot(d_branch_one, out_full, preferred_element_type=jnp.float32)
    _, gated_pull = jax.vjp(gated_norm, heads_out, gate_pre)
    d_heads_full, d_gate_pre = gated_pull(d_mixed)
    d_heads = d_heads_full.astype(jnp.bfloat16)
    d_query_parts = []
    d_keys = jnp.zeros((length, heads_dev, KD), jnp.float32)
    d_values = jnp.zeros((length, heads_dev, VD), jnp.float32)
    for block_index in range(length // BLOCK):
        start_row = block_index * BLOCK
        end_row = start_row + BLOCK
        decay, weights = block_terms(queries, keys_rot, start_row, logdecay, segments)
        d_probs = jnp.einsum(
            "bhv,mhv->hbm",
            d_heads[start_row:end_row],
            values[:end_row],
            preferred_element_type=jnp.float32,
        )
        d_scores = (d_probs * decay).astype(jnp.bfloat16)
        d_values = d_values.at[:end_row].add(
            jnp.einsum(
                "hbm,bhv->mhv",
                weights,
                d_heads[start_row:end_row],
                preferred_element_type=jnp.float32,
            )
        )
        d_query_parts.append(
            jnp.einsum(
                "hbm,mhk->bhk", d_scores, keys_rot[:end_row], preferred_element_type=jnp.float32
            )
        )
        d_keys = d_keys.at[:end_row].add(
            jnp.einsum(
                "hbm,bhk->mhk",
                d_scores,
                queries[start_row:end_row],
                preferred_element_type=jnp.float32,
            )
        )
    _, query_pull = jax.vjp(turn_query, query_pre)
    _, key_pull = jax.vjp(turn_key, key_pre)
    (d_query_pre,) = query_pull(jnp.concatenate(d_query_parts, axis=0))
    (d_key_pre,) = key_pull(d_keys)
    d_in = jnp.concatenate(
        [
            d_query_pre.reshape(length, key_cols),
            d_key_pre.reshape(length, key_cols),
            d_values.reshape(length, value_cols),
            d_gate_pre,
        ],
        axis=1,
    ).astype(jnp.bfloat16)
    grad_in = lax.dot_general(unit_one, d_in, CONTRACT_ROWS, preferred_element_type=jnp.float32)
    in_grad = scatter(grad_in)
    part_in = lax.dot_general(
        d_in, w_in, CONTRACT_COLUMNS, preferred_element_type=jnp.float32
    ).astype(jnp.bfloat16)
    (tokens_grad,) = line_pass(
        "tokens_grad", part_in, [tokens, d_residual], [jnp.bfloat16], tokens_step, False, 8, 3, local_rows, width
    )

    def gain_terms(weights, grads):
        return jnp.sum(weights.astype(jnp.float32) * grads, axis=1)

    gain_sums = lax.psum((gain_terms(w_in_own, in_grad), gain_terms(w_pair_own, pair_grad)), "tensor")
    in_grad = in_grad * gain_one
    pair_grad = pair_grad * gain_two
    return (
        result.astype(jnp.bfloat16),
        tokens_grad,
        gain_sums[0] / gain_one[:, 0],
        in_grad[:, :key_cols],
        in_grad[:, key_cols : 2 * key_cols],
        in_grad[:, 2 * key_cols : 2 * key_cols + value_cols],
        in_grad[:, 2 * key_cols + value_cols :],
        out_grad,
        gain_sums[1] / gain_two[:, 0],
        pair_grad[:, :hidden_cols],
        pair_grad[:, hidden_cols:],
        down_grad,
    )


def solution(mesh):
    return jax.shard_map(
        shards,
        mesh=mesh,
        in_specs=(
            P(("dp", "tensor"), None),
            P("dp", None),
            P("dp"),
            P("dp", "tensor"),
            P("dp", "tensor"),
            P("dp", "tensor"),
            P("dp", "tensor"),
            P("dp", "tensor"),
            P("dp"),
            P("dp", "tensor"),
            P("dp", "tensor"),
            P("dp", "tensor"),
            P(("dp", "tensor"), None),
        ),
        out_specs=(
            P(("dp", "tensor"), None),
            P(("dp", "tensor"), None),
            P("dp"),
            P("dp", "tensor"),
            P("dp", "tensor"),
            P("dp", "tensor"),
            P("dp", "tensor"),
            P("dp", "tensor"),
            P("dp"),
            P("dp", "tensor"),
            P("dp", "tensor"),
            P("dp", "tensor"),
        ),
        check_vma=False,
    )
```

```python
import functools
import jax
import jax.numpy as jnp
import numpy as np
from jax import lax
from jax.experimental import pallas as pl
from jax.experimental.pallas import tpu as pltpu
from jax.sharding import PartitionSpec as P

AXIS = "tensor"


def line_body(n, chunks, rs, ag, middle, n_in, n_out, *refs):
    ins, outs, scratch = refs[:n_in], refs[n_in : n_in + n_out], list(refs[n_in + n_out :])
    me = lax.axis_index(AXIS)
    last = n - 1
    lag = last if rs else 0
    if rs:
        part, ins = ins[0], ins[1:]
        up_buf, dn_buf, total, up_send, up_recv, dn_send, dn_recv = scratch[:7]
        scratch = scratch[7:]
        rows = up_buf.shape[1]
    if ag:
        full, outs = outs[0], outs[1:]
        own, ag_recv, ag_up, ag_dn, ag_here = scratch[:5]
        rows = own.shape[0]
    size = rows // chunks

    def cut(c, base=0):
        return pl.ds(pl.multiple_of(base + c * size, size), size)

    def send(src, dst, send_sem, recv_sem, to):
        return pltpu.make_async_remote_copy(
            src_ref=src,
            dst_ref=dst,
            send_sem=send_sem,
            recv_sem=recv_sem,
            device_id={AXIS: to},
            device_id_type=pl.DeviceIdType.MESH,
        )

    barrier = pltpu.get_barrier_semaphore()

    @pl.when(me > 0)
    def _():
        pl.semaphore_signal(barrier, inc=1, device_id={AXIS: me - 1}, device_id_type=pl.DeviceIdType.MESH)

    @pl.when(me < last)
    def _():
        pl.semaphore_signal(barrier, inc=1, device_id={AXIS: me + 1}, device_id_type=pl.DeviceIdType.MESH)

    pl.semaphore_wait(barrier, jnp.where((me > 0) & (me < last), 2, 1))

    def sum_copy(up, d, c):
        buf, s, r, to = (up_buf, up_send, up_recv, me + 1) if up else (dn_buf, dn_send, dn_recv, me - 1)
        ref = buf.at[d, cut(c)]
        return send(ref, ref, s.at[d, c], r.at[d, c], to)

    def sum_step(up, d, c):
        buf = up_buf if up else dn_buf
        first = 0 if up else last
        mine = part[cut(c, d * rows)]

        @pl.when(me == first)
        def _():
            buf[d, cut(c)] = mine

        @pl.when(me != first)
        def _():
            sum_copy(up, d, c).wait_recv()
            buf[d, cut(c)] = (buf[d, cut(c)].astype(jnp.float32) + mine.astype(jnp.float32)).astype(buf.dtype)

        sum_copy(up, d, c).start()

    def gather_copy(up, j, c, from_own=False):
        ref = full.at[cut(c, j * rows)]
        src = own.at[cut(c)] if from_own else ref
        return send(src, ref, (ag_up if up else ag_dn).at[j, c], ag_recv.at[j, c], me + 1 if up else me - 1)

    def here_copy(c):
        return pltpu.make_async_copy(own.at[cut(c)], full.at[cut(c, me * rows)], ag_here.at[c])

    def step(s, _):
        if rs:
            for up in (True, False):
                c = s - me if up else s - (last - me)
                for d in range(last, 0, -1) if up else range(last):

                    @pl.when((c >= 0) & (c < chunks) & ((me < d) if up else (me > d)))
                    def _(up=up, c=c, d=d):
                        sum_step(up, d, c)

        c_own = s - lag

        @pl.when((c_own >= 0) & (c_own < chunks))
        def _():
            c = c_own
            if rs:
                total[...] = part[cut(c, me * rows)].astype(jnp.float32)

                @pl.when(me > 0)
                def _():
                    sum_copy(True, me, c).wait_recv()
                    total[...] += up_buf[me, cut(c)].astype(jnp.float32)

                @pl.when(me < last)
                def _():
                    sum_copy(False, me, c).wait_recv()
                    total[...] += dn_buf[me, cut(c)].astype(jnp.float32)

                result = middle(cut(c), total[...], ins, outs)
            else:
                result = middle(cut(c), None, ins, outs)
            if ag:
                own[cut(c)] = result.astype(own.dtype)
                here_copy(c).start()

                @pl.when(me < last)
                def _():
                    gather_copy(True, me, c, True).start()

                @pl.when(me > 0)
                def _():
                    gather_copy(False, me, c, True).start()

        if ag:
            for t in range(1, last):
                c = s - lag - t
                for up in (True, False):
                    j = me - t if up else me + t

                    @pl.when((c >= 0) & (c < chunks) & (((j >= 0) & (me < last)) if up else ((j <= last) & (me > 0))))
                    def _(up=up, c=c, j=j):
                        gather_copy(up, j, c).wait_recv()
                        gather_copy(up, j, c).start()

        return 0

    lax.fori_loop(0, chunks + lag + (last - 1 if ag else 0), step, 0)

    def drain(c, _):
        if rs:
            for d in range(n):

                @pl.when(me < d)
                def _(d=d):
                    sum_copy(True, d, c).wait_send()

                @pl.when(me > d)
                def _(d=d):
                    sum_copy(False, d, c).wait_send()

        if ag:
            here_copy(c).wait()
            for j in range(n):

                @pl.when(((me == last) & (j < me)) | ((me == 0) & (j > me)))
                def _(j=j):
                    gather_copy(True, j, c).wait_recv()

                @pl.when((me < last) & (j <= me))
                def _(j=j):
                    gather_copy(True, j, c).wait_send()

                @pl.when((me > 0) & (j >= me))
                def _(j=j):
                    gather_copy(False, j, c).wait_send()

        return 0

    lax.fori_loop(0, chunks, drain, 0)


def line_pass(name, part, extras, extra_outs, middle, ag, chunks, collective_id, rows, width):
    n = lax.axis_size(AXIS)
    rs = part is not None
    size = rows // chunks
    vmem = pl.BlockSpec(memory_space=pltpu.VMEM)
    scratch = []
    sems = pltpu.SemaphoreType.DMA((n, chunks))
    if rs:
        scratch += [
            pltpu.VMEM((n, rows, width), jnp.bfloat16),
            pltpu.VMEM((n, rows, width), jnp.bfloat16),
            pltpu.VMEM((size, width), jnp.float32),
            sems, sems, sems, sems,
        ]
    if ag:
        scratch += [pltpu.VMEM((rows, width), jnp.bfloat16), sems, sems, sems, pltpu.SemaphoreType.DMA((chunks,))]
    operands = ([part] if rs else []) + list(extras)
    shapes = ([jax.ShapeDtypeStruct((n * rows, width), jnp.bfloat16)] if ag else []) + [
        jax.ShapeDtypeStruct((rows, width), kind) for kind in extra_outs
    ]
    specs = ([pl.BlockSpec(memory_space=pl.ANY)] if ag else []) + [vmem] * len(extra_outs)
    moved = rows * width * 2 * (n - 1)
    return pl.pallas_call(
        functools.partial(line_body, n, chunks, rs, ag, middle, len(operands), len(shapes)),
        out_shape=shapes,
        in_specs=[vmem] * len(operands),
        out_specs=specs,
        scratch_shapes=scratch,
        compiler_params=pltpu.CompilerParams(
            collective_id=collective_id, has_side_effects=True, vmem_limit_bytes=48 * 1024 * 1024
        ),
        cost_estimate=pl.CostEstimate(
            flops=0, bytes_accessed=moved * 40, transcendentals=0, remote_bytes_transferred=moved
        ),
        name=name,
    )(*operands)


HEADS = 8
KD = 256
VD = 512
ROWS = 256


EPS_NORM = 1e-06
EPS_GROUP = 1.0
CONTRACT_ROWS = (((0,), (0,)), ((), ()))
CONTRACT_COLUMNS = (((1,), (1,)), ((), ()))


def rotary_tables(length):
    positions = np.arange(length).astype(np.float32)[:, None]
    frequency = np.float32(10000.0) ** (-np.arange(KD // 2).astype(np.float32) * np.float32(2.0 / KD))
    angles = (positions * frequency[None, :]).astype(np.float32).astype(np.float64)
    return np.cos(angles).astype(np.float32), np.sin(angles).astype(np.float32)


def turn(rows, cosine, sine):
    low, high = rows[:, : KD // 2], rows[:, KD // 2 :]
    return jnp.concatenate([low * cosine - high * sine, high * cosine + low * sine], axis=1)


def dot(left, right, dims=(((1,), (0,)), ((), ()))):
    return lax.dot_general(left, right, dims, preferred_element_type=jnp.float32)


def head_decay(decay_ref, log_ref, head, reach):
    ahead = lax.broadcasted_iota(jnp.int32, decay_ref.shape, 0) - lax.broadcasted_iota(jnp.int32, decay_ref.shape, 1)
    distance = ahead + reach
    value = jnp.exp(log_ref[head] * jnp.maximum(distance, 0).astype(jnp.float32))
    decay_ref[...] = jnp.where(distance >= 0, value, 0.0)


def normed_heads(heads_out):
    centred = heads_out - jnp.mean(heads_out, axis=-1, keepdims=True)
    inverse = lax.rsqrt(jnp.mean(centred * centred, axis=-1, keepdims=True) + EPS_GROUP)
    return centred * inverse, inverse


def retention_body(block, reach, log_ref, proj, cosine, sine, seg_rows, seg_line, kept, mixed, keys, vals, decay):
    head, row = pl.program_id(0), pl.program_id(1)
    here = pl.ds(pl.multiple_of(reach + row * block, block), block)
    window = pl.ds(pl.multiple_of(row * block, block), reach + block)

    @pl.when(row == 0)
    def _():
        head_decay(decay, log_ref, head, reach)
        keys[:reach] = jnp.zeros((reach, KD), keys.dtype)
        vals[:reach] = jnp.zeros((reach, VD), vals.dtype)

    query = turn(proj[:, :KD], cosine[...], sine[...]).astype(jnp.bfloat16)
    key = (turn(proj[:, KD : 2 * KD], cosine[...], sine[...]) * KD ** (-0.5)).astype(jnp.bfloat16)
    value = proj[:, 2 * KD : 2 * KD + VD].astype(jnp.bfloat16)
    keys[here] = key
    vals[here] = value
    kept[:, :KD] = query
    kept[:, KD : 2 * KD] = key
    kept[:, 2 * KD :] = value
    weight = jnp.where(seg_rows[...] == seg_line[:, window], decay[...], 0.0)
    probs = (dot(query, keys[window], CONTRACT_COLUMNS) * weight).astype(jnp.bfloat16)
    normed, _ = normed_heads(dot(probs, vals[window]))
    mixed[...] = (jax.nn.silu(proj[:, 2 * KD + VD :]) * normed).astype(jnp.bfloat16)


def retention_pull_body(
    block, reach, log_ref, kept, gate, d_mixed, cosine, sine, seg_rows, seg_line, d_in, keys, vals, d_keys, d_vals, decay
):
    head, row = pl.program_id(0), pl.num_programs(1) - 1 - pl.program_id(1)
    mine = pl.ds(pl.multiple_of(row * block, block), block)
    here = pl.ds(pl.multiple_of(reach + row * block, block), block)
    window = pl.ds(pl.multiple_of(row * block, block), reach + block)

    @pl.when(pl.program_id(1) == 0)
    def _():
        head_decay(decay, log_ref, head, reach)
        keys[:reach] = jnp.zeros((reach, KD), keys.dtype)
        vals[:reach] = jnp.zeros((reach, VD), vals.dtype)
        keys[reach:] = kept[:, KD : 2 * KD]
        vals[reach:] = kept[:, 2 * KD :]
        d_keys[...] = jnp.zeros_like(d_keys)
        d_vals[...] = jnp.zeros_like(d_vals)

    query = kept[mine, :KD]
    weight = jnp.where(seg_rows[...] == seg_line[:, window], decay[...], 0.0)
    probs = (dot(query, keys[window], CONTRACT_COLUMNS) * weight).astype(jnp.bfloat16)
    normed, inverse = normed_heads(dot(probs, vals[window]))
    gate_pre, upstream = gate[...], d_mixed[...]
    opened = jax.nn.sigmoid(gate_pre)
    silu = gate_pre * opened
    d_in[:, 2 * KD + VD :] = (upstream * normed * (opened + silu * (1.0 - opened))).astype(jnp.bfloat16)
    e = upstream * silu
    d_heads = e - jnp.mean(e, axis=-1, keepdims=True) - normed * jnp.mean(e * normed, axis=-1, keepdims=True)
    d_heads = (d_heads * inverse).astype(jnp.bfloat16)
    d_scores = (dot(d_heads, vals[window], CONTRACT_COLUMNS) * weight).astype(jnp.bfloat16)
    d_vals[window] += dot(probs, d_heads, CONTRACT_ROWS)
    d_keys[window] += dot(d_scores, query, CONTRACT_ROWS)
    d_query = dot(d_scores, keys[window])
    d_in[:, :KD] = turn(d_query, cosine[...], -sine[...]).astype(jnp.bfloat16)
    d_in[:, KD : 2 * KD] = (turn(d_keys[here], cosine[...], -sine[...]) * KD ** (-0.5)).astype(jnp.bfloat16)
    d_in[:, 2 * KD : 2 * KD + VD] = d_vals[here].astype(jnp.bfloat16)


def retention_inputs(segments, heads):
    length = segments.shape[0]
    block = min(ROWS, length // 2)
    reach = length // 2
    head_ids = lax.axis_index("tensor") * heads + jnp.arange(heads)
    log_decay = jnp.log(1.0 - 2.0 ** (-5.0 - head_ids.astype(jnp.float32)))
    seg_line = jnp.concatenate([jnp.full((reach,), -1, jnp.int32), segments])[None, :]
    return block, reach, log_decay, segments[:, None], seg_line


def retention(projected, segments, heads):
    length = projected.shape[0]
    block, reach, log_decay, seg_rows, seg_line = retention_inputs(segments, heads)
    cosine, sine = rotary_tables(length)
    per_head = projected.shape[1] // heads
    table = pl.BlockSpec((block, KD // 2), lambda h, r: (r, 0))
    return pl.pallas_call(
        functools.partial(retention_body, block, reach),
        grid=(heads, length // block),
        in_specs=[
            pl.BlockSpec(memory_space=pltpu.SMEM),
            pl.BlockSpec((block, per_head), lambda h, r: (r, h)),
            table,
            table,
            pl.BlockSpec((block, 1), lambda h, r: (r, 0)),
            pl.BlockSpec(seg_line.shape, lambda h, r: (0, 0)),
        ],
        out_specs=[
            pl.BlockSpec((block, 2 * KD + VD), lambda h, r: (r, h)),
            pl.BlockSpec((block, VD), lambda h, r: (r, h)),
        ],
        out_shape=[
            jax.ShapeDtypeStruct((length, heads * (2 * KD + VD)), jnp.bfloat16),
            jax.ShapeDtypeStruct((length, heads * VD), jnp.bfloat16),
        ],
        scratch_shapes=[
            pltpu.VMEM((reach + length, KD), jnp.bfloat16),
            pltpu.VMEM((reach + length, VD), jnp.bfloat16),
            pltpu.VMEM((block, reach + block), jnp.float32),
        ],
        compiler_params=pltpu.CompilerParams(vmem_limit_bytes=48 * 1024 * 1024),
        cost_estimate=pl.CostEstimate(
            flops=heads * length * (reach + block) * (KD + VD) * 2, bytes_accessed=projected.size * 6, transcendentals=0
        ),
        name="retention",
    )(log_decay, projected, cosine, sine, seg_rows, seg_line)


def retention_pull(kept, projected, d_mixed, segments, heads):
    length = kept.shape[0]
    block, reach, log_decay, seg_rows, seg_line = retention_inputs(segments, heads)
    cosine, sine = rotary_tables(length)
    per_head = projected.shape[1] // heads
    last = length // block - 1
    gate_block = per_head // VD
    table = pl.BlockSpec((block, KD // 2), lambda h, r: (last - r, 0))
    return pl.pallas_call(
        functools.partial(retention_pull_body, block, reach),
        grid=(heads, last + 1),
        in_specs=[
            pl.BlockSpec(memory_space=pltpu.SMEM),
            pl.BlockSpec((length, 2 * KD + VD), lambda h, r: (0, h)),
            pl.BlockSpec((block, VD), lambda h, r: (last - r, gate_block * h + gate_block - 1)),
            pl.BlockSpec((block, VD), lambda h, r: (last - r, h)),
            table,
            table,
            pl.BlockSpec((block, 1), lambda h, r: (last - r, 0)),
            pl.BlockSpec(seg_line.shape, lambda h, r: (0, 0)),
        ],
        out_specs=pl.BlockSpec((block, per_head), lambda h, r: (last - r, h)),
        out_shape=jax.ShapeDtypeStruct(projected.shape, jnp.bfloat16),
        scratch_shapes=[
            pltpu.VMEM((reach + length, KD), jnp.bfloat16),
            pltpu.VMEM((reach + length, VD), jnp.bfloat16),
            pltpu.VMEM((reach + length, KD), jnp.float32),
            pltpu.VMEM((reach + length, VD), jnp.float32),
            pltpu.VMEM((block, reach + block), jnp.float32),
        ],
        compiler_params=pltpu.CompilerParams(vmem_limit_bytes=48 * 1024 * 1024),
        cost_estimate=pl.CostEstimate(
            flops=heads * length * (reach + block) * (3 * KD + 3 * VD) * 2, bytes_accessed=projected.size * 8, transcendentals=0
        ),
        name="retention_pull",
    )(log_decay, kept, projected, d_mixed, cosine, sine, seg_rows, seg_line)


def inverse_rms(rows):
    return lax.rsqrt(jnp.mean(rows * rows, axis=-1, keepdims=True) + EPS_NORM)


def norm_pull(unit, inverse, d_unit):
    return inverse * (d_unit - unit * jnp.mean(d_unit * unit, axis=-1, keepdims=True))


def residual_step(cut, summed, ins, outs):
    residual = ins[0][cut].astype(jnp.float32) + summed
    outs[0][cut] = residual
    return residual * inverse_rms(residual)


def d_residual_step(cut, summed, ins, outs):
    residual = ins[0][cut]
    inverse = inverse_rms(residual)
    d_residual = ins[1][cut].astype(jnp.float32) + norm_pull(residual * inverse, inverse, summed)
    outs[0][cut] = d_residual
    return d_residual


def tokens_step(cut, summed, ins, outs):
    inputs = ins[0][cut].astype(jnp.float32)
    inverse = inverse_rms(inputs)
    grad = ins[1][cut] + norm_pull(inputs * inverse, inverse, summed)
    outs[0][cut] = grad.astype(outs[0].dtype)


def hops(up):
    n = lax.axis_size(AXIS)
    return [(i, i + 1) if up else (i + 1, i) for i in range(n - 1)]


def steps_of(part, parts):
    n = lax.axis_size(AXIS)
    return range((n - 1) * part // parts, (n - 1) * (part + 1) // parts)


def gather_start(own):
    n, me = lax.axis_size(AXIS), lax.axis_index(AXIS)
    rows = own.shape[0]
    full = jnp.zeros(((n + 1) * rows,) + own.shape[1:], own.dtype)
    return own, own, lax.dynamic_update_slice_in_dim(full, own, me * rows, 0)


def gather_steps(state, steps):
    n, me = lax.axis_size(AXIS), lax.axis_index(AXIS)
    up, down, full = state
    rows = up.shape[0]
    for t in steps:
        up, down = lax.ppermute(up, AXIS, hops(True)), lax.ppermute(down, AXIS, hops(False))
        for arrived, j in ((up, me - t - 1), (down, me + t + 1)):
            full = lax.dynamic_update_slice_in_dim(full, arrived, jnp.where((j >= 0) & (j < n), j, n) * rows, 0)
    return up, down, full


def scatter_rows(part, j):
    n = lax.axis_size(AXIS)
    rows = part.shape[0] // n
    return lax.dynamic_slice_in_dim(part, jnp.clip(j, 0, n - 1) * rows, rows, 0).astype(jnp.float32)


def scatter_steps(state, part, steps):
    n, me = lax.axis_size(AXIS), lax.axis_index(AXIS)
    for t in steps:
        mine = scatter_rows(part, me + n - 1 - t), scatter_rows(part, me - n + 1 + t)
        if t:
            mine = [rows + sums.astype(jnp.float32) for rows, sums in zip(mine, state)]
        state = tuple(
            lax.ppermute(sums.astype(part.dtype), AXIS, hops(way)) for sums, way in zip(mine, (True, False))
        )
    return state


def shards(tokens,
    segment_ids,
    attn_gain,
    w_query,
    w_key,
    w_value,
    w_gate,
    w_out,
    mlp_gain,
    w_mlp_gate,
    w_mlp_up,
    w_down,
    cotangent,
):
    local_rows, width = tokens.shape
    heads = HEADS // lax.axis_size(AXIS)
    hidden_cols = w_mlp_gate.shape[1]
    segments = segment_ids[0]
    gain_one = attn_gain.astype(jnp.float32)[:, None]
    gain_two = mlp_gain.astype(jnp.float32)[:, None]
    after = lax.optimization_barrier

    def gather(own):
        return lax.all_gather(own, "dp", axis=0, tiled=True)

    def scaled(gain, weight):
        return (weight.astype(jnp.float32) * gain).astype(jnp.bfloat16)

    def scatter(grad):
        return lax.psum_scatter(grad, "dp", scatter_dimension=0, tiled=True)

    def by_head(query, key, value, gate):
        parts = []
        for head in range(heads):
            for array, columns in ((query, KD), (key, KD), (value, VD), (gate, VD)):
                parts.append(array[:, head * columns : (head + 1) * columns])
        return jnp.concatenate(parts, axis=1)

    def from_heads(array):
        found, at = ([], [], [], []), 0
        for _ in range(heads):
            for where, columns in zip(found, (KD, KD, VD, VD)):
                where.append(array[:, at : at + columns])
                at += columns
        return [jnp.concatenate(parts, axis=1) for parts in found]

    w_in_own = by_head(*[scaled(gain_one, w) for w in (w_query, w_key, w_value, w_gate)])
    w_pair_own = jnp.concatenate([scaled(gain_two, w) for w in (w_mlp_gate, w_mlp_up)], axis=1)
    mlp_own = jnp.concatenate([w_pair_own, w_down], axis=1)
    inputs = tokens.astype(jnp.float32)
    unit_own = (inputs * inverse_rms(inputs)).astype(jnp.bfloat16)
    w_in = gather(w_in_own)
    (unit_one,) = line_pass(
        "gather_one", None, [unit_own], [], lambda cut, _, ins, outs: ins[0][cut], True, 4, 0, local_rows, width
    )
    w_in, unit_one, w_out, cot_own = after((w_in, unit_one, w_out, cotangent))
    out_full = gather(w_out)
    cot = gather_steps(gather_start(cot_own), steps_of(0, 3))
    projected = dot(unit_one, w_in)
    projected, *cot = after((projected, *cot))
    cot = gather_steps(cot, steps_of(1, 3))
    kept, mixed = retention(projected, segments, heads)
    part_out = dot(mixed, out_full, CONTRACT_COLUMNS).astype(jnp.bfloat16)
    part_out, mlp_own, *cot = after((part_out, mlp_own, *cot))
    mlp_full = gather(mlp_own)
    unit_two, residual = line_pass(
        "residual", part_out, [tokens], [jnp.float32], residual_step, True, 16, 1, local_rows, width
    )
    unit_two, mlp_full, *cot = after((unit_two, mlp_full, *cot))
    w_pair, down_full = mlp_full[:, : 2 * hidden_cols], mlp_full[:, 2 * hidden_cols :]

    cot = gather_steps(cot, steps_of(2, 3))
    both_hidden = dot(unit_two, w_pair)
    hidden_gate, hidden_up = both_hidden[:, :hidden_cols], both_hidden[:, hidden_cols:]
    hidden = (jax.nn.gelu(hidden_gate, approximate=True) * hidden_up).astype(jnp.bfloat16)
    part_down = dot(hidden, down_full, CONTRACT_COLUMNS).astype(jnp.bfloat16)
    part_down, cot_full = after((part_down, cot[2]))
    cot_full = cot_full[: unit_two.shape[0]]

    sums = scatter_steps(None, part_down, steps_of(0, 3))
    grad_down = dot(cot_full, hidden, CONTRACT_ROWS).astype(jnp.bfloat16)
    d_hidden = dot(cot_full, down_full)
    _, gelu_pull = jax.vjp(
        lambda gate_part, up_part: jax.nn.gelu(gate_part, approximate=True) * up_part,
        hidden_gate,
        hidden_up,
    )
    d_pair = jnp.concatenate(gelu_pull(d_hidden), axis=1).astype(jnp.bfloat16)
    d_pair, grad_down, *sums = after((d_pair, grad_down, *sums))
    sums = scatter_steps(sums, part_down, steps_of(1, 3))
    grad_pair = dot(unit_two, d_pair, CONTRACT_ROWS).astype(jnp.bfloat16)
    part_pair = dot(d_pair, w_pair, CONTRACT_COLUMNS).astype(jnp.bfloat16)
    part_pair, grad_pair, grad_down, *sums = after((part_pair, grad_pair, grad_down, *sums))
    pair_grad = scatter(grad_pair)
    d_branch_one, d_residual = line_pass(
        "d_residual", part_pair, [residual, cotangent], [jnp.float32], d_residual_step, True, 16, 2, local_rows, width
    )
    d_branch_one, d_residual, pair_grad, grad_down, *sums = after((d_branch_one, d_residual, pair_grad, grad_down, *sums))

    down_grad = scatter(grad_down)
    sums = scatter_steps(sums, part_down, steps_of(2, 3))
    grad_out = dot(d_branch_one, mixed, CONTRACT_ROWS).astype(jnp.bfloat16)
    out_grad = scatter(grad_out)
    d_mixed = dot(d_branch_one, out_full)
    d_in = retention_pull(kept, projected, d_mixed, segments, heads)
    grad_in = dot(unit_one, d_in, CONTRACT_ROWS).astype(jnp.bfloat16)
    result = residual + sum(sums_in.astype(jnp.float32) for sums_in in sums) + scatter_rows(part_down, lax.axis_index(AXIS))
    result = result.astype(jnp.bfloat16)
    d_in, grad_in, result = after((d_in, grad_in, result))
    in_grad = scatter(grad_in)
    part_in = dot(d_in, w_in, CONTRACT_COLUMNS).astype(jnp.bfloat16)
    (tokens_grad,) = line_pass(
        "tokens_grad", part_in, [tokens, d_residual], [jnp.bfloat16], tokens_step, False, 8, 3, local_rows, width
    )

    def gain_terms(weights, grads):
        return jnp.sum(weights.astype(jnp.float32) * grads.astype(jnp.float32), axis=1)

    gain_sums = lax.psum((gain_terms(w_in_own, in_grad), gain_terms(w_pair_own, pair_grad)), AXIS)
    in_grads = [grad.astype(jnp.float32) * gain_one for grad in from_heads(in_grad)]
    pair_grad = pair_grad.astype(jnp.float32) * gain_two
    return (
        result,
        tokens_grad,
        gain_sums[0] / gain_one[:, 0],
        *in_grads,
        out_grad.astype(jnp.float32),
        gain_sums[1] / gain_two[:, 0],
        pair_grad[:, :hidden_cols],
        pair_grad[:, hidden_cols:],
        down_grad.astype(jnp.float32),
    )


def solution(mesh):
    return jax.shard_map(
        shards,
        mesh=mesh,
        in_specs=(
            P(("dp", "tensor"), None),
            P("dp", None),
            P("dp"),
            P("dp", "tensor"),
            P("dp", "tensor"),
            P("dp", "tensor"),
            P("dp", "tensor"),
            P("dp", "tensor"),
            P("dp"),
            P("dp", "tensor"),
            P("dp", "tensor"),
            P("dp", "tensor"),
            P(("dp", "tensor"), None),
        ),
        out_specs=(
            P(("dp", "tensor"), None),
            P(("dp", "tensor"), None),
            P("dp"),
            P("dp", "tensor"),
            P("dp", "tensor"),
            P("dp", "tensor"),
            P("dp", "tensor"),
            P("dp", "tensor"),
            P("dp"),
            P("dp", "tensor"),
            P("dp", "tensor"),
            P("dp", "tensor"),
        ),
        check_vma=False,
    )
```

```python
import functools
import jax
import jax.numpy as jnp
import numpy as np
from jax import lax
from jax.experimental import pallas as pl
from jax.experimental.pallas import tpu as pltpu
from jax.sharding import PartitionSpec as P

AXIS = "tensor"
TALL = 256
COLUMNS = 1024


def line_body(n, chunks, rs, ag, rolled, middle, square, n_in, n_out, *refs):
    ins, outs, scratch = refs[:n_in], refs[n_in : n_in + n_out], list(refs[n_in + n_out :])
    me = lax.axis_index(AXIS)
    last = n - 1
    lag = last if rs else 0
    greet, also, finish, steps = lambda barrier: 0, lambda s: None, lambda: None, 0
    if rs:
        here, load_sems, left_sems, right_sems = scratch[:n_in], *scratch[n_in : n_in + 3]
        scratch = scratch[n_in + 3 :]
        outside, (left, right) = ins, here[:2]
        groups = left.shape[0] // TALL
        rows, tall, wide = left.shape[0] // n, left.shape[0] // n // groups, min(COLUMNS, right.shape[0])

        def left_copy(g, j):
            at = pl.ds(j * rows + g * tall, tall)
            return pltpu.make_async_copy(outside[0].at[at], left.at[at], left_sems.at[g, j])

        def right_copy(q):
            at = pl.ds(pl.multiple_of(q * wide, wide), wide)
            return pltpu.make_async_copy(outside[1].at[at, pl.ds(0, right.shape[1])], right.at[at], right_sems.at[q])

        def later_copies():
            return [left_copy(g, j) for g in range(1, groups) for j in range(n)] + [
                pltpu.make_async_copy(outside[i], here[i], load_sems.at[i]) for i in range(2, n_in)
            ]

        for j in range(n):
            left_copy(0, j).start()
        for q in range(right.shape[0] // wide):
            right_copy(q).start()
        for copy in later_copies():
            copy.start()
        ins = here
    if square is not None:
        counts = square[1:]
        square_refs = ins[n_in - counts[0] :], outs[n_out - counts[1] :], scratch[len(scratch) - counts[2] :]
        ins, outs, scratch = ins[: n_in - counts[0]], outs[: n_out - counts[1]], scratch[: len(scratch) - counts[2]]
        greet, also, finish, steps = square[0](ins[0], *square_refs)
    if rs:
        ins = ins[2:]
        part, up_buf, dn_buf, total, up_send, up_recv, dn_send, dn_recv = scratch[:8]
        scratch = scratch[8:]
    if ag:
        full, outs = outs[0], outs[1:]
        own, ag_recv, ag_up, ag_dn, ag_here = scratch[:5]
        rows = own.shape[0]
    size = rows // chunks

    def cut(c, base=0):
        return pl.ds(pl.multiple_of(base + c * size, size), size)

    def slot(j, device, turned):
        return lax.rem(j - device + n, n) if turned else j

    def product(g):
        block = jnp.concatenate([left[pl.ds(pl.multiple_of(j * rows + g * tall, tall), tall)] for j in range(n)], axis=0)

        def tile(q, _):
            @pl.when(g == 0)
            def _():
                right_copy(q).wait()

            columns = pl.ds(pl.multiple_of(q * wide, wide), wide)
            found = lax.dot_general(block, right[columns], (((1,), (1,)), ((), ())), preferred_element_type=jnp.float32)
            for j in range(n):
                part[pl.ds(pl.multiple_of(j * rows + g * tall, tall), tall), columns] = found[
                    j * tall : (j + 1) * tall
                ].astype(part.dtype)
            return 0

        lax.fori_loop(0, right.shape[0] // wide, tile, 0)

    def send(src, dst, send_sem, recv_sem, to):
        return pltpu.make_async_remote_copy(
            src_ref=src,
            dst_ref=dst,
            send_sem=send_sem,
            recv_sem=recv_sem,
            device_id={AXIS: to},
            device_id_type=pl.DeviceIdType.MESH,
        )

    barrier = pltpu.get_barrier_semaphore()

    @pl.when(me > 0)
    def _():
        pl.semaphore_signal(barrier, inc=1, device_id={AXIS: me - 1}, device_id_type=pl.DeviceIdType.MESH)

    @pl.when(me < last)
    def _():
        pl.semaphore_signal(barrier, inc=1, device_id={AXIS: me + 1}, device_id_type=pl.DeviceIdType.MESH)

    others = greet(barrier)
    pl.semaphore_wait(barrier, jnp.where((me > 0) & (me < last), 2, 1) + others)

    def sum_copy(up, d, c):
        buf, s, r, to = (up_buf, up_send, up_recv, me + 1) if up else (dn_buf, dn_send, dn_recv, me - 1)
        ref = buf.at[d - up, cut(c)]
        return send(ref, ref, s.at[d, c], r.at[d, c], to)

    def sum_step(up, d, c):
        buf = up_buf if up else dn_buf
        first = 0 if up else last
        mine = part[cut(c, slot(d, me, rolled[0]) * rows)]

        @pl.when(me == first)
        def _():
            buf[d - up, cut(c)] = mine

        @pl.when(me != first)
        def _():
            sum_copy(up, d, c).wait_recv()
            buf[d - up, cut(c)] = (buf[d - up, cut(c)].astype(jnp.float32) + mine.astype(jnp.float32)).astype(buf.dtype)

        sum_copy(up, d, c).start()

    def gather_copy(up, j, c, from_own=False):
        to = me + 1 if up else me - 1
        src = own.at[cut(c)] if from_own else full.at[cut(c, slot(j, me, rolled[1]) * rows)]
        dst = full.at[cut(c, slot(j, to, rolled[1]) * rows)]
        return send(src, dst, (ag_up if up else ag_dn).at[j, c], ag_recv.at[j, c], to)

    def here_copy(c):
        return pltpu.make_async_copy(own.at[cut(c)], full.at[cut(c, slot(me, me, rolled[1]) * rows)], ag_here.at[c])

    def step(s, _):
        if rs:
            for up in (True, False):
                c = s - me if up else s - (last - me)
                for d in range(last, 0, -1) if up else range(last):

                    @pl.when((c >= 0) & (c < chunks) & ((me < d) if up else (me > d)))
                    def _(up=up, c=c, d=d):
                        sum_step(up, d, c)

            @pl.when(s == 0)
            def _():
                for copy in later_copies():
                    copy.wait()

            per_group = chunks // groups

            @pl.when((lax.rem(s, per_group) == 0) & (s + per_group < chunks))
            def _():
                product(s // per_group + 1)

        also(s)
        c_own = s - lag

        @pl.when((c_own >= 0) & (c_own < chunks))
        def _():
            c = c_own
            if rs:
                total[...] = part[cut(c, slot(me, me, rolled[0]) * rows)].astype(jnp.float32)

                @pl.when(me > 0)
                def _():
                    sum_copy(True, me, c).wait_recv()
                    total[...] += up_buf[me - 1, cut(c)].astype(jnp.float32)

                @pl.when(me < last)
                def _():
                    sum_copy(False, me, c).wait_recv()
                    total[...] += dn_buf[me, cut(c)].astype(jnp.float32)

                result = middle(cut(c), total[...], ins, outs)
            else:
                result = middle(cut(c), None, ins, outs)
            if ag:
                own[cut(c)] = result.astype(own.dtype)
                here_copy(c).start()

                @pl.when(me < last)
                def _():
                    gather_copy(True, me, c, True).start()

                @pl.when(me > 0)
                def _():
                    gather_copy(False, me, c, True).start()

        if ag:
            for t in range(1, last):
                c = s - lag - t
                for up in (True, False):
                    j = me - t if up else me + t

                    @pl.when((c >= 0) & (c < chunks) & (((j >= 0) & (me < last)) if up else ((j <= last) & (me > 0))))
                    def _(up=up, c=c, j=j):
                        gather_copy(up, j, c).wait_recv()
                        gather_copy(up, j, c).start()

        return 0

    if rs:
        for j in range(n):
            left_copy(0, j).wait()
        product(0)
    lax.fori_loop(0, max(chunks + lag + (last - 1 if ag else 0), steps), step, 0)
    finish()

    def drain(c, _):
        if rs:
            for d in range(n):

                @pl.when(me < d)
                def _(d=d):
                    sum_copy(True, d, c).wait_send()

                @pl.when(me > d)
                def _(d=d):
                    sum_copy(False, d, c).wait_send()

        if ag:
            here_copy(c).wait()
            for j in range(n):

                @pl.when(((me == last) & (j < me)) | ((me == 0) & (j > me)))
                def _(j=j):
                    gather_copy(True, j, c).wait_recv()

                @pl.when((me < last) & (j <= me))
                def _(j=j):
                    gather_copy(True, j, c).wait_send()

                @pl.when((me > 0) & (j >= me))
                def _(j=j):
                    gather_copy(False, j, c).wait_send()

        return 0

    lax.fori_loop(0, chunks, drain, 0)


def line_pass(name, summed, extras, extra_outs, middle, ag, chunks, collective_id, rows, width, rolled=(False, False), square=None, square_ins=(), square_outs=(), square_scratch=()):
    n = lax.axis_size(AXIS)
    rs = summed is not None
    size = rows // chunks
    vmem = pl.BlockSpec(memory_space=pltpu.VMEM)
    operands = (list(summed) if rs else []) + list(extras) + list(square_ins)
    scratch = []
    sems = pltpu.SemaphoreType.DMA((n, chunks))
    if rs:
        depth = summed[0].shape[1]
        shapes = [(n * rows, depth), (width, depth)] + [operand.shape for operand in operands[2:]]
        scratch += [pltpu.VMEM(shape, operand.dtype) for shape, operand in zip(shapes, operands)]
        scratch += [
            pltpu.SemaphoreType.DMA((len(operands),)),
            pltpu.SemaphoreType.DMA((n * rows // TALL, n)),
            pltpu.SemaphoreType.DMA((width // min(COLUMNS, width),)),
            pltpu.VMEM((n * rows, width), jnp.bfloat16),
            pltpu.VMEM((n - 1, rows, width), jnp.bfloat16),
            pltpu.VMEM((n - 1, rows, width), jnp.bfloat16),
            pltpu.VMEM((size, width), jnp.float32),
            sems, sems, sems, sems,
        ]
    if ag:
        scratch += [pltpu.VMEM((rows, width), jnp.bfloat16), sems, sems, sems, pltpu.SemaphoreType.DMA((chunks,))]
    shapes = ([jax.ShapeDtypeStruct((n * rows, width), jnp.bfloat16)] if ag else []) + [
        jax.ShapeDtypeStruct((rows, width), kind) for kind in extra_outs
    ] + list(square_outs)
    specs = ([pl.BlockSpec(memory_space=pl.ANY)] if ag else []) + [vmem] * (len(extra_outs) + len(square_outs))
    if square is not None:
        square = (square, len(square_ins), len(square_outs), len(square_scratch))
    moved = rows * width * 2 * (n - 1)
    return pl.pallas_call(
        functools.partial(line_body, n, chunks, rs, ag, rolled, middle, square, len(operands), len(shapes)),
        out_shape=shapes,
        in_specs=[pl.BlockSpec(memory_space=pl.ANY) if rs else vmem] * len(operands),
        out_specs=specs,
        scratch_shapes=scratch + list(square_scratch),
        compiler_params=pltpu.CompilerParams(
            collective_id=collective_id, has_side_effects=True, vmem_limit_bytes=(62 if square else 52 if rs else 16) * 1024 * 1024
        ),
        cost_estimate=pl.CostEstimate(
            flops=0, bytes_accessed=moved * 40, transcendentals=0, remote_bytes_transferred=moved
        ),
        name=name,
    )(*operands)


def flipped(index, bit):
    return index + (1 << bit) - 2 * (1 << bit) * lax.rem(index // (1 << bit), 2)


def square_parts(heads, left, ins, outs, scratch):
    turned, gain, weights = ins
    gain_sum, grads = outs[0], outs[1:]
    sums, sums_in, sums_send, sums_recv, sent, own, *rest = scratch
    line = lax.axis_index(AXIS)
    line_bits = lax.axis_size(AXIS).bit_length() - 1
    size = lax.axis_size("dp")
    bits = size.bit_length() - 1
    arrived, (first_send, first_recv), sems = rest[:bits], rest[bits : bits + 2], rest[bits + 2 :]
    me = lax.axis_index("dp")
    rows, wide = own.shape[2:]
    half = wide // 2
    pairs = arrived[0].shape[0]
    orders = list(range(bits - 1)), list(range(bits - 1))[::-1]

    def greet(barrier):
        for bit in range(bits):
            pl.semaphore_signal(barrier, inc=1, device_id={"dp": flipped(me, bit)}, device_id_type=pl.DeviceIdType.MESH)
        for bit in range(line_bits):
            pl.semaphore_signal(barrier, inc=1, device_id={AXIS: flipped(line, bit)}, device_id_type=pl.DeviceIdType.MESH)
        return bits + line_bits

    def sums_copy(bit):
        return pltpu.make_async_remote_copy(
            src_ref=sums.at[bit],
            dst_ref=sums_in.at[bit],
            send_sem=sums_send.at[bit],
            recv_sem=sums_recv.at[bit],
            device_id={AXIS: flipped(line, bit)},
            device_id_type=pl.DeviceIdType.MESH,
        )

    def send(src, dst, send_sem, recv_sem, bit):
        return pltpu.make_async_remote_copy(
            src_ref=src,
            dst_ref=dst,
            send_sem=send_sem,
            recv_sem=recv_sem,
            device_id={"dp": flipped(me, bit)},
            device_id_type=pl.DeviceIdType.MESH,
        )

    def first_copy(p, u):
        return send(sent.at[lax.rem(p, 2), u], arrived[0].at[p, u], first_send.at[p, u], first_recv.at[p, u], 0)

    def kept(side, stage):
        done = orders[side][: stage - 1]
        return [u for u in range(size // 2) if all(not u >> bit & 1 for bit in done)]

    def later_copies(p, side, stage):
        bit = orders[side][stage - 1]
        stay = kept(side, stage + 1)
        columns = pl.ds(side * half, half)
        send_sem, recv_sem = sems[2 * (stage - 1)], sems[2 * (stage - 1) + 1]
        return [
            send(
                arrived[0].at[p, u | 1 << bit, :, columns],
                arrived[stage].at[p, rank, :, columns],
                send_sem.at[p, side, rank],
                recv_sem.at[p, side, rank],
                bit + 1,
            )
            for rank, u in enumerate(stay)
        ]

    def multiply(p, u, odd):
        owner = me
        for bit in range(bits):
            set_bit = odd if bit == 0 else lax.rem(u // (1 << (bit - 1)), 2)
            owner = owner + set_bit * (1 << bit) * (1 - 2 * lax.rem(me // (1 << bit), 2))
        block = turned[pl.ds(pl.multiple_of(owner * rows, rows), rows)]
        columns = left[:, pl.ds(pl.multiple_of(p * wide, wide), wide)]
        return jnp.dot(block, columns, preferred_element_type=jnp.float32).astype(own.dtype)

    def also(s):
        @pl.when(s < pairs)
        def _():
            p = s

            @pl.when(p >= 2)
            def _():
                for u in range(size // 2):
                    first_copy(p - 2, u).wait_send()

            def to_send(u, _):
                sent[lax.rem(p, 2), u] = multiply(p, u, 1)
                first_copy(p, u).start()
                return 0

            def to_keep(u, _):
                own[lax.rem(p, 2), u] = multiply(p, u, 0)
                return 0

            lax.fori_loop(0, size // 2, to_send, 0)
            lax.fori_loop(0, size // 2, to_keep, 0)

        for stage in range(1, bits + 1):

            @pl.when((s >= stage) & (s < pairs + stage))
            def _(stage=stage):
                p = s - stage
                if stage == 1:
                    for u in range(size // 2):
                        first_copy(p, u).wait_recv()
                        summed = arrived[0][p, u].astype(jnp.float32) + own[lax.rem(p, 2), u].astype(jnp.float32)
                        arrived[0][p, u] = summed.astype(own.dtype)
                for side in range(2):
                    columns = pl.ds(side * half, half)
                    if stage > 1:
                        for copy in later_copies(p, side, stage - 1):
                            copy.wait_recv()
                        for rank, u in enumerate(kept(side, stage)):
                            summed = arrived[0][p, u, :, columns].astype(jnp.float32) + arrived[stage - 1][
                                p, rank, :, columns
                            ].astype(jnp.float32)
                            if stage < bits:
                                arrived[0][p, u, :, columns] = summed.astype(own.dtype)
                            else:
                                result(p, side, summed)
                    if stage < bits:
                        for copy in later_copies(p, side, stage):
                            copy.start()

        for bit in range(line_bits + 1):

            @pl.when(s == pairs + bits + bit)
            def _(bit=bit):
                if bit:
                    sums_copy(bit - 1).wait()
                    sums[bit] = sums[bit - 1] + sums_in[bit - 1]
                if bit < line_bits:
                    sums_copy(bit).start()
                else:
                    gain_sum[...] = sums[bit]

    def result(p, side, summed):
        at = pl.ds(pl.multiple_of(p * wide + side * half, half), half)
        terms = jnp.sum(summed * weights[:, at].astype(jnp.float32), axis=1, keepdims=True)
        terms = jnp.broadcast_to(terms, sums.shape[1:])
        if side:
            sums[0] += terms
        else:

            @pl.when(p == 0)
            def _():
                sums[0] = terms

            @pl.when(p > 0)
            def _():
                sums[0] += terms

        summed = summed * gain[...]
        for found in range(pairs):
            head, kind = found // (pairs // heads), found % (pairs // heads)
            where = grads[side] if kind == 0 else grads[1 + kind]
            start = head * half if kind == 0 else head * wide + side * half

            @pl.when(p == found)
            def _(where=where, start=start):
                where[:, start : start + half] = summed

    def finish():
        for p in range(max(pairs - 2, 0), pairs):
            for u in range(size // 2):
                first_copy(p, u).wait_send()

        def drain(p, _):
            for side in range(2):
                for stage in range(1, bits):
                    for copy in later_copies(p, side, stage):
                        copy.wait_send()
            return 0

        lax.fori_loop(0, pairs, drain, 0)

    return greet, also, finish, pairs + bits + line_bits + 1


def square_shapes(rows, heads, columns):
    size = lax.axis_size("dp")
    bits = size.bit_length() - 1
    wide = 2 * KD
    pairs = columns // wide
    sums = [pltpu.VMEM((pairs, size >> (stage + 1), rows, wide), jnp.bfloat16) for stage in range(bits)]
    sems = [pltpu.SemaphoreType.DMA((pairs, size // 2))] * 2
    for stage in range(1, bits):
        sems += [pltpu.SemaphoreType.DMA((pairs, 2, size >> (stage + 1)))] * 2
    outs = [jax.ShapeDtypeStruct((rows, 128), jnp.float32)]
    line_bits = lax.axis_size(AXIS).bit_length() - 1
    line_sems = pltpu.SemaphoreType.DMA((max(line_bits, 1),))
    line_scratch = [
        pltpu.VMEM((line_bits + 1, rows, 128), jnp.float32),
        pltpu.VMEM((max(line_bits, 1), rows, 128), jnp.float32),
        line_sems,
        line_sems,
    ]
    outs += [jax.ShapeDtypeStruct((rows, heads * cols), jnp.float32) for cols in (KD, KD, VD, VD)]
    return outs, line_scratch + [pltpu.VMEM((2, size // 2, rows, wide), jnp.bfloat16)] * 2 + sums + sems


def turn_parts(blocks, left, ins, outs, scratch):
    (rows_in,), (turned,) = ins, outs
    columns = rows_in.shape[1] // blocks

    def also(s):
        for block in range(blocks):

            @pl.when(s == block)
            def _(block=block):
                at = pl.ds(block * columns, columns)
                turned[at] = rows_in[:, at].T

    return lambda barrier: 0, also, lambda: None, blocks


HEADS = 8
KD = 256
VD = 512
ROWS = 256


EPS_NORM = 1e-06
EPS_GROUP = 1.0
CONTRACT_ROWS = (((0,), (0,)), ((), ()))
CONTRACT_COLUMNS = (((1,), (1,)), ((), ()))


def rotary_tables(length):
    positions = np.arange(length).astype(np.float32)[:, None]
    frequency = np.float32(10000.0) ** (-np.arange(KD // 2).astype(np.float32) * np.float32(2.0 / KD))
    angles = (positions * frequency[None, :]).astype(np.float32).astype(np.float64)
    return np.cos(angles).astype(np.float32), np.sin(angles).astype(np.float32)


def turn(rows, cosine, sine):
    low, high = rows[:, : KD // 2], rows[:, KD // 2 :]
    return jnp.concatenate([low * cosine - high * sine, high * cosine + low * sine], axis=1)


def dot(left, right, dims=(((1,), (0,)), ((), ()))):
    return lax.dot_general(left, right, dims, preferred_element_type=jnp.float32)


def head_decay(decay_ref, log_ref, head, reach):
    ahead = lax.broadcasted_iota(jnp.int32, decay_ref.shape, 0) - lax.broadcasted_iota(jnp.int32, decay_ref.shape, 1)
    distance = ahead + reach
    value = jnp.exp(log_ref[head] * jnp.maximum(distance, 0).astype(jnp.float32))
    decay_ref[...] = jnp.where(distance >= 0, value, 0.0)


def normed_heads(heads_out):
    centred = heads_out - jnp.mean(heads_out, axis=-1, keepdims=True)
    inverse = lax.rsqrt(jnp.mean(centred * centred, axis=-1, keepdims=True) + EPS_GROUP)
    return centred * inverse, inverse


def retention_body(block, reach, log_ref, proj, cosine, sine, seg_rows, seg_line, kept, mixed, keys, vals, decay):
    head, row = pl.program_id(0), pl.program_id(1)
    here = pl.ds(pl.multiple_of(reach + row * block, block), block)
    window = pl.ds(pl.multiple_of(row * block, block), reach + block)

    @pl.when(row == 0)
    def _():
        head_decay(decay, log_ref, head, reach)
        keys[:reach] = jnp.zeros((reach, KD), keys.dtype)
        vals[:reach] = jnp.zeros((reach, VD), vals.dtype)

    query = turn(proj[:, :KD], cosine[...], sine[...]).astype(jnp.bfloat16)
    key = (turn(proj[:, KD : 2 * KD], cosine[...], sine[...]) * KD ** (-0.5)).astype(jnp.bfloat16)
    value = proj[:, 2 * KD : 2 * KD + VD].astype(jnp.bfloat16)
    keys[here] = key
    vals[here] = value
    kept[:, :KD] = query
    kept[:, KD : 2 * KD] = key
    kept[:, 2 * KD :] = value
    weight = jnp.where(seg_rows[...] == seg_line[:, window], decay[...], 0.0)
    probs = (dot(query, keys[window], CONTRACT_COLUMNS) * weight).astype(jnp.bfloat16)
    normed, _ = normed_heads(dot(probs, vals[window]))
    mixed[...] = (jax.nn.silu(proj[:, 2 * KD + VD :]) * normed).astype(jnp.bfloat16)


def retention_pull_body(
    block, reach, log_ref, kept, gate, d_branch, w_out, cosine, sine, seg_rows, seg_line, d_in, keys, vals, d_keys, d_vals, decay
):
    head, row = pl.program_id(0), pl.num_programs(1) - 1 - pl.program_id(1)
    mine = pl.ds(pl.multiple_of(row * block, block), block)
    here = pl.ds(pl.multiple_of(reach + row * block, block), block)
    window = pl.ds(pl.multiple_of(row * block, block), reach + block)

    @pl.when(pl.program_id(1) == 0)
    def _():
        head_decay(decay, log_ref, head, reach)
        keys[:reach] = jnp.zeros((reach, KD), keys.dtype)
        vals[:reach] = jnp.zeros((reach, VD), vals.dtype)
        keys[reach:] = kept[:, KD : 2 * KD]
        vals[reach:] = kept[:, 2 * KD :]
        d_keys[...] = jnp.zeros_like(d_keys)
        d_vals[...] = jnp.zeros_like(d_vals)

    query = kept[mine, :KD]
    weight = jnp.where(seg_rows[...] == seg_line[:, window], decay[...], 0.0)
    probs = (dot(query, keys[window], CONTRACT_COLUMNS) * weight).astype(jnp.bfloat16)
    normed, inverse = normed_heads(dot(probs, vals[window]))
    gate_pre, upstream = gate[...], dot(d_branch[...], w_out[...])
    opened = jax.nn.sigmoid(gate_pre)
    silu = gate_pre * opened
    d_in[:, 2 * KD + VD :] = (upstream * normed * (opened + silu * (1.0 - opened))).astype(jnp.bfloat16)
    e = upstream * silu
    d_heads = e - jnp.mean(e, axis=-1, keepdims=True) - normed * jnp.mean(e * normed, axis=-1, keepdims=True)
    d_heads = (d_heads * inverse).astype(jnp.bfloat16)
    d_scores = (dot(d_heads, vals[window], CONTRACT_COLUMNS) * weight).astype(jnp.bfloat16)
    d_vals[window] += dot(probs, d_heads, CONTRACT_ROWS)
    d_keys[window] += dot(d_scores, query, CONTRACT_ROWS)
    d_query = dot(d_scores, keys[window])
    d_in[:, :KD] = turn(d_query, cosine[...], -sine[...]).astype(jnp.bfloat16)
    d_in[:, KD : 2 * KD] = (turn(d_keys[here], cosine[...], -sine[...]) * KD ** (-0.5)).astype(jnp.bfloat16)
    d_in[:, 2 * KD : 2 * KD + VD] = d_vals[here].astype(jnp.bfloat16)


def retention_inputs(segments, heads):
    length = segments.shape[0]
    block = min(ROWS, length // 2)
    reach = length // 2
    head_ids = lax.axis_index("tensor") * heads + jnp.arange(heads)
    log_decay = jnp.log(1.0 - 2.0 ** (-5.0 - head_ids.astype(jnp.float32)))
    seg_line = jnp.concatenate([jnp.full((reach,), -1, jnp.int32), segments])[None, :]
    return block, reach, log_decay, segments[:, None], seg_line


def retention(projected, segments, heads):
    length = projected.shape[0]
    block, reach, log_decay, seg_rows, seg_line = retention_inputs(segments, heads)
    cosine, sine = rotary_tables(length)
    per_head = projected.shape[1] // heads
    table = pl.BlockSpec((block, KD // 2), lambda h, r: (r, 0))
    return pl.pallas_call(
        functools.partial(retention_body, block, reach),
        grid=(heads, length // block),
        in_specs=[
            pl.BlockSpec(memory_space=pltpu.SMEM),
            pl.BlockSpec((block, per_head), lambda h, r: (r, h)),
            table,
            table,
            pl.BlockSpec((block, 1), lambda h, r: (r, 0)),
            pl.BlockSpec(seg_line.shape, lambda h, r: (0, 0)),
        ],
        out_specs=[
            pl.BlockSpec((block, 2 * KD + VD), lambda h, r: (r, h)),
            pl.BlockSpec((block, VD), lambda h, r: (r, h)),
        ],
        out_shape=[
            jax.ShapeDtypeStruct((length, heads * (2 * KD + VD)), jnp.bfloat16),
            jax.ShapeDtypeStruct((length, heads * VD), jnp.bfloat16),
        ],
        scratch_shapes=[
            pltpu.VMEM((reach + length, KD), jnp.bfloat16),
            pltpu.VMEM((reach + length, VD), jnp.bfloat16),
            pltpu.VMEM((block, reach + block), jnp.float32),
        ],
        compiler_params=pltpu.CompilerParams(vmem_limit_bytes=48 * 1024 * 1024),
        cost_estimate=pl.CostEstimate(
            flops=heads * length * (reach + block) * (KD + VD) * 2, bytes_accessed=projected.size * 6, transcendentals=0
        ),
        name="retention",
    )(log_decay, projected, cosine, sine, seg_rows, seg_line)


def retention_pull(kept, projected, d_branch, w_out, segments, heads):
    length = kept.shape[0]
    block, reach, log_decay, seg_rows, seg_line = retention_inputs(segments, heads)
    cosine, sine = rotary_tables(length)
    per_head = projected.shape[1] // heads
    last = length // block - 1
    gate_block = per_head // VD
    table = pl.BlockSpec((block, KD // 2), lambda h, r: (last - r, 0))
    return pl.pallas_call(
        functools.partial(retention_pull_body, block, reach),
        grid=(heads, last + 1),
        in_specs=[
            pl.BlockSpec(memory_space=pltpu.SMEM),
            pl.BlockSpec((length, 2 * KD + VD), lambda h, r: (0, h)),
            pl.BlockSpec((block, VD), lambda h, r: (last - r, gate_block * h + gate_block - 1)),
            pl.BlockSpec((block, d_branch.shape[1]), lambda h, r: (last - r, 0)),
            pl.BlockSpec((w_out.shape[0], VD), lambda h, r: (0, h)),
            table,
            table,
            pl.BlockSpec((block, 1), lambda h, r: (last - r, 0)),
            pl.BlockSpec(seg_line.shape, lambda h, r: (0, 0)),
        ],
        out_specs=pl.BlockSpec((block, per_head), lambda h, r: (last - r, h)),
        out_shape=jax.ShapeDtypeStruct(projected.shape, jnp.bfloat16),
        scratch_shapes=[
            pltpu.VMEM((reach + length, KD), jnp.bfloat16),
            pltpu.VMEM((reach + length, VD), jnp.bfloat16),
            pltpu.VMEM((reach + length, KD), jnp.float32),
            pltpu.VMEM((reach + length, VD), jnp.float32),
            pltpu.VMEM((block, reach + block), jnp.float32),
        ],
        compiler_params=pltpu.CompilerParams(vmem_limit_bytes=48 * 1024 * 1024),
        cost_estimate=pl.CostEstimate(
            flops=heads * length * (reach + block) * (3 * KD + 3 * VD) * 2, bytes_accessed=projected.size * 8, transcendentals=0
        ),
        name="retention_pull",
    )(log_decay, kept, projected, d_branch, w_out, cosine, sine, seg_rows, seg_line)


def inverse_rms(rows):
    return lax.rsqrt(jnp.mean(rows * rows, axis=-1, keepdims=True) + EPS_NORM)


def norm_pull(unit, inverse, d_unit):
    return inverse * (d_unit - unit * jnp.mean(d_unit * unit, axis=-1, keepdims=True))


def unit_step(cut, summed, ins, outs):
    inputs = ins[0][cut].astype(jnp.float32)
    return inputs * inverse_rms(inputs)


def residual_step(cut, summed, ins, outs):
    residual = ins[0][cut].astype(jnp.float32) + summed
    outs[0][cut] = residual
    return residual * inverse_rms(residual)


def d_residual_step(cut, summed, ins, outs):
    residual = ins[0][cut]
    inverse = inverse_rms(residual)
    d_residual = ins[1][cut].astype(jnp.float32) + norm_pull(residual * inverse, inverse, summed)
    outs[0][cut] = d_residual
    return d_residual


def tokens_step(cut, summed, ins, outs):
    inputs = ins[0][cut].astype(jnp.float32)
    inverse = inverse_rms(inputs)
    grad = ins[1][cut] + norm_pull(inputs * inverse, inverse, summed)
    outs[0][cut] = grad.astype(outs[0].dtype)


def hops(up):
    n = lax.axis_size(AXIS)
    return [(i, i + 1) if up else (i + 1, i) for i in range(n - 1)]


def joined_body(parts, plain, *refs):
    *arrays, gain, out = refs
    at = 0
    for array, index, columns in parts:
        found = arrays[array][:, index * columns : (index + 1) * columns]
        if array < len(arrays) - plain:
            found = (found.astype(jnp.float32) * gain[...]).astype(out.dtype)
        out[:, at : at + columns] = found
        at += columns


def joined(name, arrays, gain, parts, plain=0):
    columns = sum(part[2] for part in parts)
    return pl.pallas_call(
        functools.partial(joined_body, parts, plain),
        out_shape=jax.ShapeDtypeStruct((gain.shape[0], columns), arrays[0].dtype),
        compiler_params=pltpu.CompilerParams(vmem_limit_bytes=16 * 1024 * 1024),
        name=name,
    )(*arrays, gain)


def steps_of(part, parts):
    n = lax.axis_size(AXIS)
    return range((n - 1) * part // parts, (n - 1) * (part + 1) // parts)


def gather_steps(state, steps):
    for _ in steps:
        up, down = state[-2:]
        state = [*state, lax.ppermute(up, AXIS, hops(True)), lax.ppermute(down, AXIS, hops(False))]
    return state


def gather_end(state):
    n, me = lax.axis_size(AXIS), lax.axis_index(AXIS)
    ups, downs = state[::2], state[1::2]
    return jnp.concatenate([ups[0]] + [jnp.where(me + k < n, downs[k], ups[n - k]) for k in range(1, n)], axis=0)


def scatter_steps(state, part, steps):
    n = lax.axis_size(AXIS)
    rows = part.shape[0] // n
    for t in steps:
        mine = [part[k * rows : (k + 1) * rows].astype(jnp.float32) for k in (n - 1 - t, 1 + t)]
        if t:
            mine = [own + sums.astype(jnp.float32) for own, sums in zip(mine, state)]
        state = [lax.ppermute(sums.astype(part.dtype), AXIS, hops(way)) for sums, way in zip(mine, (True, False))]
    return state


def line_sum(value):
    n, step = lax.axis_size(AXIS), 1
    while step < n:
        value = value + lax.ppermute(value, AXIS, [(i, i ^ step) for i in range(n)])
        step *= 2
    return value


def shards(tokens,
    segment_ids,
    attn_gain,
    w_query,
    w_key,
    w_value,
    w_gate,
    w_out,
    mlp_gain,
    w_mlp_gate,
    w_mlp_up,
    w_down,
    cotangent,
):
    local_rows, width = tokens.shape
    heads = HEADS // lax.axis_size(AXIS)
    hidden_cols = w_mlp_gate.shape[1]
    segments = segment_ids[0]
    gain_one = attn_gain.astype(jnp.float32)[:, None]
    gain_two = mlp_gain.astype(jnp.float32)[:, None]
    after = lax.optimization_barrier

    def gather(own):
        return lax.all_gather(own, "dp", axis=0, tiled=True)

    def scatter(grad):
        return lax.psum_scatter(grad, "dp", scatter_dimension=0, tiled=True)

    def gain_terms(weights, grads):
        return jnp.sum(weights.astype(jnp.float32) * grads.astype(jnp.float32), axis=1)

    in_parts = [(array, head, columns) for head in range(heads) for array, columns in enumerate((KD, KD, VD, VD))]
    w_in_own = joined("join_in", [w_query, w_key, w_value, w_gate], gain_one, in_parts)
    mlp_own = joined("join_mlp", [w_mlp_gate, w_mlp_up, w_down], gain_two, [(i, 0, hidden_cols) for i in range(3)], 1)
    w_in = gather(w_in_own)
    (unit_one,) = line_pass(
        "gather_one", None, [tokens], [], unit_step, True, 4, 0, local_rows, width
    )
    w_in, unit_one, w_out, cot_own, mlp_own = after((w_in, unit_one, w_out, cotangent, mlp_own))
    out_full = gather(w_out)
    cot = gather_steps([cot_own, cot_own], steps_of(0, 3))
    projected = dot(unit_one, w_in)
    projected, *cot = after((projected, *cot))
    cot = gather_steps(cot, steps_of(1, 3))
    kept, mixed = retention(projected, segments, heads)
    mixed, out_full, mlp_send, *cot = after((mixed, out_full, mlp_own, *cot))
    mlp_full = gather(mlp_send)
    unit_two, residual, unit_turned = line_pass(
        "residual",
        (mixed, out_full),
        [tokens],
        [jnp.float32],
        residual_step,
        True,
        16,
        1,
        local_rows,
        width,
        (False, True),
        square=functools.partial(turn_parts, 8),
        square_ins=[unit_one],
        square_outs=[jax.ShapeDtypeStruct(unit_one.shape[::-1], unit_one.dtype)],
    )
    unit_two, mlp_full, *cot = after((unit_two, mlp_full, *cot))
    w_pair, down_full = mlp_full[:, : 2 * hidden_cols], mlp_full[:, 2 * hidden_cols :]

    cot = gather_steps(cot, steps_of(2, 3))
    both_hidden = dot(unit_two, w_pair)
    hidden_gate, hidden_up = both_hidden[:, :hidden_cols], both_hidden[:, hidden_cols:]
    hidden = (jax.nn.gelu(hidden_gate, approximate=True) * hidden_up).astype(jnp.bfloat16)
    part_down = dot(hidden, down_full, CONTRACT_COLUMNS).astype(jnp.bfloat16)
    part_down, *cot = after((part_down, *cot))
    cot_full = gather_end(cot)

    sums = scatter_steps(None, part_down, steps_of(0, 3))
    grad_down = dot(cot_full, hidden, CONTRACT_ROWS).astype(jnp.bfloat16)
    d_hidden = dot(cot_full, down_full)
    _, gelu_pull = jax.vjp(
        lambda gate_part, up_part: jax.nn.gelu(gate_part, approximate=True) * up_part,
        hidden_gate,
        hidden_up,
    )
    d_pair = jnp.concatenate(gelu_pull(d_hidden), axis=1).astype(jnp.bfloat16)
    d_pair, grad_down, *sums = after((d_pair, grad_down, *sums))
    down_grad = scatter(grad_down)
    sums = scatter_steps(sums, part_down, steps_of(1, 3))
    grad_pair = dot(unit_two, d_pair, CONTRACT_ROWS).astype(jnp.bfloat16)
    d_pair, grad_pair, *sums = after((d_pair, grad_pair, *sums))
    pair_grad = scatter(grad_pair)
    d_branch_one, d_residual = line_pass(
        "d_residual", (d_pair, mlp_full), [residual, cotangent], [jnp.float32], d_residual_step, True, 16, 2, local_rows, width, (True, False)
    )
    d_branch_one, d_residual, pair_grad, down_grad, *sums = after((d_branch_one, d_residual, pair_grad, down_grad, *sums))

    sums = scatter_steps(sums, part_down, steps_of(2, 3))
    grad_out = dot(d_branch_one, mixed, CONTRACT_ROWS).astype(jnp.bfloat16)
    out_grad = scatter(grad_out)
    d_in = retention_pull(kept, projected, d_branch_one, out_full, segments, heads)
    result = residual + part_down[:local_rows].astype(jnp.float32) + sum(arrived.astype(jnp.float32) for arrived in sums)
    result = result.astype(jnp.bfloat16)
    gain_sum_two = line_sum(gain_terms(mlp_own[:, : 2 * hidden_cols], pair_grad)) / gain_two[:, 0]
    pair_grad = pair_grad.astype(jnp.float32) * gain_two
    gate_grad, up_grad = pair_grad[:, :hidden_cols], pair_grad[:, hidden_cols:]
    down_grad = down_grad.astype(jnp.float32)
    d_in, result, gain_sum_two, gate_grad, up_grad, down_grad = after(
        (d_in, result, gain_sum_two, gate_grad, up_grad, down_grad)
    )
    square_outs, square_scratch = square_shapes(gain_one.shape[0], heads, w_in.shape[1])
    tokens_grad, gain_sum_one, *in_grads = line_pass(
        "tokens_grad",
        (d_in, w_in),
        [tokens, d_residual],
        [jnp.bfloat16],
        tokens_step,
        False,
        8,
        3,
        local_rows,
        width,
        square=functools.partial(square_parts, heads),
        square_ins=[unit_turned, gain_one, w_in_own],
        square_outs=square_outs,
        square_scratch=square_scratch,
    )
    gain_sum_one = gain_sum_one[:, 0] / gain_one[:, 0]
    return (
        result,
        tokens_grad,
        gain_sum_one,
        *in_grads,
        out_grad.astype(jnp.float32),
        gain_sum_two,
        gate_grad,
        up_grad,
        down_grad,
    )


def solution(mesh):
    return jax.shard_map(
        shards,
        mesh=mesh,
        in_specs=(
            P(("dp", "tensor"), None),
            P("dp", None),
            P("dp"),
            P("dp", "tensor"),
            P("dp", "tensor"),
            P("dp", "tensor"),
            P("dp", "tensor"),
            P("dp", "tensor"),
            P("dp"),
            P("dp", "tensor"),
            P("dp", "tensor"),
            P("dp", "tensor"),
            P(("dp", "tensor"), None),
        ),
        out_specs=(
            P(("dp", "tensor"), None),
            P(("dp", "tensor"), None),
            P("dp"),
            P("dp", "tensor"),
            P("dp", "tensor"),
            P("dp", "tensor"),
            P("dp", "tensor"),
            P("dp", "tensor"),
            P("dp"),
            P("dp", "tensor"),
            P("dp", "tensor"),
            P("dp", "tensor"),
        ),
        check_vma=False,
    )
```

```python
import functools
import math
import jax
import jax.numpy as jnp
import numpy as np
from jax import lax
from jax.experimental import pallas as pl
from jax.experimental.pallas import tpu as pltpu
from jax.sharding import PartitionSpec as P

AXIS = "tensor"
TALL = 256
COLUMNS = 1024
VMEM = 62 * 1024 * 1024


def line_body(n, chunks, rs, ag, rolled, middle, square, n_in, n_out, *refs):
    ins, outs, scratch = refs[:n_in], refs[n_in : n_in + n_out], list(refs[n_in + n_out :])
    me = lax.axis_index(AXIS)
    last = n - 1
    lag = last if rs else 0
    greet, also, finish, steps = lambda barrier: 0, lambda s: None, lambda: None, 0
    if rs:
        here, load_sems, left_sems, right_sems = scratch[:n_in], *scratch[n_in : n_in + 3]
        scratch = scratch[n_in + 3 :]
        outside, (left, right) = ins, here[:2]
        groups = left.shape[0] // TALL
        rows, tall, wide = left.shape[0] // n, left.shape[0] // n // groups, min(COLUMNS, right.shape[0])

        def left_copy(g, j):
            at = pl.ds(j * rows + g * tall, tall)
            return pltpu.make_async_copy(outside[0].at[at], left.at[at], left_sems.at[g, j])

        def right_copy(q):
            at = pl.ds(pl.multiple_of(q * wide, wide), wide)
            return pltpu.make_async_copy(outside[1].at[at, pl.ds(0, right.shape[1])], right.at[at], right_sems.at[q])

        def later_copies():
            return [left_copy(g, j) for g in range(1, groups) for j in range(n)] + [
                pltpu.make_async_copy(outside[i], here[i], load_sems.at[i]) for i in range(2, n_in)
            ]

        for j in range(n):
            left_copy(0, j).start()
        for q in range(right.shape[0] // wide):
            right_copy(q).start()
        for copy in later_copies():
            copy.start()
        ins = here
    if square is not None:
        counts = square[1:]
        square_refs = ins[n_in - counts[0] :], outs[n_out - counts[1] :], scratch[len(scratch) - counts[2] :]
        ins, outs, scratch = ins[: n_in - counts[0]], outs[: n_out - counts[1]], scratch[: len(scratch) - counts[2]]
        greet, also, finish, steps = square[0](ins[0], *square_refs)
    if rs:
        ins = ins[2:]
        part, up_buf, dn_buf, total, up_send, up_recv, dn_send, dn_recv = scratch[:8]
        scratch = scratch[8:]
    if ag:
        full, outs = outs[0], outs[1:]
        own, ag_recv, ag_up, ag_dn, ag_here = scratch[:5]
        rows = own.shape[0]
    size = rows // chunks

    def cut(c, base=0):
        return pl.ds(pl.multiple_of(base + c * size, size), size)

    def slot(j, device, turned):
        return lax.rem(j - device + n, n) if turned else j

    def product(g):
        block = jnp.concatenate([left[pl.ds(pl.multiple_of(j * rows + g * tall, tall), tall)] for j in range(n)], axis=0)

        def tile(q, _):
            @pl.when(g == 0)
            def _():
                right_copy(q).wait()

            columns = pl.ds(pl.multiple_of(q * wide, wide), wide)
            found = lax.dot_general(block, right[columns], (((1,), (1,)), ((), ())), preferred_element_type=jnp.float32)
            for j in range(n):
                part[pl.ds(pl.multiple_of(j * rows + g * tall, tall), tall), columns] = found[
                    j * tall : (j + 1) * tall
                ].astype(part.dtype)
            return 0

        lax.fori_loop(0, right.shape[0] // wide, tile, 0)

    def send(src, dst, send_sem, recv_sem, to):
        return pltpu.make_async_remote_copy(
            src_ref=src,
            dst_ref=dst,
            send_sem=send_sem,
            recv_sem=recv_sem,
            device_id={AXIS: to},
            device_id_type=pl.DeviceIdType.MESH,
        )

    barrier = pltpu.get_barrier_semaphore()

    @pl.when(me > 0)
    def _():
        pl.semaphore_signal(barrier, inc=1, device_id={AXIS: me - 1}, device_id_type=pl.DeviceIdType.MESH)

    @pl.when(me < last)
    def _():
        pl.semaphore_signal(barrier, inc=1, device_id={AXIS: me + 1}, device_id_type=pl.DeviceIdType.MESH)

    others = greet(barrier)
    pl.semaphore_wait(barrier, jnp.where((me > 0) & (me < last), 2, 1) + others)

    def sum_copy(up, d, c):
        buf, s, r, to = (up_buf, up_send, up_recv, me + 1) if up else (dn_buf, dn_send, dn_recv, me - 1)
        ref = buf.at[d - up, cut(c)]
        return send(ref, ref, s.at[d, c], r.at[d, c], to)

    def sum_step(up, d, c):
        buf = up_buf if up else dn_buf
        first = 0 if up else last
        mine = part[cut(c, slot(d, me, rolled[0]) * rows)]

        @pl.when(me == first)
        def _():
            buf[d - up, cut(c)] = mine

        @pl.when(me != first)
        def _():
            sum_copy(up, d, c).wait_recv()
            buf[d - up, cut(c)] += mine

        sum_copy(up, d, c).start()

    def gather_copy(up, j, c, from_own=False):
        to = me + 1 if up else me - 1
        src = own.at[cut(c)] if from_own else full.at[cut(c, slot(j, me, rolled[1]) * rows)]
        dst = full.at[cut(c, slot(j, to, rolled[1]) * rows)]
        return send(src, dst, (ag_up if up else ag_dn).at[j, c], ag_recv.at[j, c], to)

    def here_copy(c):
        return pltpu.make_async_copy(own.at[cut(c)], full.at[cut(c, slot(me, me, rolled[1]) * rows)], ag_here.at[c])

    def step(s, _):
        if rs:
            for up in (True, False):
                c = s - me if up else s - (last - me)
                for d in range(last, 0, -1) if up else range(last):

                    @pl.when((c >= 0) & (c < chunks) & ((me < d) if up else (me > d)))
                    def _(up=up, c=c, d=d):
                        sum_step(up, d, c)

            @pl.when(s == 0)
            def _():
                for copy in later_copies():
                    copy.wait()

        also(s)
        if rs:
            per_group = chunks // groups

            @pl.when((lax.rem(s, per_group) == 0) & (s + per_group < chunks))
            def _():
                product(s // per_group + 1)

        c_own = s - lag

        @pl.when((c_own >= 0) & (c_own < chunks))
        def _():
            c = c_own
            if rs:
                total[...] = part[cut(c, slot(me, me, rolled[0]) * rows)].astype(jnp.float32)

                @pl.when(me > 0)
                def _():
                    sum_copy(True, me, c).wait_recv()
                    total[...] += up_buf[me - 1, cut(c)].astype(jnp.float32)

                @pl.when(me < last)
                def _():
                    sum_copy(False, me, c).wait_recv()
                    total[...] += dn_buf[me, cut(c)].astype(jnp.float32)

                result = middle(cut(c), total[...], ins, outs)
            else:
                result = middle(cut(c), None, ins, outs)
            if ag:
                own[cut(c)] = result.astype(own.dtype)
                here_copy(c).start()

                @pl.when(me < last)
                def _():
                    gather_copy(True, me, c, True).start()

                @pl.when(me > 0)
                def _():
                    gather_copy(False, me, c, True).start()

        if ag:
            for t in range(1, last):
                c = s - lag - t
                for up in (True, False):
                    j = me - t if up else me + t

                    @pl.when((c >= 0) & (c < chunks) & (((j >= 0) & (me < last)) if up else ((j <= last) & (me > 0))))
                    def _(up=up, c=c, j=j):
                        gather_copy(up, j, c).wait_recv()
                        gather_copy(up, j, c).start()

        return 0

    if rs:
        for j in range(n):
            left_copy(0, j).wait()
        product(0)
    lax.fori_loop(0, max(chunks + lag + (last - 1 if ag else 0), steps), step, 0)
    finish()

    def drain(c, _):
        if rs:
            for d in range(n):

                @pl.when(me < d)
                def _(d=d):
                    sum_copy(True, d, c).wait_send()

                @pl.when(me > d)
                def _(d=d):
                    sum_copy(False, d, c).wait_send()

        if ag:
            here_copy(c).wait()
            for j in range(n):

                @pl.when(((me == last) & (j < me)) | ((me == 0) & (j > me)))
                def _(j=j):
                    gather_copy(True, j, c).wait_recv()

                @pl.when((me < last) & (j <= me))
                def _(j=j):
                    gather_copy(True, j, c).wait_send()

                @pl.when((me > 0) & (j >= me))
                def _(j=j):
                    gather_copy(False, j, c).wait_send()

        return 0

    lax.fori_loop(0, chunks, drain, 0)


def line_pass(name, summed, extras, extra_outs, middle, ag, chunks, collective_id, rows, width, rolled=(False, False), square=None, square_ins=(), square_outs=(), square_scratch=()):
    n = lax.axis_size(AXIS)
    rs = summed is not None
    size = rows // chunks
    vmem = pl.BlockSpec(memory_space=pltpu.VMEM)
    operands = (list(summed) if rs else []) + list(extras) + list(square_ins)
    scratch = []
    sems = pltpu.SemaphoreType.DMA((n, chunks))
    if rs:
        depth = summed[0].shape[1]
        shapes = [(n * rows, depth), (width, depth)] + [operand.shape for operand in operands[2:]]
        scratch += [pltpu.VMEM(shape, operand.dtype) for shape, operand in zip(shapes, operands)]
        scratch += [
            pltpu.SemaphoreType.DMA((len(operands),)),
            pltpu.SemaphoreType.DMA((n * rows // TALL, n)),
            pltpu.SemaphoreType.DMA((width // min(COLUMNS, width),)),
            pltpu.VMEM((n * rows, width), jnp.bfloat16),
            pltpu.VMEM((n - 1, rows, width), jnp.bfloat16),
            pltpu.VMEM((n - 1, rows, width), jnp.bfloat16),
            pltpu.VMEM((size, width), jnp.float32),
            sems, sems, sems, sems,
        ]
    if ag:
        scratch += [pltpu.VMEM((rows, width), jnp.bfloat16), sems, sems, sems, pltpu.SemaphoreType.DMA((chunks,))]
    shapes = ([jax.ShapeDtypeStruct((n * rows, width), jnp.bfloat16)] if ag else []) + [
        jax.ShapeDtypeStruct((rows, width), kind) for kind in extra_outs
    ] + list(square_outs)
    specs = ([pl.BlockSpec(memory_space=pl.ANY)] if ag else []) + [vmem] * (len(extra_outs) + len(square_outs))
    if square is not None:
        square = (square, len(square_ins), len(square_outs), len(square_scratch))
    moved = rows * width * 2 * (n - 1)
    return pl.pallas_call(
        functools.partial(line_body, n, chunks, rs, ag, rolled, middle, square, len(operands), len(shapes)),
        out_shape=shapes,
        in_specs=[pl.BlockSpec(memory_space=pl.ANY) if rs else vmem] * len(operands),
        out_specs=specs,
        scratch_shapes=scratch + list(square_scratch),
        compiler_params=pltpu.CompilerParams(
            collective_id=collective_id, has_side_effects=True, vmem_limit_bytes=VMEM
        ),
        cost_estimate=pl.CostEstimate(
            flops=0, bytes_accessed=moved * 40, transcendentals=0, remote_bytes_transferred=moved
        ),
        name=name,
    )(*operands)


def flipped(index, bit):
    return index + (1 << bit) - 2 * (1 << bit) * lax.rem(index // (1 << bit), 2)


def square_parts(heads, left, ins, outs, scratch):
    turned, gain, weights, other_terms = ins
    gain_sum, grads = outs[0], outs[1:]
    terms_one, sums, sums_in, sums_send, sums_recv, sent, *rest = scratch
    line = lax.axis_index(AXIS)
    line_bits = lax.axis_size(AXIS).bit_length() - 1
    size = lax.axis_size("dp")
    bits = size.bit_length() - 1
    arrived, sems = rest[:bits], rest[bits:]
    me = lax.axis_index("dp")
    rows, wide = sent.shape[-2:]
    half = wide // 2
    pairs = arrived[0].shape[0]
    orders = list(range(bits - 1)), list(range(bits - 1))[::-1]

    def greet(barrier):
        for bit in range(bits):
            pl.semaphore_signal(barrier, inc=1, device_id={"dp": flipped(me, bit)}, device_id_type=pl.DeviceIdType.MESH)
        for bit in range(line_bits):
            pl.semaphore_signal(barrier, inc=1, device_id={AXIS: flipped(line, bit)}, device_id_type=pl.DeviceIdType.MESH)
        return bits + line_bits

    def sums_copy(bit):
        return pltpu.make_async_remote_copy(
            src_ref=sums.at[bit],
            dst_ref=sums_in.at[bit],
            send_sem=sums_send.at[bit],
            recv_sem=sums_recv.at[bit],
            device_id={AXIS: flipped(line, bit)},
            device_id_type=pl.DeviceIdType.MESH,
        )

    def send(src, dst, send_sem, recv_sem, bit):
        return pltpu.make_async_remote_copy(
            src_ref=src,
            dst_ref=dst,
            send_sem=send_sem,
            recv_sem=recv_sem,
            device_id={"dp": flipped(me, bit)},
            device_id_type=pl.DeviceIdType.MESH,
        )

    def first_copy(p):
        return send(sent.at[lax.rem(p, 2)], arrived[0].at[p], sems[0].at[p], sems[1].at[p], 0)

    def places(side, stage, at):
        found = [slice(None)] * (bits - 1)
        for done in orders[side][: stage - 1]:
            found[done] = 0
        found[orders[side][stage - 1]] = at
        return tuple(found)

    def later_copy(p, side, stage):
        columns = (slice(None), pl.ds(side * half, half))
        return send(
            arrived[0].at[(p, *places(side, stage, 1), *columns)],
            arrived[stage].at[(p, *[slice(None)] * (bits - 1 - stage), *columns)],
            sems[2 * stage].at[p, side],
            sems[2 * stage + 1].at[p, side],
            orders[side][stage - 1] + 1,
        )

    def multiply(p, u, odd):
        owner = me
        for bit in range(bits):
            set_bit = odd if bit == 0 else u[bits - 1 - bit]
            if set_bit:
                owner = flipped(owner, bit)
        block = turned[pl.ds(pl.multiple_of(owner * rows, rows), rows)]
        columns = left[:, pl.ds(pl.multiple_of(p * wide, wide), wide)]
        return jnp.dot(block, columns, preferred_element_type=jnp.float32)

    blocks = [tuple(u >> bit & 1 for bit in range(bits - 1))[::-1] for u in range(size // 2)]

    def also(s):
        @pl.when(s < pairs)
        def _():
            p = s

            @pl.when(p >= 2)
            def _():
                first_copy(p - 2).wait_send()

            for u in blocks:
                sent[(lax.rem(p, 2), *u[::-1])] = multiply(p, u, 1).astype(sent.dtype)
            first_copy(p).start()

        for stage in range(1, bits + 1):

            @pl.when((s >= stage) & (s < pairs + stage))
            def _(stage=stage):
                p = s - stage
                if stage == 1:
                    first_copy(p).wait_recv()
                    for u in blocks:
                        at = (p, *u[::-1])
                        arrived[0][at] = (multiply(p, u, 0) + arrived[0][at].astype(jnp.float32)).astype(sent.dtype)
                for side in range(2):
                    columns = (slice(None), pl.ds(side * half, half))
                    if stage > 1:
                        later_copy(p, side, stage - 1).wait_recv()
                        at = (p, *places(side, stage - 1, 0), *columns)
                        came = (p, *[slice(None)] * (bits - stage), *columns)
                        if stage < bits:
                            arrived[0][at] += arrived[stage - 1][came]
                        else:
                            result(p, side, arrived[0][at].astype(jnp.float32) + arrived[stage - 1][came].astype(jnp.float32))
                    if stage < bits:
                        later_copy(p, side, stage).start()

        for bit in range(line_bits + 1):

            @pl.when(s == pairs + bits + bit)
            def _(bit=bit):
                if bit:
                    sums_copy(bit - 1).wait()
                    sums[bit] = sums[bit - 1] + sums_in[bit - 1]
                else:
                    sums[0, 0] = terms_one[...].T[: sums.shape[2]]
                    sums[0, 1] = other_terms[...].T[: sums.shape[2]]
                if bit < line_bits:
                    sums_copy(bit).start()
                else:
                    gain_sum[...] = sums[bit]

    def result(p, side, summed):
        at = pl.ds(pl.multiple_of(p * wide + side * half, half), half)
        terms = jnp.sum(summed * weights[:, at].astype(jnp.float32), axis=1, keepdims=True)
        terms = jnp.broadcast_to(terms, terms_one.shape)
        if side:
            terms_one[...] += terms
        else:

            @pl.when(p == 0)
            def _():
                terms_one[...] = terms

            @pl.when(p > 0)
            def _():
                terms_one[...] += terms

        summed = summed * gain[...]
        for found in range(pairs):
            head, kind = found // (pairs // heads), found % (pairs // heads)
            where = grads[side] if kind == 0 else grads[1 + kind]
            start = head * half if kind == 0 else head * wide + side * half

            @pl.when(p == found)
            def _(where=where, start=start):
                where[:, start : start + half] = summed

    def finish():
        for p in range(max(pairs - 2, 0), pairs):
            first_copy(p).wait_send()

        def drain(p, _):
            for side in range(2):
                for stage in range(1, bits):
                    later_copy(p, side, stage).wait_send()
            return 0

        lax.fori_loop(0, pairs, drain, 0)

    return greet, also, finish, pairs + bits + line_bits + 1


def square_shapes(rows, heads, columns):
    size = lax.axis_size("dp")
    bits = size.bit_length() - 1
    wide = 2 * KD
    pairs = columns // wide
    twos = [2] * (bits - 1)
    sums = [pltpu.VMEM((pairs, *twos[stage:], rows, wide), jnp.bfloat16) for stage in range(bits)]
    sems = [pltpu.SemaphoreType.DMA((pairs,))] * 2
    for _ in range(1, bits):
        sems += [pltpu.SemaphoreType.DMA((pairs, 2))] * 2
    outs = [jax.ShapeDtypeStruct((2, 8, rows), jnp.float32)]
    line_bits = lax.axis_size(AXIS).bit_length() - 1
    line_sems = pltpu.SemaphoreType.DMA((max(line_bits, 1),))
    line_scratch = [
        pltpu.VMEM((rows, 128), jnp.float32),
        pltpu.VMEM((line_bits + 1, 2, 8, rows), jnp.float32),
        pltpu.VMEM((max(line_bits, 1), 2, 8, rows), jnp.float32),
        line_sems,
        line_sems,
    ]
    outs += [jax.ShapeDtypeStruct((rows, heads * cols), jnp.float32) for cols in (KD, KD, VD, VD)]
    return outs, line_scratch + [pltpu.VMEM((2, *twos, rows, wide), jnp.bfloat16)] + sums + sems


def turn_parts(blocks, left, ins, outs, scratch):
    (rows_in,), (turned,) = ins, outs
    columns = rows_in.shape[1] // blocks

    def also(s):
        for block in range(blocks):

            @pl.when(s == block)
            def _(block=block):
                at = pl.ds(block * columns, columns)
                turned[at] = rows_in[:, at].T

    return lambda barrier: 0, also, lambda: None, blocks


HEADS = 8
KD = 256
VD = 512
ROWS = 256


EPS_NORM = 1e-06
EPS_GROUP = 1.0
CONTRACT_ROWS = (((0,), (0,)), ((), ()))
CONTRACT_COLUMNS = (((1,), (1,)), ((), ()))


def rotary_tables(length):
    positions = np.arange(length).astype(np.float32)[:, None]
    frequency = np.float32(10000.0) ** (-np.arange(KD // 2).astype(np.float32) * np.float32(2.0 / KD))
    angles = (positions * frequency[None, :]).astype(np.float32).astype(np.float64)
    return np.cos(angles).astype(np.float32), np.sin(angles).astype(np.float32)


def turn(rows, cosine, sine):
    low, high = rows[:, : KD // 2], rows[:, KD // 2 :]
    return jnp.concatenate([low * cosine - high * sine, high * cosine + low * sine], axis=1)


def dot(left, right, dims=(((1,), (0,)), ((), ()))):
    return lax.dot_general(left, right, dims, preferred_element_type=jnp.float32)


def head_decay(decay_ref, log_ref, head, reach):
    ahead = lax.broadcasted_iota(jnp.int32, decay_ref.shape, 0) - lax.broadcasted_iota(jnp.int32, decay_ref.shape, 1)
    distance = ahead + reach
    value = jnp.exp(log_ref[head] * jnp.maximum(distance, 0).astype(jnp.float32))
    decay_ref[...] = jnp.where(distance >= 0, value, 0.0)


def normed_heads(heads_out):
    centred = heads_out - jnp.mean(heads_out, axis=-1, keepdims=True)
    inverse = lax.rsqrt(jnp.mean(centred * centred, axis=-1, keepdims=True) + EPS_GROUP)
    return centred * inverse, inverse


def retention_body(block, reach, log_ref, proj, cosine, sine, seg_rows, seg_line, kept, mixed, keys, vals, decay):
    head, row = pl.program_id(0), pl.program_id(1)
    here = pl.ds(pl.multiple_of(reach + row * block, block), block)
    window = pl.ds(pl.multiple_of(row * block, block), reach + block)

    @pl.when(row == 0)
    def _():
        head_decay(decay, log_ref, head, reach)
        keys[:reach] = jnp.zeros((reach, KD), keys.dtype)
        vals[:reach] = jnp.zeros((reach, VD), vals.dtype)

    query = turn(proj[:, :KD], cosine[...], sine[...]).astype(jnp.bfloat16)
    key = (turn(proj[:, KD : 2 * KD], cosine[...], sine[...]) * KD ** (-0.5)).astype(jnp.bfloat16)
    value = proj[:, 2 * KD : 2 * KD + VD].astype(jnp.bfloat16)
    keys[here] = key
    vals[here] = value
    kept[:, :KD] = query
    kept[:, KD : 2 * KD] = key
    kept[:, 2 * KD :] = value
    weight = jnp.where(seg_rows[...] == seg_line[:, window], decay[...], 0.0)
    probs = (dot(query, keys[window], CONTRACT_COLUMNS) * weight).astype(jnp.bfloat16)
    normed, _ = normed_heads(dot(probs, vals[window]))
    mixed[...] = (jax.nn.silu(proj[:, 2 * KD + VD :]) * normed).astype(jnp.bfloat16)


def retention_pull_body(
    block, reach, log_ref, kept, gate, d_branch, w_out, cosine, sine, seg_rows, seg_line, d_in, keys, vals, d_keys, d_vals, decay
):
    head, row = pl.program_id(0), pl.num_programs(1) - 1 - pl.program_id(1)
    mine = pl.ds(pl.multiple_of(row * block, block), block)
    here = pl.ds(pl.multiple_of(reach + row * block, block), block)
    window = pl.ds(pl.multiple_of(row * block, block), reach + block)

    @pl.when(pl.program_id(1) == 0)
    def _():
        head_decay(decay, log_ref, head, reach)
        keys[:reach] = jnp.zeros((reach, KD), keys.dtype)
        vals[:reach] = jnp.zeros((reach, VD), vals.dtype)
        keys[reach:] = kept[:, KD : 2 * KD]
        vals[reach:] = kept[:, 2 * KD :]
        d_keys[...] = jnp.zeros_like(d_keys)
        d_vals[...] = jnp.zeros_like(d_vals)

    query = kept[mine, :KD]
    weight = jnp.where(seg_rows[...] == seg_line[:, window], decay[...], 0.0)
    probs = (dot(query, keys[window], CONTRACT_COLUMNS) * weight).astype(jnp.bfloat16)
    normed, inverse = normed_heads(dot(probs, vals[window]))
    gate_pre, upstream = gate[...], dot(d_branch[...], w_out[...])
    opened = jax.nn.sigmoid(gate_pre)
    silu = gate_pre * opened
    d_in[:, 2 * KD + VD :] = (upstream * normed * (opened + silu * (1.0 - opened))).astype(jnp.bfloat16)
    e = upstream * silu
    d_heads = e - jnp.mean(e, axis=-1, keepdims=True) - normed * jnp.mean(e * normed, axis=-1, keepdims=True)
    d_heads = (d_heads * inverse).astype(jnp.bfloat16)
    d_scores = (dot(d_heads, vals[window], CONTRACT_COLUMNS) * weight).astype(jnp.bfloat16)
    d_vals[window] += dot(probs, d_heads, CONTRACT_ROWS)
    d_keys[window] += dot(d_scores, query, CONTRACT_ROWS)
    d_query = dot(d_scores, keys[window])
    d_in[:, :KD] = turn(d_query, cosine[...], -sine[...]).astype(jnp.bfloat16)
    d_in[:, KD : 2 * KD] = (turn(d_keys[here], cosine[...], -sine[...]) * KD ** (-0.5)).astype(jnp.bfloat16)
    d_in[:, 2 * KD : 2 * KD + VD] = d_vals[here].astype(jnp.bfloat16)


def hop_valid(kind, t, device, up):
    last = lax.axis_size(AXIS) - 1
    passed = device if up else last - device
    inside = (passed >= 0) & (passed < last)
    return inside & ((passed >= t) if kind == "gather" else (passed <= t))


def hop_call(body, hop, collective_id, *, grid, in_specs, out_specs, out_shape, scratch_shapes=(), cost, name):
    def params(**more):
        return pltpu.CompilerParams(vmem_limit_bytes=VMEM, **more)

    if hop is None:
        return pl.pallas_call(
            body,
            grid=grid,
            in_specs=in_specs,
            out_specs=out_specs,
            out_shape=out_shape,
            scratch_shapes=list(scratch_shapes),
            compiler_params=params(),
            cost_estimate=cost,
            name=name,
        )
    kind, t, up, down = hop
    n_in, n_out = len(in_specs), len(out_specs)

    def with_hop(*refs):
        ins, sources = refs[:n_in], refs[n_in : n_in + 2]
        outs, targets = refs[n_in + 2 : n_in + 2 + n_out], refs[n_in + 2 + n_out : n_in + 4 + n_out]
        *scratch, send_sems, recv_sems = refs[n_in + 4 + n_out :]
        me = lax.axis_index(AXIS)
        last = lax.axis_size(AXIS) - 1
        steps = [pl.program_id(i) for i in range(len(grid))]
        at_first = functools.reduce(jnp.logical_and, [step == 0 for step in steps])
        at_last = functools.reduce(jnp.logical_and, [step == size - 1 for step, size in zip(steps, grid)])

        def copy(way):
            return pltpu.make_async_remote_copy(
                src_ref=sources[way],
                dst_ref=targets[way],
                send_sem=send_sems.at[way],
                recv_sem=recv_sems.at[way],
                device_id={AXIS: me - 1 if way else me + 1},
                device_id_type=pl.DeviceIdType.MESH,
            )

        @pl.when(at_first)
        def _():
            barrier = pltpu.get_barrier_semaphore()
            for way in range(2):

                @pl.when((me > 0) if way else (me < last))
                def _(way=way):
                    to = me - 1 if way else me + 1
                    pl.semaphore_signal(barrier, inc=1, device_id={AXIS: to}, device_id_type=pl.DeviceIdType.MESH)

            pl.semaphore_wait(barrier, jnp.where((me > 0) & (me < last), 2, 1))
            for way in range(2):

                @pl.when(hop_valid(kind, t, me, way == 0))
                def _(way=way):
                    copy(way).start()

        body(*ins, *outs, *scratch)

        @pl.when(at_last)
        def _():
            for way in range(2):

                @pl.when(hop_valid(kind, t, me, way == 0))
                def _(way=way):
                    copy(way).wait_send()

                @pl.when(hop_valid(kind, t, me + 1 if way else me - 1, way == 0))
                def _(way=way):
                    copy(way).wait_recv()

    anywhere = [pl.BlockSpec(memory_space=pl.ANY)] * 2
    call = pl.pallas_call(
        with_hop,
        grid=grid,
        in_specs=[*in_specs, *anywhere],
        out_specs=[*out_specs, *anywhere],
        out_shape=[*out_shape, *[jax.ShapeDtypeStruct(up.shape, up.dtype)] * 2],
        scratch_shapes=[*scratch_shapes, pltpu.SemaphoreType.DMA((2,)), pltpu.SemaphoreType.DMA((2,))],
        compiler_params=params(collective_id=collective_id, has_side_effects=True),
        cost_estimate=cost,
        name=name,
    )
    return lambda *operands: call(*operands, up, down)


def work(flops, moved):
    return pl.CostEstimate(flops=flops, bytes_accessed=moved, transcendentals=0)


def project_body(block, rows_in, weights, out):
    def part(q, _):
        at = pl.ds(pl.multiple_of(q * block, block), block)
        out[at] = dot(rows_in[at], weights[...])
        return 0

    lax.fori_loop(0, rows_in.shape[0] // block, part, 0)


def project(rows_in, weights, hop):
    length, depth = rows_in.shape
    columns = weights.shape[1]
    tile = min(512, columns)
    return hop_call(
        functools.partial(project_body, ROWS),
        hop,
        4,
        grid=(columns // tile,),
        in_specs=[pl.BlockSpec((length, depth), lambda c: (0, 0)), pl.BlockSpec((depth, tile), lambda c: (0, c))],
        out_specs=[pl.BlockSpec((length, tile), lambda c: (0, c))],
        out_shape=[jax.ShapeDtypeStruct((length, columns), jnp.float32)],
        cost=work(2 * length * weights.size, 2 * rows_in.size + 2 * weights.size + 4 * length * columns),
        name="project",
    )(rows_in, weights)


def hidden_body(rows_in, w_pair, w_down, both, hidden, part):
    found = dot(rows_in[...], w_pair[...])
    both[...] = found
    columns = hidden.shape[1]
    hidden[...] = (jax.nn.gelu(found[:, :columns], approximate=True) * found[:, columns:]).astype(hidden.dtype)
    part[...] = dot(hidden[...], w_down[...], CONTRACT_COLUMNS).astype(part.dtype)


def hidden_layer(rows_in, mlp_full, hop):
    length, width = rows_in.shape
    columns = mlp_full.shape[1] // 3
    once = pl.Buffered(1)
    return hop_call(
        hidden_body,
        hop,
        6,
        grid=(length // ROWS,),
        in_specs=[
            pl.BlockSpec((ROWS, width), lambda r: (r, 0)),
            pl.BlockSpec((width, 2 * columns), lambda r: (0, 0), pipeline_mode=once),
            pl.BlockSpec((width, columns), lambda r: (0, 2), pipeline_mode=once),
        ],
        out_specs=[
            pl.BlockSpec((ROWS, 2 * columns), lambda r: (r, 0)),
            pl.BlockSpec((ROWS, columns), lambda r: (r, 0)),
            pl.BlockSpec((ROWS, width), lambda r: (r, 0)),
        ],
        out_shape=[
            jax.ShapeDtypeStruct((length, 2 * columns), jnp.float32),
            jax.ShapeDtypeStruct((length, columns), jnp.bfloat16),
            jax.ShapeDtypeStruct((length, width), jnp.bfloat16),
        ],
        cost=work(6 * length * width * columns, 2 * mlp_full.size + 14 * length * columns),
        name="hidden_layer",
    )(rows_in, mlp_full, mlp_full)


def turned_body(*refs):
    *pairs, out = refs
    at = 0
    for left, right in zip(pairs[::2], pairs[1::2]):
        columns = right.shape[1]
        out[:, at : at + columns] = dot(left[...], right[...], CONTRACT_ROWS).astype(out.dtype)
        at += columns


def turned_dots(pairs, hop, collective_id, name):
    length, width = pairs[0][0].shape
    columns = sum(right.shape[1] for _, right in pairs)
    specs = []
    for _, right in pairs:
        specs.append(pl.BlockSpec((length, ROWS), lambda r: (0, r)))
        specs.append(pl.BlockSpec(right.shape, lambda r: (0, 0), pipeline_mode=pl.Buffered(1)))
    return hop_call(
        turned_body,
        hop,
        collective_id,
        grid=(width // ROWS,),
        in_specs=specs,
        out_specs=[pl.BlockSpec((ROWS, columns), lambda r: (r, 0))],
        out_shape=[jax.ShapeDtypeStruct((width, columns), jnp.bfloat16)],
        cost=work(2 * length * width * columns, 2 * (len(pairs) * length * width + length * columns + width * columns)),
        name=name,
    )(*[array for pair in pairs for array in pair])


def retention_inputs(segments, heads):
    length = segments.shape[0]
    block = min(ROWS, length // 2)
    reach = length // 2
    head_ids = lax.axis_index("tensor") * heads + jnp.arange(heads)
    log_decay = jnp.log(1.0 - 2.0 ** (-5.0 - head_ids.astype(jnp.float32)))
    seg_line = jnp.concatenate([jnp.full((reach,), -1, jnp.int32), segments])[None, :]
    return block, reach, log_decay, segments[:, None], seg_line


def retention(projected, segments, heads, hop):
    length = projected.shape[0]
    block, reach, log_decay, seg_rows, seg_line = retention_inputs(segments, heads)
    cosine, sine = rotary_tables(length)
    per_head = projected.shape[1] // heads
    table = pl.BlockSpec((block, KD // 2), lambda h, r: (r, 0))
    return hop_call(
        functools.partial(retention_body, block, reach),
        hop,
        5,
        grid=(heads, length // block),
        in_specs=[
            pl.BlockSpec(memory_space=pltpu.SMEM),
            pl.BlockSpec((block, per_head), lambda h, r: (r, h)),
            table,
            table,
            pl.BlockSpec((block, 1), lambda h, r: (r, 0)),
            pl.BlockSpec(seg_line.shape, lambda h, r: (0, 0)),
        ],
        out_specs=[
            pl.BlockSpec((block, 2 * KD + VD), lambda h, r: (r, h)),
            pl.BlockSpec((block, VD), lambda h, r: (r, h)),
        ],
        out_shape=[
            jax.ShapeDtypeStruct((length, heads * (2 * KD + VD)), jnp.bfloat16),
            jax.ShapeDtypeStruct((length, heads * VD), jnp.bfloat16),
        ],
        scratch_shapes=[
            pltpu.VMEM((reach + length, KD), jnp.bfloat16),
            pltpu.VMEM((reach + length, VD), jnp.bfloat16),
            pltpu.VMEM((block, reach + block), jnp.float32),
        ],
        cost=work(2 * heads * length * (reach + block) * (KD + VD), projected.size * 6),
        name="retention",
    )(log_decay, projected, cosine, sine, seg_rows, seg_line)


def retention_pull(kept, projected, d_branch, w_out, segments, heads, hop):
    length = kept.shape[0]
    block, reach, log_decay, seg_rows, seg_line = retention_inputs(segments, heads)
    cosine, sine = rotary_tables(length)
    per_head = projected.shape[1] // heads
    last = length // block - 1
    gate_block = per_head // VD
    table = pl.BlockSpec((block, KD // 2), lambda h, r: (last - r, 0))
    return hop_call(
        functools.partial(retention_pull_body, block, reach),
        hop,
        9,
        grid=(heads, last + 1),
        in_specs=[
            pl.BlockSpec(memory_space=pltpu.SMEM),
            pl.BlockSpec((length, 2 * KD + VD), lambda h, r: (0, h)),
            pl.BlockSpec((block, VD), lambda h, r: (last - r, gate_block * h + gate_block - 1)),
            pl.BlockSpec((block, d_branch.shape[1]), lambda h, r: (last - r, 0)),
            pl.BlockSpec((w_out.shape[0], VD), lambda h, r: (0, h)),
            table,
            table,
            pl.BlockSpec((block, 1), lambda h, r: (last - r, 0)),
            pl.BlockSpec(seg_line.shape, lambda h, r: (0, 0)),
        ],
        out_specs=[pl.BlockSpec((block, per_head), lambda h, r: (last - r, h))],
        out_shape=[jax.ShapeDtypeStruct(projected.shape, jnp.bfloat16)],
        scratch_shapes=[
            pltpu.VMEM((reach + length, KD), jnp.bfloat16),
            pltpu.VMEM((reach + length, VD), jnp.bfloat16),
            pltpu.VMEM((reach + length, KD), jnp.float32),
            pltpu.VMEM((reach + length, VD), jnp.float32),
            pltpu.VMEM((block, reach + block), jnp.float32),
        ],
        cost=work(2 * heads * length * ((reach + block) * 3 * (KD + VD) + d_branch.shape[1] * VD), projected.size * 8),
        name="retention_pull",
    )(log_decay, kept, projected, d_branch, w_out, cosine, sine, seg_rows, seg_line)


def inverse_rms(rows):
    return lax.rsqrt(jnp.mean(rows * rows, axis=-1, keepdims=True) + EPS_NORM)


def norm_pull(unit, inverse, d_unit):
    return inverse * (d_unit - unit * jnp.mean(d_unit * unit, axis=-1, keepdims=True))


def unit_step(cut, summed, ins, outs):
    inputs = ins[0][cut].astype(jnp.float32)
    return inputs * inverse_rms(inputs)


def residual_step(cut, summed, ins, outs):
    residual = ins[0][cut].astype(jnp.float32) + summed
    outs[0][cut] = residual
    return residual * inverse_rms(residual)


def d_residual_step(cut, summed, ins, outs):
    residual = ins[0][cut]
    inverse = inverse_rms(residual)
    d_residual = ins[1][cut].astype(jnp.float32) + norm_pull(residual * inverse, inverse, summed)
    outs[0][cut] = d_residual
    return d_residual


def tokens_step(cut, summed, ins, outs):
    inputs = ins[0][cut].astype(jnp.float32)
    inverse = inverse_rms(inputs)
    grad = ins[1][cut] + norm_pull(inputs * inverse, inverse, summed)
    outs[0][cut] = grad.astype(outs[0].dtype)


def hops(up):
    n = lax.axis_size(AXIS)
    return [(i, i + 1) if up else (i + 1, i) for i in range(n - 1)]


def joined_body(parts, plain, *refs):
    *arrays, gain, out = refs
    at = 0
    for array, index, columns in parts:
        found = arrays[array][:, index * columns : (index + 1) * columns]
        if array < len(arrays) - plain:
            found = (found.astype(jnp.float32) * gain[...]).astype(out.dtype)
        out[:, at : at + columns] = found
        at += columns


def join_parts(parts, plain, left, ins, outs, scratch):
    def also(s):
        @pl.when(s == 0)
        def _():
            joined_body(parts, plain, *ins, *outs)

    return lambda barrier: 0, also, lambda: None, 1


def joined(name, arrays, gain, parts, plain=0):
    columns = sum(part[2] for part in parts)
    return pl.pallas_call(
        functools.partial(joined_body, parts, plain),
        out_shape=jax.ShapeDtypeStruct((gain.shape[0], columns), arrays[0].dtype),
        compiler_params=pltpu.CompilerParams(vmem_limit_bytes=VMEM),
        name=name,
    )(*arrays, gain)


def hidden_pull_body(cotangent, w_down, both, d_pair):
    columns = w_down.shape[1]
    d_hidden = dot(cotangent[...], w_down[...])
    gate, up = both[:, :columns], both[:, columns:]
    slope = math.sqrt(2.0 / math.pi)
    cubed = 0.044715 * gate * gate
    bent = jnp.tanh(slope * gate * (1.0 + cubed))
    half = 0.5 + 0.5 * bent
    d_gelu = half + 0.5 * gate * (1.0 - bent * bent) * slope * (1.0 + 3.0 * cubed)
    d_pair[:, :columns] = (d_hidden * up * d_gelu).astype(d_pair.dtype)
    d_pair[:, columns:] = (d_hidden * gate * half).astype(d_pair.dtype)


def hidden_pull(cotangent, mlp_full, both, hop):
    length, width = cotangent.shape
    columns = both.shape[1] // 2
    return hop_call(
        hidden_pull_body,
        hop,
        7,
        grid=(length // ROWS,),
        in_specs=[
            pl.BlockSpec((ROWS, width), lambda r: (r, 0)),
            pl.BlockSpec((width, columns), lambda r: (0, 2), pipeline_mode=pl.Buffered(1)),
            pl.BlockSpec((ROWS, 2 * columns), lambda r: (r, 0)),
        ],
        out_specs=[pl.BlockSpec((ROWS, 2 * columns), lambda r: (r, 0))],
        out_shape=[jax.ShapeDtypeStruct(both.shape, jnp.bfloat16)],
        cost=work(2 * length * width * columns, both.size * 6 + cotangent.size * 4),
        name="hidden_pull",
    )(cotangent, mlp_full, both)


def steps_of(part, parts):
    n = lax.axis_size(AXIS)
    return range((n - 1) * part // parts, (n - 1) * (part + 1) // parts)


def gather_hop(state, steps):
    for _ in steps[:-1]:
        up, down = state[-2:]
        state = [*state, lax.ppermute(up, AXIS, hops(True)), lax.ppermute(down, AXIS, hops(False))]
    return state, ("gather", steps[-1], *state[-2:]) if len(steps) else None


def gather_end(state):
    n, me = lax.axis_size(AXIS), lax.axis_index(AXIS)
    ups, downs = state[::2], state[1::2]
    return jnp.concatenate([ups[0]] + [jnp.where(me + k < n, downs[k], ups[n - k]) for k in range(1, n)], axis=0)


def scatter_masked(state, t):
    n, me = lax.axis_size(AXIS), lax.axis_index(AXIS)
    found = []
    for sums, up in zip(state, (True, False)):
        came = hop_valid("scatter", t - 1, me - 1 if up else me + 1, up)
        found.append(jnp.where(came, sums, jnp.zeros_like(sums)).astype(jnp.float32))
    return found


def scatter_hop(state, part, steps):
    n = lax.axis_size(AXIS)
    rows = part.shape[0] // n
    for t in steps:
        mine = [part[k * rows : (k + 1) * rows].astype(jnp.float32) for k in (n - 1 - t, 1 + t)]
        if t:
            mine = [own + sums for own, sums in zip(mine, scatter_masked(state, t))]
        mine = [sums.astype(part.dtype) for sums in mine]
        if t == steps[-1]:
            return ("scatter", t, *mine)
        state = [lax.ppermute(sums, AXIS, hops(way)) for sums, way in zip(mine, (True, False))]
    return None


def shards(tokens,
    segment_ids,
    attn_gain,
    w_query,
    w_key,
    w_value,
    w_gate,
    w_out,
    mlp_gain,
    w_mlp_gate,
    w_mlp_up,
    w_down,
    cotangent,
):
    local_rows, width = tokens.shape
    heads = HEADS // lax.axis_size(AXIS)
    hidden_cols = w_mlp_gate.shape[1]
    segments = segment_ids[0]
    gain_one = attn_gain.astype(jnp.float32)[:, None]
    gain_two = mlp_gain.astype(jnp.float32)[:, None]
    after = lax.optimization_barrier

    def gather(own):
        return lax.all_gather(own, "dp", axis=0, tiled=True)

    def scatter(grad):
        return lax.psum_scatter(grad, "dp", scatter_dimension=0, tiled=True)

    def gain_terms(weights, grads):
        return jnp.sum(weights.astype(jnp.float32) * grads.astype(jnp.float32), axis=1)

    in_parts = [(array, head, columns) for head in range(heads) for array, columns in enumerate((KD, KD, VD, VD))]
    w_in_own = joined("join_in", [w_query, w_key, w_value, w_gate], gain_one, in_parts)
    w_in = gather(w_in_own)
    unit_one, mlp_own = line_pass(
        "gather_one",
        None,
        [tokens],
        [],
        unit_step,
        True,
        4,
        0,
        local_rows,
        width,
        square=functools.partial(join_parts, [(i, 0, hidden_cols) for i in range(3)], 1),
        square_ins=[w_mlp_gate, w_mlp_up, w_down, gain_two],
        square_outs=[jax.ShapeDtypeStruct((gain_two.shape[0], 3 * hidden_cols), jnp.bfloat16)],
    )
    w_in, unit_one, w_out, cot_own, mlp_own = after((w_in, unit_one, w_out, cotangent, mlp_own))
    out_full = gather(w_out)
    cot, hop = gather_hop([cot_own, cot_own], steps_of(0, 3))
    projected, *came = project(unit_one, w_in, hop)
    cot, hop = gather_hop([*cot, *came], steps_of(1, 3))
    kept, mixed, *came = retention(projected, segments, heads, hop)
    cot = [*cot, *came]
    mixed, out_full, mlp_send, *cot = after((mixed, out_full, mlp_own, *cot))
    mlp_full = gather(mlp_send)
    unit_two, residual, unit_turned = line_pass(
        "residual",
        (mixed, out_full),
        [tokens],
        [jnp.float32],
        residual_step,
        True,
        16,
        1,
        local_rows,
        width,
        (False, True),
        square=functools.partial(turn_parts, 8),
        square_ins=[unit_one],
        square_outs=[jax.ShapeDtypeStruct(unit_one.shape[::-1], unit_one.dtype)],
    )
    unit_two, mlp_full, *cot = after((unit_two, mlp_full, *cot))
    cot, hop = gather_hop(cot, steps_of(2, 3))
    both_hidden, hidden, part_down, *came = hidden_layer(unit_two, mlp_full, hop)
    cot_full = gather_end([*cot, *came])
    (d_pair,) = hidden_pull(cot_full, mlp_full, both_hidden, None)
    hop = scatter_hop(None, part_down, steps_of(0, 3))
    grad_mlp, *sums = turned_dots([(unit_two, d_pair), (cot_full, hidden)], hop, 8, "mlp_grads")
    mlp_grad = scatter(grad_mlp)
    d_branch_one, d_residual = line_pass(
        "d_residual", (d_pair, mlp_full), [residual, cotangent], [jnp.float32], d_residual_step, True, 16, 2, local_rows, width, (True, False)
    )
    d_branch_one, d_residual, mlp_grad = after((d_branch_one, d_residual, mlp_grad))
    hop = scatter_hop(sums, part_down, steps_of(1, 3))
    grad_out, *sums = turned_dots([(d_branch_one, mixed)], hop, 10, "out_grads")
    out_grad = scatter(grad_out)
    hop = scatter_hop(sums, part_down, steps_of(2, 3))
    d_in, *sums = retention_pull(kept, projected, d_branch_one, out_full, segments, heads, hop)
    sums = scatter_masked(sums, lax.axis_size(AXIS) - 1)
    result = residual + part_down[:local_rows].astype(jnp.float32) + sum(sums)
    result = result.astype(jnp.bfloat16)
    pair_grad, down_grad = mlp_grad[:, : 2 * hidden_cols], mlp_grad[:, 2 * hidden_cols :].astype(jnp.float32)
    terms_two = gain_terms(mlp_own[:, : 2 * hidden_cols], pair_grad)
    terms_two = jnp.broadcast_to(terms_two[:, None], (terms_two.shape[0], 128))
    pair_grad = pair_grad.astype(jnp.float32) * gain_two
    gate_grad, up_grad = pair_grad[:, :hidden_cols], pair_grad[:, hidden_cols:]
    d_in, result, gate_grad, up_grad, down_grad = after((d_in, result, gate_grad, up_grad, down_grad))
    square_outs, square_scratch = square_shapes(gain_one.shape[0], heads, w_in.shape[1])
    tokens_grad, gain_sums, *in_grads = line_pass(
        "tokens_grad",
        (d_in, w_in),
        [tokens, d_residual],
        [jnp.bfloat16],
        tokens_step,
        False,
        8,
        3,
        local_rows,
        width,
        square=functools.partial(square_parts, heads),
        square_ins=[unit_turned, gain_one, w_in_own, terms_two],
        square_outs=square_outs,
        square_scratch=square_scratch,
    )
    gain_sum_one, gain_sum_two = gain_sums[0, 0] / gain_one[:, 0], gain_sums[1, 0] / gain_two[:, 0]
    return (
        result,
        tokens_grad,
        gain_sum_one,
        *in_grads,
        out_grad.astype(jnp.float32),
        gain_sum_two,
        gate_grad,
        up_grad,
        down_grad,
    )


def solution(mesh):
    return jax.shard_map(
        shards,
        mesh=mesh,
        in_specs=(
            P(("dp", "tensor"), None),
            P("dp", None),
            P("dp"),
            P("dp", "tensor"),
            P("dp", "tensor"),
            P("dp", "tensor"),
            P("dp", "tensor"),
            P("dp", "tensor"),
            P("dp"),
            P("dp", "tensor"),
            P("dp", "tensor"),
            P("dp", "tensor"),
            P(("dp", "tensor"), None),
        ),
        out_specs=(
            P(("dp", "tensor"), None),
            P(("dp", "tensor"), None),
            P("dp"),
            P("dp", "tensor"),
            P("dp", "tensor"),
            P("dp", "tensor"),
            P("dp", "tensor"),
            P("dp", "tensor"),
            P("dp"),
            P("dp", "tensor"),
            P("dp", "tensor"),
            P("dp", "tensor"),
        ),
        check_vma=False,
    )
```

```python
import functools
import math
import jax
import jax.numpy as jnp
import numpy as np
from jax import lax
from jax.experimental import pallas as pl
from jax.experimental.pallas import tpu as pltpu
from jax.sharding import PartitionSpec as P

AXIS = "tensor"
TALL = 256
COLUMNS = 1024
VMEM = 62 * 1024 * 1024


def line_body(n, chunks, rs, ag, rolled, middle, square, n_in, n_out, *refs):
    ins, outs, scratch = refs[:n_in], refs[n_in : n_in + n_out], list(refs[n_in + n_out :])
    me = lax.axis_index(AXIS)
    last = n - 1
    lag = last if rs else 0
    greet, also, finish, steps, early = lambda barrier: 0, lambda s: None, lambda: None, 0, False
    if rs:
        here, load_sems, left_sems, right_sems = scratch[:n_in], *scratch[n_in : n_in + 3]
        scratch = scratch[n_in + 3 :]
        outside, (left, right) = ins, here[:2]
        groups = left.shape[0] // TALL
        rows, tall, wide = left.shape[0] // n, left.shape[0] // n // groups, min(COLUMNS, right.shape[0])

        def left_copy(g, j):
            at = pl.ds(j * rows + g * tall, tall)
            return pltpu.make_async_copy(outside[0].at[at], left.at[at], left_sems.at[g, j])

        def right_copy(q):
            at = pl.ds(pl.multiple_of(q * wide, wide), wide)
            return pltpu.make_async_copy(outside[1].at[at, pl.ds(0, right.shape[1])], right.at[at], right_sems.at[q])

        def other_copy(i):
            return pltpu.make_async_copy(outside[i], here[i], load_sems.at[i])

        soon = n_in - square[1] if square is not None else n_in
        others = [i for i in range(2, n_in) if i != soon]

        def start_loads():
            starts = [left_copy(0, j) for j in range(n)]
            later = [left_copy(g, j) for g in range(1, groups) for j in range(n)]
            later += [other_copy(soon)] if soon < n_in else []
            tiles = [right_copy(q) for q in range(right.shape[0] // wide)]
            for copy in starts + (later + tiles if early else tiles + later) + [other_copy(i) for i in others]:
                copy.start()

        def wait_soon():
            for g in range(1, groups):
                for j in range(n):
                    left_copy(g, j).wait()
            if soon < n_in:
                other_copy(soon).wait()

        ins = here
    if square is not None:
        counts = square[1:]
        square_refs = ins[n_in - counts[0] :], outs[n_out - counts[1] :], scratch[len(scratch) - counts[2] :]
        ins, outs, scratch = ins[: n_in - counts[0]], outs[: n_out - counts[1]], scratch[: len(scratch) - counts[2]]
        greet, also, finish, steps, early = square[0](ins[0], *square_refs)
    if rs:
        start_loads()
        ins = ins[2:]
        part, up_buf, dn_buf, total, up_send, up_recv, dn_send, dn_recv = scratch[:8]
        scratch = scratch[8:]
    if ag:
        full, outs = outs[0], outs[1:]
        own, ag_recv, ag_up, ag_dn, ag_here = scratch[:5]
        rows = own.shape[0]
    size = rows // chunks

    def cut(c, base=0):
        return pl.ds(pl.multiple_of(base + c * size, size), size)

    def slot(j, device, turned):
        return lax.rem(j - device + n, n) if turned else j

    def product(g):
        block = jnp.concatenate([left[pl.ds(pl.multiple_of(j * rows + g * tall, tall), tall)] for j in range(n)], axis=0)

        def tile(q, _):
            @pl.when(g == 0)
            def _():
                right_copy(q).wait()

            columns = pl.ds(pl.multiple_of(q * wide, wide), wide)
            found = lax.dot_general(block, right[columns], (((1,), (1,)), ((), ())), preferred_element_type=jnp.float32)
            for j in range(n):
                part[pl.ds(pl.multiple_of(j * rows + g * tall, tall), tall), columns] = found[
                    j * tall : (j + 1) * tall
                ].astype(part.dtype)
            return 0

        lax.fori_loop(0, right.shape[0] // wide, tile, 0)

    def send(src, dst, send_sem, recv_sem, to):
        return pltpu.make_async_remote_copy(
            src_ref=src,
            dst_ref=dst,
            send_sem=send_sem,
            recv_sem=recv_sem,
            device_id={AXIS: to},
            device_id_type=pl.DeviceIdType.MESH,
        )

    barrier = pltpu.get_barrier_semaphore()

    @pl.when(me > 0)
    def _():
        pl.semaphore_signal(barrier, inc=1, device_id={AXIS: me - 1}, device_id_type=pl.DeviceIdType.MESH)

    @pl.when(me < last)
    def _():
        pl.semaphore_signal(barrier, inc=1, device_id={AXIS: me + 1}, device_id_type=pl.DeviceIdType.MESH)

    greeted = greet(barrier)
    pl.semaphore_wait(barrier, jnp.where((me > 0) & (me < last), 2, 1) + greeted)

    def sum_copy(up, d, c):
        buf, s, r, to = (up_buf, up_send, up_recv, me + 1) if up else (dn_buf, dn_send, dn_recv, me - 1)
        ref = buf.at[d - up, cut(c)]
        return send(ref, ref, s.at[d, c], r.at[d, c], to)

    def sum_step(up, d, c):
        buf = up_buf if up else dn_buf
        first = 0 if up else last
        mine = part[cut(c, slot(d, me, rolled[0]) * rows)]

        @pl.when(me == first)
        def _():
            buf[d - up, cut(c)] = mine

        @pl.when(me != first)
        def _():
            sum_copy(up, d, c).wait_recv()
            buf[d - up, cut(c)] += mine

        sum_copy(up, d, c).start()

    def gather_copy(up, j, c, from_own=False):
        to = me + 1 if up else me - 1
        src = own.at[cut(c)] if from_own else full.at[cut(c, slot(j, me, rolled[1]) * rows)]
        dst = full.at[cut(c, slot(j, to, rolled[1]) * rows)]
        return send(src, dst, (ag_up if up else ag_dn).at[j, c], ag_recv.at[j, c], to)

    def here_copy(c):
        return pltpu.make_async_copy(own.at[cut(c)], full.at[cut(c, slot(me, me, rolled[1]) * rows)], ag_here.at[c])

    def step(s, _):
        if rs:
            for up in (True, False):
                c = s - me if up else s - (last - me)
                for d in range(last, 0, -1) if up else range(last):

                    @pl.when((c >= 0) & (c < chunks) & ((me < d) if up else (me > d)))
                    def _(up=up, c=c, d=d):
                        sum_step(up, d, c)

            if not early:
                pl.when(s == 0)(wait_soon)

            @pl.when(s == 1)
            def _():
                for i in others:
                    other_copy(i).wait()

        also(s + 1 if early else s)
        if rs:
            per_group = chunks // groups

            @pl.when((lax.rem(s, per_group) == 0) & (s + per_group < chunks))
            def _():
                product(s // per_group + 1)

        c_own = s - lag

        @pl.when((c_own >= 0) & (c_own < chunks))
        def _():
            c = c_own
            if rs:
                total[...] = part[cut(c, slot(me, me, rolled[0]) * rows)].astype(jnp.float32)

                @pl.when(me > 0)
                def _():
                    sum_copy(True, me, c).wait_recv()
                    total[...] += up_buf[me - 1, cut(c)].astype(jnp.float32)

                @pl.when(me < last)
                def _():
                    sum_copy(False, me, c).wait_recv()
                    total[...] += dn_buf[me, cut(c)].astype(jnp.float32)

                result = middle(cut(c), total[...], ins, outs)
            else:
                result = middle(cut(c), None, ins, outs)
            if ag:
                own[cut(c)] = result.astype(own.dtype)
                here_copy(c).start()

                @pl.when(me < last)
                def _():
                    gather_copy(True, me, c, True).start()

                @pl.when(me > 0)
                def _():
                    gather_copy(False, me, c, True).start()

        if ag:
            for t in range(1, last):
                c = s - lag - t
                for up in (True, False):
                    j = me - t if up else me + t

                    @pl.when((c >= 0) & (c < chunks) & (((j >= 0) & (me < last)) if up else ((j <= last) & (me > 0))))
                    def _(up=up, c=c, j=j):
                        gather_copy(up, j, c).wait_recv()
                        gather_copy(up, j, c).start()

        return 0

    if rs:
        for j in range(n):
            left_copy(0, j).wait()
        if early:
            wait_soon()
            also(0)
        product(0)
    lax.fori_loop(0, max(chunks + lag + (last - 1 if ag else 0), steps - early), step, 0)
    finish()

    def drain(c, _):
        if rs:
            for d in range(n):

                @pl.when(me < d)
                def _(d=d):
                    sum_copy(True, d, c).wait_send()

                @pl.when(me > d)
                def _(d=d):
                    sum_copy(False, d, c).wait_send()

        if ag:
            here_copy(c).wait()
            for j in range(n):

                @pl.when(((me == last) & (j < me)) | ((me == 0) & (j > me)))
                def _(j=j):
                    gather_copy(True, j, c).wait_recv()

                @pl.when((me < last) & (j <= me))
                def _(j=j):
                    gather_copy(True, j, c).wait_send()

                @pl.when((me > 0) & (j >= me))
                def _(j=j):
                    gather_copy(False, j, c).wait_send()

        return 0

    lax.fori_loop(0, chunks, drain, 0)


def line_pass(name, summed, extras, extra_outs, middle, ag, chunks, collective_id, rows, width, rolled=(False, False), square=None, square_ins=(), square_outs=(), square_scratch=()):
    n = lax.axis_size(AXIS)
    rs = summed is not None
    size = rows // chunks
    vmem = pl.BlockSpec(memory_space=pltpu.VMEM)
    operands = (list(summed) if rs else []) + list(extras) + list(square_ins)
    scratch = []
    sems = pltpu.SemaphoreType.DMA((n, chunks))
    if rs:
        depth = summed[0].shape[1]
        shapes = [(n * rows, depth), (width, depth)] + [operand.shape for operand in operands[2:]]
        scratch += [pltpu.VMEM(shape, operand.dtype) for shape, operand in zip(shapes, operands)]
        scratch += [
            pltpu.SemaphoreType.DMA((len(operands),)),
            pltpu.SemaphoreType.DMA((n * rows // TALL, n)),
            pltpu.SemaphoreType.DMA((width // min(COLUMNS, width),)),
            pltpu.VMEM((n * rows, width), jnp.bfloat16),
            pltpu.VMEM((n - 1, rows, width), jnp.bfloat16),
            pltpu.VMEM((n - 1, rows, width), jnp.bfloat16),
            pltpu.VMEM((size, width), jnp.float32),
            sems, sems, sems, sems,
        ]
    if ag:
        scratch += [pltpu.VMEM((rows, width), jnp.bfloat16), sems, sems, sems, pltpu.SemaphoreType.DMA((chunks,))]
    shapes = ([jax.ShapeDtypeStruct((n * rows, width), jnp.bfloat16)] if ag else []) + [
        jax.ShapeDtypeStruct((rows, width), kind) for kind in extra_outs
    ] + list(square_outs)
    specs = ([pl.BlockSpec(memory_space=pl.ANY)] if ag else []) + [vmem] * (len(extra_outs) + len(square_outs))
    if square is not None:
        square = (square, len(square_ins), len(square_outs), len(square_scratch))
    moved = rows * width * 2 * (n - 1)
    return pl.pallas_call(
        functools.partial(line_body, n, chunks, rs, ag, rolled, middle, square, len(operands), len(shapes)),
        out_shape=shapes,
        in_specs=[pl.BlockSpec(memory_space=pl.ANY) if rs else vmem] * len(operands),
        out_specs=specs,
        scratch_shapes=scratch + list(square_scratch),
        compiler_params=pltpu.CompilerParams(
            collective_id=collective_id, has_side_effects=True, vmem_limit_bytes=VMEM
        ),
        cost_estimate=pl.CostEstimate(
            flops=0, bytes_accessed=moved * 40, transcendentals=0, remote_bytes_transferred=moved
        ),
        name=name,
    )(*operands)


def flipped(index, bit):
    return index + (1 << bit) - 2 * (1 << bit) * lax.rem(index // (1 << bit), 2)


def square_parts(heads, left, ins, outs, scratch):
    turned, gain, weights, other_terms, other_gain = ins
    gain_sum, grads = outs[0], outs[1:]
    terms_one, sums, sums_in, sums_send, sums_recv, sent, *rest = scratch
    line = lax.axis_index(AXIS)
    line_bits = lax.axis_size(AXIS).bit_length() - 1
    size = lax.axis_size("dp")
    bits = size.bit_length() - 1
    arrived, sems = rest[:bits], rest[bits:]
    me = lax.axis_index("dp")
    rows, wide = sent.shape[-2:]
    half = wide // 2
    pairs = arrived[0].shape[0]
    orders = list(range(bits - 1)), list(range(bits - 1))[::-1]

    def greet(barrier):
        for bit in range(bits):
            pl.semaphore_signal(barrier, inc=1, device_id={"dp": flipped(me, bit)}, device_id_type=pl.DeviceIdType.MESH)
        for bit in range(line_bits):
            pl.semaphore_signal(barrier, inc=1, device_id={AXIS: flipped(line, bit)}, device_id_type=pl.DeviceIdType.MESH)
        return bits + line_bits

    def sums_copy(bit):
        return pltpu.make_async_remote_copy(
            src_ref=sums.at[bit],
            dst_ref=sums_in.at[bit],
            send_sem=sums_send.at[bit],
            recv_sem=sums_recv.at[bit],
            device_id={AXIS: flipped(line, bit)},
            device_id_type=pl.DeviceIdType.MESH,
        )

    def send(src, dst, send_sem, recv_sem, bit):
        return pltpu.make_async_remote_copy(
            src_ref=src,
            dst_ref=dst,
            send_sem=send_sem,
            recv_sem=recv_sem,
            device_id={"dp": flipped(me, bit)},
            device_id_type=pl.DeviceIdType.MESH,
        )

    def first_copy(p):
        return send(sent.at[lax.rem(p, 2)], arrived[0].at[p], sems[0].at[p], sems[1].at[p], 0)

    def places(side, stage, at):
        found = [slice(None)] * (bits - 1)
        for done in orders[side][: stage - 1]:
            found[done] = 0
        found[orders[side][stage - 1]] = at
        return tuple(found)

    def later_copy(p, side, stage):
        columns = (slice(None), pl.ds(side * half, half))
        return send(
            arrived[0].at[(p, *places(side, stage, 1), *columns)],
            arrived[stage].at[(p, *[slice(None)] * (bits - 1 - stage), *columns)],
            sems[2 * stage].at[p, side],
            sems[2 * stage + 1].at[p, side],
            orders[side][stage - 1] + 1,
        )

    def multiply(p, u, odd):
        owner = me
        for bit in range(bits):
            set_bit = odd if bit == 0 else u[bits - 1 - bit]
            if set_bit:
                owner = flipped(owner, bit)
        block = turned[pl.ds(pl.multiple_of(owner * rows, rows), rows)]
        columns = left[:, pl.ds(pl.multiple_of(p * wide, wide), wide)]
        return jnp.dot(block, columns, preferred_element_type=jnp.float32)

    blocks = [tuple(u >> bit & 1 for bit in range(bits - 1))[::-1] for u in range(size // 2)]

    def also(s):
        @pl.when(s < pairs)
        def _():
            p = s

            @pl.when(p >= 2)
            def _():
                first_copy(p - 2).wait_send()

            for u in blocks:
                sent[(lax.rem(p, 2), *u[::-1])] = multiply(p, u, 1).astype(sent.dtype)
            first_copy(p).start()

        for stage in range(1, bits + 1):

            @pl.when((s >= stage) & (s < pairs + stage))
            def _(stage=stage):
                p = s - stage
                if stage == 1:
                    first_copy(p).wait_recv()
                    for u in blocks:
                        at = (p, *u[::-1])
                        arrived[0][at] = (multiply(p, u, 0) + arrived[0][at].astype(jnp.float32)).astype(sent.dtype)
                for side in range(2):
                    columns = (slice(None), pl.ds(side * half, half))
                    if stage > 1:
                        later_copy(p, side, stage - 1).wait_recv()
                        at = (p, *places(side, stage - 1, 0), *columns)
                        came = (p, *[slice(None)] * (bits - stage), *columns)
                        if stage < bits:
                            arrived[0][at] += arrived[stage - 1][came]
                        else:
                            result(p, side, arrived[0][at].astype(jnp.float32) + arrived[stage - 1][came].astype(jnp.float32))
                    if stage < bits:
                        later_copy(p, side, stage).start()

        for bit in range(line_bits + 1):

            @pl.when(s == pairs + bits + bit)
            def _(bit=bit):
                if bit:
                    sums_copy(bit - 1).wait()
                    sums[bit] = sums[bit - 1] + sums_in[bit - 1]
                else:
                    sums[0, 0] = terms_one[...].T[: sums.shape[2]]
                    sums[0, 1] = other_terms[...].T[: sums.shape[2]]
                if bit < line_bits:
                    sums_copy(bit).start()
                else:
                    gain_sum[0] = sums[bit, 0] / gain[...]
                    gain_sum[1] = sums[bit, 1] / other_gain[...]

    def result(p, side, summed):
        at = pl.ds(pl.multiple_of(p * wide + side * half, half), half)
        terms = jnp.sum(summed * weights[:, at].astype(jnp.float32), axis=1, keepdims=True)
        terms = jnp.broadcast_to(terms, terms_one.shape)
        if side:
            terms_one[...] += terms
        else:

            @pl.when(p == 0)
            def _():
                terms_one[...] = terms

            @pl.when(p > 0)
            def _():
                terms_one[...] += terms

        summed = summed * as_column(gain[...])
        for found in range(pairs):
            head, kind = found // (pairs // heads), found % (pairs // heads)
            where = grads[side] if kind == 0 else grads[1 + kind]
            start = head * half if kind == 0 else head * wide + side * half

            @pl.when(p == found)
            def _(where=where, start=start):
                where[:, start : start + half] = summed

    def finish():
        for p in range(max(pairs - 2, 0), pairs):
            first_copy(p).wait_send()

        def drain(p, _):
            for side in range(2):
                for stage in range(1, bits):
                    later_copy(p, side, stage).wait_send()
            return 0

        lax.fori_loop(0, pairs, drain, 0)

    return greet, also, finish, pairs + bits + line_bits + 1, False


def square_shapes(rows, heads, columns):
    size = lax.axis_size("dp")
    bits = size.bit_length() - 1
    wide = 2 * KD
    pairs = columns // wide
    twos = [2] * (bits - 1)
    sums = [pltpu.VMEM((pairs, *twos[stage:], rows, wide), jnp.bfloat16) for stage in range(bits)]
    sems = [pltpu.SemaphoreType.DMA((pairs,))] * 2
    for _ in range(1, bits):
        sems += [pltpu.SemaphoreType.DMA((pairs, 2))] * 2
    outs = [jax.ShapeDtypeStruct((2, 8, rows), jnp.float32)]
    line_bits = lax.axis_size(AXIS).bit_length() - 1
    line_sems = pltpu.SemaphoreType.DMA((max(line_bits, 1),))
    line_scratch = [
        pltpu.VMEM((rows, 128), jnp.float32),
        pltpu.VMEM((line_bits + 1, 2, 8, rows), jnp.float32),
        pltpu.VMEM((max(line_bits, 1), 2, 8, rows), jnp.float32),
        line_sems,
        line_sems,
    ]
    outs += [jax.ShapeDtypeStruct((rows, heads * cols), jnp.float32) for cols in (KD, KD, VD, VD)]
    return outs, line_scratch + [pltpu.VMEM((2, *twos, rows, wide), jnp.bfloat16)] + sums + sems


def turn_parts(blocks, left, ins, outs, scratch):
    (rows_in,), (turned,) = ins, outs
    columns = rows_in.shape[1] // blocks

    def also(s):
        for block in range(blocks):

            @pl.when(s == block)
            def _(block=block):
                at = pl.ds(block * columns, columns)
                turned[at] = rows_in[:, at].T

    return lambda barrier: 0, also, lambda: None, blocks, False


HEADS = 8
KD = 256
VD = 512
ROWS = 256


EPS_NORM = 1e-06
EPS_GROUP = 1.0
CONTRACT_ROWS = (((0,), (0,)), ((), ()))
CONTRACT_COLUMNS = (((1,), (1,)), ((), ()))


def rotary_tables(length):
    positions = np.arange(length).astype(np.float32)[:, None]
    frequency = np.float32(10000.0) ** (-np.arange(KD // 2).astype(np.float32) * np.float32(2.0 / KD))
    angles = (positions * frequency[None, :]).astype(np.float32).astype(np.float64)
    return np.cos(angles).astype(np.float32), np.sin(angles).astype(np.float32)


def turn(rows, cosine, sine):
    low, high = rows[:, : KD // 2], rows[:, KD // 2 :]
    return jnp.concatenate([low * cosine - high * sine, high * cosine + low * sine], axis=1)


def dot(left, right, dims=(((1,), (0,)), ((), ()))):
    return lax.dot_general(left, right, dims, preferred_element_type=jnp.float32)


def head_decay(decay_ref, log_ref, heads, head, reach):
    ahead = lax.broadcasted_iota(jnp.int32, decay_ref.shape, 0) - lax.broadcasted_iota(jnp.int32, decay_ref.shape, 1)
    distance = ahead + reach
    mine = lax.axis_index(AXIS) * heads + head
    value = jnp.exp(log_ref[mine] * jnp.maximum(distance, 0).astype(jnp.float32))
    decay_ref[...] = jnp.where(distance >= 0, value, 0.0)


def normed_heads(heads_out):
    centred = heads_out - jnp.mean(heads_out, axis=-1, keepdims=True)
    inverse = lax.rsqrt(jnp.mean(centred * centred, axis=-1, keepdims=True) + EPS_GROUP)
    return centred * inverse, inverse


def retention_body(block, reach, log_ref, proj, cosine, sine, segments, kept, mixed, keys, vals, decay, seg_line):
    head, row = pl.program_id(0), pl.program_id(1)
    here = pl.ds(pl.multiple_of(reach + row * block, block), block)
    window = pl.ds(pl.multiple_of(row * block, block), reach + block)

    @pl.when(row == 0)
    def _():
        head_decay(decay, log_ref, pl.num_programs(0), head, reach)
        keys[:reach] = jnp.zeros((reach, KD), keys.dtype)
        vals[:reach] = jnp.zeros((reach, VD), vals.dtype)
        seg_line[:, :reach] = jnp.full((1, reach), -1, jnp.int32)
        seg_line[:, reach:] = segments[...]

    query = turn(proj[:, :KD], cosine[...], sine[...]).astype(jnp.bfloat16)
    key = (turn(proj[:, KD : 2 * KD], cosine[...], sine[...]) * KD ** (-0.5)).astype(jnp.bfloat16)
    value = proj[:, 2 * KD : 2 * KD + VD].astype(jnp.bfloat16)
    keys[here] = key
    vals[here] = value
    kept[:, :KD] = query
    kept[:, KD : 2 * KD] = key
    kept[:, 2 * KD :] = value
    weight = jnp.where(as_column(seg_line[:, here]) == seg_line[:, window], decay[...], 0.0)
    probs = (dot(query, keys[window], CONTRACT_COLUMNS) * weight).astype(jnp.bfloat16)
    normed, _ = normed_heads(dot(probs, vals[window]))
    mixed[...] = (jax.nn.silu(proj[:, 2 * KD + VD :]) * normed).astype(jnp.bfloat16)


def retention_pull_body(
    block, reach, log_ref, kept, gate, d_branch, w_out, cosine, sine, segments, d_in, keys, vals, d_keys, d_vals, decay, seg_line
):
    head, row = pl.program_id(0), pl.num_programs(1) - 1 - pl.program_id(1)
    mine = pl.ds(pl.multiple_of(row * block, block), block)
    here = pl.ds(pl.multiple_of(reach + row * block, block), block)
    window = pl.ds(pl.multiple_of(row * block, block), reach + block)

    @pl.when(pl.program_id(1) == 0)
    def _():
        head_decay(decay, log_ref, pl.num_programs(0), head, reach)
        keys[:reach] = jnp.zeros((reach, KD), keys.dtype)
        vals[:reach] = jnp.zeros((reach, VD), vals.dtype)
        seg_line[:, :reach] = jnp.full((1, reach), -1, jnp.int32)
        seg_line[:, reach:] = segments[...]
        keys[reach:] = kept[:, KD : 2 * KD]
        vals[reach:] = kept[:, 2 * KD :]
        d_keys[...] = jnp.zeros_like(d_keys)
        d_vals[...] = jnp.zeros_like(d_vals)

    query = kept[mine, :KD]
    weight = jnp.where(as_column(seg_line[:, here]) == seg_line[:, window], decay[...], 0.0)
    probs = (dot(query, keys[window], CONTRACT_COLUMNS) * weight).astype(jnp.bfloat16)
    normed, inverse = normed_heads(dot(probs, vals[window]))
    gate_pre, upstream = gate[...], dot(d_branch[...], w_out[...])
    opened = jax.nn.sigmoid(gate_pre)
    silu = gate_pre * opened
    d_in[:, 2 * KD + VD :] = (upstream * normed * (opened + silu * (1.0 - opened))).astype(jnp.bfloat16)
    e = upstream * silu
    d_heads = e - jnp.mean(e, axis=-1, keepdims=True) - normed * jnp.mean(e * normed, axis=-1, keepdims=True)
    d_heads = (d_heads * inverse).astype(jnp.bfloat16)
    d_scores = (dot(d_heads, vals[window], CONTRACT_COLUMNS) * weight).astype(jnp.bfloat16)
    d_vals[window] += dot(probs, d_heads, CONTRACT_ROWS)
    d_keys[window] += dot(d_scores, query, CONTRACT_ROWS)
    d_query = dot(d_scores, keys[window])
    d_in[:, :KD] = turn(d_query, cosine[...], -sine[...]).astype(jnp.bfloat16)
    d_in[:, KD : 2 * KD] = (turn(d_keys[here], cosine[...], -sine[...]) * KD ** (-0.5)).astype(jnp.bfloat16)
    d_in[:, 2 * KD : 2 * KD + VD] = d_vals[here].astype(jnp.bfloat16)


def hop_valid(kind, t, device, up):
    last = lax.axis_size(AXIS) - 1
    passed = device if up else last - device
    inside = (passed >= 0) & (passed < last)
    return inside & ((passed >= t) if kind == "gather" else (passed <= t))


def hop_call(body, hop, collective_id, then=None, *, grid, in_specs, out_specs, out_shape, scratch_shapes=(), cost, name):
    def params(**more):
        return pltpu.CompilerParams(vmem_limit_bytes=VMEM, **more)

    if hop is None:
        return pl.pallas_call(
            body,
            grid=grid,
            in_specs=in_specs,
            out_specs=out_specs,
            out_shape=out_shape,
            scratch_shapes=list(scratch_shapes),
            compiler_params=params(),
            cost_estimate=cost,
            name=name,
        )
    kind, t, *arrays = hop
    n = lax.axis_size(AXIS)
    n_in, n_out, n_sent = len(in_specs), len(out_specs), len(arrays)
    rows, width = arrays[0].shape[0] // (n if n_sent == 1 else 1), arrays[0].shape[1]
    shape = jax.ShapeDtypeStruct((rows, width), arrays[0].dtype)
    added = [] if then is None else list(then)
    n_got = 1 if len(added) == 2 else 2

    def with_hop(*refs):
        ins, sources, refs = refs[:n_in], refs[n_in : n_in + n_sent], refs[n_in + n_sent :]
        terms, outs, refs = refs[: len(added)], refs[len(added) : len(added) + n_out], refs[len(added) + n_out :]
        targets, (*scratch, send_sems, recv_sems) = refs[:n_got], refs[n_got:]
        found = targets
        if added:
            *scratch, came, mine, mine_sems = scratch
            targets = [came.at[0], came.at[1]]
        if len(added) == 2:
            *scratch, kept, kept_sem = scratch
        me = lax.axis_index(AXIS)
        last = n - 1
        steps = [pl.program_id(i) for i in range(len(grid))]
        at_first = functools.reduce(jnp.logical_and, [step == 0 for step in steps])
        at_last = functools.reduce(jnp.logical_and, [step == size - 1 for step, size in zip(steps, grid)])

        def copy(way):
            source = sources[way] if n_sent == 2 else sources[0].at[pl.ds((1 if way else last) * rows, rows)]
            return pltpu.make_async_remote_copy(
                src_ref=source,
                dst_ref=targets[way],
                send_sem=send_sems.at[way],
                recv_sem=recv_sems.at[way],
                device_id={AXIS: me - 1 if way else me + 1},
                device_id_type=pl.DeviceIdType.MESH,
            )

        def term_copies():
            if not added:
                return []
            slots = [0] if len(added) == 2 else [last - t - 1, 2 + t]
            copies = [
                pltpu.make_async_copy(terms[0].at[pl.ds(slot * rows, rows)], mine.at[way], mine_sems.at[way])
                for way, slot in enumerate(slots)
            ]
            return copies + ([pltpu.make_async_copy(terms[1], kept, kept_sem)] if len(added) == 2 else [])

        @pl.when(at_first)
        def _():
            barrier = pltpu.get_barrier_semaphore()
            for way in range(2):

                @pl.when((me > 0) if way else (me < last))
                def _(way=way):
                    to = me - 1 if way else me + 1
                    pl.semaphore_signal(barrier, inc=1, device_id={AXIS: to}, device_id_type=pl.DeviceIdType.MESH)

            pl.semaphore_wait(barrier, jnp.where((me > 0) & (me < last), 2, 1))
            for way in range(2):

                @pl.when(hop_valid(kind, t, me, way == 0))
                def _(way=way):
                    copy(way).start()

            for term in term_copies():
                term.start()

        body(*ins, *outs, *scratch)

        @pl.when(at_last)
        def _():
            for term in term_copies():
                term.wait()
            if len(added) == 1:
                for way in range(2):
                    found[way][...] = mine[way]
            if len(added) == 2:
                kept[...] += mine[0].astype(jnp.float32)
            for way in range(2):

                @pl.when(hop_valid(kind, t, me, way == 0))
                def _(way=way):
                    copy(way).wait_send()

                @pl.when(hop_valid(kind, t, me + 1 if way else me - 1, way == 0))
                def _(way=way):
                    copy(way).wait_recv()
                    if len(added) == 1:
                        found[way][...] += came[way]
                    if len(added) == 2:
                        kept[...] += came[way].astype(jnp.float32)

            if len(added) == 2:
                found[0][...] = kept[...].astype(shape.dtype)

    anywhere = pl.BlockSpec(memory_space=pl.ANY)
    got = pl.BlockSpec((rows, width), lambda *_: (0, 0)) if added else anywhere
    more = []
    if len(added) == 2:
        more += [pltpu.VMEM((rows, width), jnp.float32), pltpu.SemaphoreType.DMA]
    if added:
        more += [pltpu.VMEM((2, rows, width), shape.dtype)] * 2 + [pltpu.SemaphoreType.DMA((2,))]
    call = pl.pallas_call(
        with_hop,
        grid=grid,
        in_specs=[*in_specs, *[anywhere] * (n_sent + len(added))],
        out_specs=[*out_specs, *[got] * n_got],
        out_shape=[*out_shape, *[shape] * n_got],
        scratch_shapes=[*scratch_shapes, *more, pltpu.SemaphoreType.DMA((2,)), pltpu.SemaphoreType.DMA((2,))],
        compiler_params=params(collective_id=collective_id, has_side_effects=True),
        cost_estimate=cost,
        name=name,
    )
    return lambda *operands: call(*operands, *arrays, *added)


def work(flops, moved):
    return pl.CostEstimate(flops=flops, bytes_accessed=moved, transcendentals=0)


def project_body(block, rows_in, weights, out):
    def part(q, _):
        at = pl.ds(pl.multiple_of(q * block, block), block)
        out[at] = dot(rows_in[at], weights[...])
        return 0

    lax.fori_loop(0, rows_in.shape[0] // block, part, 0)


def project(rows_in, weights, hop):
    length, depth = rows_in.shape
    columns = weights.shape[1]
    tile = min(512, columns)
    return hop_call(
        functools.partial(project_body, ROWS),
        hop,
        4,
        grid=(columns // tile,),
        in_specs=[pl.BlockSpec((length, depth), lambda c: (0, 0)), pl.BlockSpec((depth, tile), lambda c: (0, c))],
        out_specs=[pl.BlockSpec((length, tile), lambda c: (0, c))],
        out_shape=[jax.ShapeDtypeStruct((length, columns), jnp.float32)],
        cost=work(2 * length * weights.size, 2 * rows_in.size + 2 * weights.size + 4 * length * columns),
        name="project",
    )(rows_in, weights)


def hidden_body(rows_in, w_pair, w_down, both, hidden, part):
    found = dot(rows_in[...], w_pair[...])
    both[...] = found
    columns = hidden.shape[1]
    hidden[...] = (jax.nn.gelu(found[:, :columns], approximate=True) * found[:, columns:]).astype(hidden.dtype)
    part[...] = dot(hidden[...], w_down[...], CONTRACT_COLUMNS).astype(part.dtype)


def hidden_layer(rows_in, mlp_full, hop):
    length, width = rows_in.shape
    columns = mlp_full.shape[1] // 3
    once = pl.Buffered(1)
    return hop_call(
        hidden_body,
        hop,
        6,
        grid=(length // ROWS,),
        in_specs=[
            pl.BlockSpec((ROWS, width), lambda r: (r, 0)),
            pl.BlockSpec((width, 2 * columns), lambda r: (0, 0), pipeline_mode=once),
            pl.BlockSpec((width, columns), lambda r: (0, 2), pipeline_mode=once),
        ],
        out_specs=[
            pl.BlockSpec((ROWS, 2 * columns), lambda r: (r, 0)),
            pl.BlockSpec((ROWS, columns), lambda r: (r, 0)),
            pl.BlockSpec((ROWS, width), lambda r: (r, 0)),
        ],
        out_shape=[
            jax.ShapeDtypeStruct((length, 2 * columns), jnp.float32),
            jax.ShapeDtypeStruct((length, columns), jnp.bfloat16),
            jax.ShapeDtypeStruct((length, width), jnp.bfloat16),
        ],
        cost=work(6 * length * width * columns, 2 * mlp_full.size + 14 * length * columns),
        name="hidden_layer",
    )(rows_in, mlp_full, mlp_full)


def turned_body(*refs):
    *pairs, out = refs
    at = 0
    for left, right in zip(pairs[::2], pairs[1::2]):
        columns = right.shape[1]
        out[:, at : at + columns] = dot(left[...], right[...], CONTRACT_ROWS).astype(out.dtype)
        at += columns


def turned_dots(pairs, hop, collective_id, then, name):
    length, width = pairs[0][0].shape
    columns = sum(right.shape[1] for _, right in pairs)
    specs = []
    for _, right in pairs:
        specs.append(pl.BlockSpec((length, ROWS), lambda r: (0, r)))
        specs.append(pl.BlockSpec(right.shape, lambda r: (0, 0), pipeline_mode=pl.Buffered(1)))
    return hop_call(
        turned_body,
        hop,
        collective_id,
        then,
        grid=(width // ROWS,),
        in_specs=specs,
        out_specs=[pl.BlockSpec((ROWS, columns), lambda r: (r, 0))],
        out_shape=[jax.ShapeDtypeStruct((width, columns), jnp.bfloat16)],
        cost=work(2 * length * width * columns, 2 * (len(pairs) * length * width + length * columns + width * columns)),
        name=name,
    )(*[array for pair in pairs for array in pair])


def retention_inputs(segments):
    length = segments.shape[1]
    block = min(ROWS, length // 2)
    reach = length // 2
    log_decay = np.log(1.0 - 2.0 ** (-5.0 - np.arange(HEADS))).astype(np.float32)
    return block, reach, log_decay


def retention(projected, segments, heads, hop):
    length = projected.shape[0]
    block, reach, log_decay = retention_inputs(segments)
    cosine, sine = rotary_tables(length)
    per_head = projected.shape[1] // heads
    table = pl.BlockSpec((block, KD // 2), lambda h, r: (r, 0))
    return hop_call(
        functools.partial(retention_body, block, reach),
        hop,
        5,
        grid=(heads, length // block),
        in_specs=[
            pl.BlockSpec(memory_space=pltpu.SMEM),
            pl.BlockSpec((block, per_head), lambda h, r: (r, h)),
            table,
            table,
            pl.BlockSpec(segments.shape, lambda h, r: (0, 0)),
        ],
        out_specs=[
            pl.BlockSpec((block, 2 * KD + VD), lambda h, r: (r, h)),
            pl.BlockSpec((block, VD), lambda h, r: (r, h)),
        ],
        out_shape=[
            jax.ShapeDtypeStruct((length, heads * (2 * KD + VD)), jnp.bfloat16),
            jax.ShapeDtypeStruct((length, heads * VD), jnp.bfloat16),
        ],
        scratch_shapes=[
            pltpu.VMEM((reach + length, KD), jnp.bfloat16),
            pltpu.VMEM((reach + length, VD), jnp.bfloat16),
            pltpu.VMEM((block, reach + block), jnp.float32),
            pltpu.VMEM((1, reach + length), jnp.int32),
        ],
        cost=work(2 * heads * length * (reach + block) * (KD + VD), projected.size * 6),
        name="retention",
    )(log_decay, projected, cosine, sine, segments)


def retention_pull(kept, projected, d_branch, w_out, segments, heads, hop, then):
    length = kept.shape[0]
    block, reach, log_decay = retention_inputs(segments)
    cosine, sine = rotary_tables(length)
    per_head = projected.shape[1] // heads
    last = length // block - 1
    gate_block = per_head // VD
    table = pl.BlockSpec((block, KD // 2), lambda h, r: (last - r, 0))
    return hop_call(
        functools.partial(retention_pull_body, block, reach),
        hop,
        9,
        then,
        grid=(heads, last + 1),
        in_specs=[
            pl.BlockSpec(memory_space=pltpu.SMEM),
            pl.BlockSpec((length, 2 * KD + VD), lambda h, r: (0, h)),
            pl.BlockSpec((block, VD), lambda h, r: (last - r, gate_block * h + gate_block - 1)),
            pl.BlockSpec((block, d_branch.shape[1]), lambda h, r: (last - r, 0)),
            pl.BlockSpec((w_out.shape[0], VD), lambda h, r: (0, h)),
            table,
            table,
            pl.BlockSpec(segments.shape, lambda h, r: (0, 0)),
        ],
        out_specs=[pl.BlockSpec((block, per_head), lambda h, r: (last - r, h))],
        out_shape=[jax.ShapeDtypeStruct(projected.shape, jnp.bfloat16)],
        scratch_shapes=[
            pltpu.VMEM((reach + length, KD), jnp.bfloat16),
            pltpu.VMEM((reach + length, VD), jnp.bfloat16),
            pltpu.VMEM((reach + length, KD), jnp.float32),
            pltpu.VMEM((reach + length, VD), jnp.float32),
            pltpu.VMEM((block, reach + block), jnp.float32),
            pltpu.VMEM((1, reach + length), jnp.int32),
        ],
        cost=work(2 * heads * length * ((reach + block) * 3 * (KD + VD) + d_branch.shape[1] * VD), projected.size * 8),
        name="retention_pull",
    )(log_decay, kept, projected, d_branch, w_out, cosine, sine, segments)


def inverse_rms(rows):
    return lax.rsqrt(jnp.mean(rows * rows, axis=-1, keepdims=True) + EPS_NORM)


def norm_pull(unit, inverse, d_unit):
    return inverse * (d_unit - unit * jnp.mean(d_unit * unit, axis=-1, keepdims=True))


def unit_step(cut, summed, ins, outs):
    inputs = ins[0][cut].astype(jnp.float32)
    return inputs * inverse_rms(inputs)


def residual_step(cut, summed, ins, outs):
    residual = ins[0][cut].astype(jnp.float32) + summed
    outs[0][cut] = residual
    return residual * inverse_rms(residual)


def d_residual_step(cut, summed, ins, outs):
    residual = ins[0][cut]
    inverse = inverse_rms(residual)
    d_residual = ins[1][cut].astype(jnp.float32) + norm_pull(residual * inverse, inverse, summed)
    outs[0][cut] = d_residual
    return d_residual


def tokens_step(cut, summed, ins, outs):
    inputs = ins[0][cut].astype(jnp.float32)
    inverse = inverse_rms(inputs)
    grad = ins[1][cut] + norm_pull(inputs * inverse, inverse, summed)
    outs[0][cut] = grad.astype(outs[0].dtype)


def hops(up):
    n = lax.axis_size(AXIS)
    return [(i, i + 1) if up else (i + 1, i) for i in range(n - 1)]


def as_column(row):
    return jnp.broadcast_to(row, (128, row.shape[1])).T[:, :1]


def joined_body(parts, plain, *refs):
    *arrays, gain_row, out = refs
    gain = as_column(gain_row[...].astype(jnp.float32))
    at = 0
    for array, index, columns in parts:
        found = arrays[array][:, index * columns : (index + 1) * columns]
        if array < len(arrays) - plain:
            found = (found.astype(jnp.float32) * gain).astype(out.dtype)
        out[:, at : at + columns] = found
        at += columns


def join_parts(parts, plain, left, ins, outs, scratch):
    def also(s):
        @pl.when(s == 4)
        def _():
            joined_body(parts, plain, *ins, *outs)

    return lambda barrier: 0, also, lambda: None, 5, False


def joined(name, arrays, gain, parts, plain=0):
    columns = sum(part[2] for part in parts)
    return pl.pallas_call(
        functools.partial(joined_body, parts, plain),
        out_shape=jax.ShapeDtypeStruct((gain.shape[1], columns), arrays[0].dtype),
        compiler_params=pltpu.CompilerParams(vmem_limit_bytes=VMEM),
        name=name,
    )(*arrays, gain)


def mlp_pull_body(count, n, *refs):
    pieces, refs = refs[: 2 * n - 1], refs[2 * n - 1 :]
    w_down, both, hidden, unit, d_pair_out, grads, cotangent, d_pair, sems = refs
    ups, downs = pieces[:1] + pieces[1::2], pieces[:1] + pieces[2::2]
    step, me = pl.program_id(0), lax.axis_index(AXIS)
    columns = w_down.shape[1]
    rows = cotangent.shape[0] // n

    def load(k, source):
        return pltpu.make_async_copy(source, cotangent.at[pl.ds(k * rows, rows)], sems.at[k])

    @pl.when(step == 0)
    def _():
        load(0, ups[0]).start()
        for k in range(1, n):

            @pl.when(me + k < n)
            def _(k=k):
                load(k, downs[k]).start()

            @pl.when(me + k >= n)
            def _(k=k):
                load(k, ups[n - k]).start()

    for k in range(n):

        @pl.when(step == k * rows // ROWS)
        def _(k=k):
            load(k, ups[0]).wait()

    @pl.when(step < count)
    def _():
        mine = pl.ds(pl.multiple_of(step * ROWS, ROWS), ROWS)
        d_hidden = dot(cotangent[mine], w_down[...])
        gate, up = both[:, :columns], both[:, columns:]
        slope = math.sqrt(2.0 / math.pi)
        cubed = 0.044715 * gate * gate
        bent = jnp.tanh(slope * gate * (1.0 + cubed))
        half = 0.5 + 0.5 * bent
        d_gelu = half + 0.5 * gate * (1.0 - bent * bent) * slope * (1.0 + 3.0 * cubed)
        d_gate = (d_hidden * up * d_gelu).astype(d_pair.dtype)
        d_up = (d_hidden * gate * half).astype(d_pair.dtype)
        for out in (d_pair_out, d_pair.at[mine]):
            out[:, :columns] = d_gate
            out[:, columns:] = d_up

    @pl.when(step >= count)
    def _():
        at = pl.ds(pl.multiple_of((step - count) * ROWS, ROWS), ROWS)
        grads[:, : 2 * columns] = dot(unit[...], d_pair[...], CONTRACT_ROWS).astype(grads.dtype)
        grads[:, 2 * columns :] = dot(cotangent[:, at], hidden[...], CONTRACT_ROWS).astype(grads.dtype)


def mlp_pull(pieces, mlp_full, both, hidden, unit, hop, then):
    n = lax.axis_size(AXIS)
    length, width = unit.shape
    columns = hidden.shape[1]
    count = length // ROWS
    once = pl.Buffered(1)
    return hop_call(
        functools.partial(mlp_pull_body, count, n),
        hop,
        7,
        then,
        grid=(count + width // ROWS,),
        in_specs=[pl.BlockSpec(memory_space=pl.ANY)] * len(pieces)
        + [
            pl.BlockSpec((width, columns), lambda i: (0, 2), pipeline_mode=once),
            pl.BlockSpec((ROWS, 2 * columns), lambda i: (jnp.minimum(i, count - 1), 0)),
            pl.BlockSpec((length, columns), lambda i: (0, 0), pipeline_mode=once),
            pl.BlockSpec((length, ROWS), lambda i: (0, jnp.maximum(i - count, 0))),
        ],
        out_specs=[
            pl.BlockSpec((ROWS, 2 * columns), lambda i: (jnp.minimum(i, count - 1), 0)),
            pl.BlockSpec((ROWS, 3 * columns), lambda i: (jnp.maximum(i - count, 0), 0)),
        ],
        out_shape=[
            jax.ShapeDtypeStruct((length, 2 * columns), jnp.bfloat16),
            jax.ShapeDtypeStruct((width, 3 * columns), jnp.bfloat16),
        ],
        scratch_shapes=[
            pltpu.VMEM((length, width), jnp.bfloat16),
            pltpu.VMEM((length, 2 * columns), jnp.bfloat16),
            pltpu.SemaphoreType.DMA((n,)),
        ],
        cost=work(8 * length * width * columns, 2 * (3 * length * width + 4 * width * columns + 8 * length * columns)),
        name="mlp_pull",
    )(*pieces, mlp_full, both, hidden, unit)


def steps_of(part, parts):
    n = lax.axis_size(AXIS)
    return range((n - 1) * part // parts, (n - 1) * (part + 1) // parts)


def gather_hop(state, steps):
    for _ in steps[:-1]:
        up, down = state[-2:]
        state = [*state, lax.ppermute(up, AXIS, hops(True)), lax.ppermute(down, AXIS, hops(False))]
    return state, ("gather", steps[-1], *state[-2:]) if len(steps) else None


def scatter_hop(part, steps, sums=None):
    n, me = lax.axis_size(AXIS), lax.axis_index(AXIS)
    rows = part.shape[0] // n
    if sums is None:
        sums = [part[k * rows : (k + 1) * rows] for k in (n - 1, 1)] if len(steps) > 1 else [part]
    for t in steps[:-1]:
        came = [lax.ppermute(rows_out, AXIS, hops(way)) for rows_out, way in zip(sums, (True, False))]
        sums = [part[k * rows : (k + 1) * rows] + rows_in for k, rows_in in zip((n - 2 - t, 2 + t), came)]
    return ("scatter", steps[-1], *sums)


def shards(tokens,
    segment_ids,
    attn_gain,
    w_query,
    w_key,
    w_value,
    w_gate,
    w_out,
    mlp_gain,
    w_mlp_gate,
    w_mlp_up,
    w_down,
    cotangent,
):
    local_rows, width = tokens.shape
    heads = HEADS // lax.axis_size(AXIS)
    hidden_cols = w_mlp_gate.shape[1]
    gain_one = attn_gain.astype(jnp.float32)[None, :]
    gain_two = mlp_gain.astype(jnp.float32)[None, :]
    after = lax.optimization_barrier

    def gather(own):
        return lax.all_gather(own, "dp", axis=0, tiled=True)

    def scatter(grad):
        return lax.psum_scatter(grad, "dp", scatter_dimension=0, tiled=True)

    def gain_terms(weights, grads):
        return jnp.sum(weights.astype(jnp.float32) * grads.astype(jnp.float32), axis=1)

    in_parts = [(array, head, columns) for head in range(heads) for array, columns in enumerate((KD, KD, VD, VD))]
    w_in_own = joined("join_in", [w_query, w_key, w_value, w_gate], attn_gain[None, :], in_parts)
    w_in = gather(w_in_own)
    unit_one, mlp_own = line_pass(
        "gather_one",
        None,
        [tokens],
        [],
        unit_step,
        True,
        4,
        0,
        local_rows,
        width,
        square=functools.partial(join_parts, [(i, 0, hidden_cols) for i in range(3)], 1),
        square_ins=[w_mlp_gate, w_mlp_up, w_down, mlp_gain[None, :]],
        square_outs=[jax.ShapeDtypeStruct((gain_two.shape[1], 3 * hidden_cols), jnp.bfloat16)],
    )
    w_in, unit_one, w_out, cot_own, mlp_own = after((w_in, unit_one, w_out, cotangent, mlp_own))
    out_full = gather(w_out)
    cot, hop = gather_hop([cot_own, cot_own], steps_of(0, 3))
    projected, *came = project(unit_one, w_in, hop)
    cot, hop = gather_hop([*cot, *came], steps_of(1, 3))
    kept, mixed, *came = retention(projected, segment_ids, heads, hop)
    cot = [*cot, *came]
    mixed, out_full, mlp_send, *cot = after((mixed, out_full, mlp_own, *cot))
    mlp_full = gather(mlp_send)
    unit_two, residual, unit_turned = line_pass(
        "residual",
        (mixed, out_full),
        [tokens],
        [jnp.float32],
        residual_step,
        True,
        16,
        1,
        local_rows,
        width,
        (False, True),
        square=functools.partial(turn_parts, 8),
        square_ins=[unit_one],
        square_outs=[jax.ShapeDtypeStruct(unit_one.shape[::-1], unit_one.dtype)],
    )
    unit_two, mlp_full, *cot = after((unit_two, mlp_full, *cot))
    cot, hop = gather_hop(cot, steps_of(2, 3))
    both_hidden, hidden, part_down, *came = hidden_layer(unit_two, mlp_full, hop)
    hop = scatter_hop(part_down, steps_of(0, 3))
    d_pair, grad_mlp, *sums = mlp_pull([*cot, *came][1:], mlp_full, both_hidden, hidden, unit_two, hop, (part_down,))
    mlp_grad = scatter(grad_mlp)
    d_branch_one, d_residual = line_pass(
        "d_residual",
        (d_pair, mlp_full),
        [residual, cotangent],
        [jnp.float32],
        d_residual_step,
        True,
        16,
        2,
        local_rows,
        width,
        (True, False),
    )
    d_branch_one, d_residual, mlp_grad = after((d_branch_one, d_residual, mlp_grad))
    hop = scatter_hop(part_down, steps_of(1, 3), sums)
    grad_out, *sums = turned_dots([(d_branch_one, mixed)], hop, 10, (part_down,), "out_grads")
    out_grad = scatter(grad_out)
    hop = scatter_hop(part_down, steps_of(2, 3), sums)
    d_in, result = retention_pull(
        kept, projected, d_branch_one, out_full, segment_ids, heads, hop, (part_down, residual)
    )
    pair_grad, down_grad = mlp_grad[:, : 2 * hidden_cols], mlp_grad[:, 2 * hidden_cols :].astype(jnp.float32)
    terms_two = gain_terms(mlp_own[:, : 2 * hidden_cols], pair_grad)
    terms_two = jnp.broadcast_to(terms_two[:, None], (terms_two.shape[0], 128))
    pair_grad = pair_grad.astype(jnp.float32) * gain_two.T
    gate_grad, up_grad = pair_grad[:, :hidden_cols], pair_grad[:, hidden_cols:]
    d_in, result, gate_grad, up_grad, down_grad = after((d_in, result, gate_grad, up_grad, down_grad))
    square_outs, square_scratch = square_shapes(gain_one.shape[1], heads, w_in.shape[1])
    tokens_grad, gain_sums, *in_grads = line_pass(
        "tokens_grad",
        (d_in, w_in),
        [tokens, d_residual],
        [jnp.bfloat16],
        tokens_step,
        False,
        8,
        3,
        local_rows,
        width,
        square=functools.partial(square_parts, heads),
        square_ins=[unit_turned, gain_one, w_in_own, terms_two, gain_two],
        square_outs=square_outs,
        square_scratch=square_scratch,
    )
    gain_sum_one, gain_sum_two = gain_sums[0, 0], gain_sums[1, 0]
    return (
        result,
        tokens_grad,
        gain_sum_one,
        *in_grads,
        out_grad.astype(jnp.float32),
        gain_sum_two,
        gate_grad,
        up_grad,
        down_grad,
    )


def solution(mesh):
    return jax.shard_map(
        shards,
        mesh=mesh,
        in_specs=(
            P(("dp", "tensor"), None),
            P("dp", None),
            P("dp"),
            P("dp", "tensor"),
            P("dp", "tensor"),
            P("dp", "tensor"),
            P("dp", "tensor"),
            P("dp", "tensor"),
            P("dp"),
            P("dp", "tensor"),
            P("dp", "tensor"),
            P("dp", "tensor"),
            P(("dp", "tensor"), None),
        ),
        out_specs=(
            P(("dp", "tensor"), None),
            P(("dp", "tensor"), None),
            P("dp"),
            P("dp", "tensor"),
            P("dp", "tensor"),
            P("dp", "tensor"),
            P("dp", "tensor"),
            P("dp", "tensor"),
            P("dp"),
            P("dp", "tensor"),
            P("dp", "tensor"),
            P("dp", "tensor"),
        ),
        check_vma=False,
    )
```

```python
import functools
import math
import jax
import jax.numpy as jnp
import numpy as np
from jax import lax
from jax.experimental import pallas as pl
from jax.experimental.pallas import tpu as pltpu
from jax.sharding import PartitionSpec as P

AXIS = "tensor"
TALL = 256
COLUMNS = 1024
VMEM = 62 * 1024 * 1024


def line_body(n, chunks, rs, ag, rolled, middle, square, n_in, n_out, *refs):
    ins, outs, scratch = refs[:n_in], refs[n_in : n_in + n_out], list(refs[n_in + n_out :])
    me = lax.axis_index(AXIS)
    last = n - 1
    lag = last if rs else 0
    greet, also, finish, steps, early = lambda barrier: 0, lambda s: None, lambda: None, 0, False
    if rs:
        here, load_sems, left_sems, right_sems = scratch[:n_in], *scratch[n_in : n_in + 3]
        scratch = scratch[n_in + 3 :]
        outside, (left, right) = ins, here[:2]
        groups = left.shape[0] // TALL
        rows, tall, wide = left.shape[0] // n, left.shape[0] // n // groups, min(COLUMNS, right.shape[0])

        def left_copy(g, j):
            at = pl.ds(j * rows + g * tall, tall)
            return pltpu.make_async_copy(outside[0].at[at], left.at[at], left_sems.at[g, j])

        def right_copy(q):
            at = pl.ds(pl.multiple_of(q * wide, wide), wide)
            return pltpu.make_async_copy(outside[1].at[at, pl.ds(0, right.shape[1])], right.at[at], right_sems.at[q])

        def other_copy(i):
            return pltpu.make_async_copy(outside[i], here[i], load_sems.at[i])

        soon = n_in - square[1] if square is not None else n_in
        others = [i for i in range(2, n_in) if i != soon]

        def start_loads():
            starts = [left_copy(0, j) for j in range(n)]
            later = [left_copy(g, j) for g in range(1, groups) for j in range(n)]
            later += [other_copy(soon)] if soon < n_in else []
            tiles = [right_copy(q) for q in range(right.shape[0] // wide)]
            for copy in starts + (later + tiles if early else tiles + later) + [other_copy(i) for i in others]:
                copy.start()

        def wait_soon():
            for g in range(1, groups):
                for j in range(n):
                    left_copy(g, j).wait()
            if soon < n_in:
                other_copy(soon).wait()

        ins = here
    if square is not None:
        counts = square[1:]
        square_refs = ins[n_in - counts[0] :], outs[n_out - counts[1] :], scratch[len(scratch) - counts[2] :]
        ins, outs, scratch = ins[: n_in - counts[0]], outs[: n_out - counts[1]], scratch[: len(scratch) - counts[2]]
        greet, also, finish, steps, early = square[0](ins[0], *square_refs)
    if rs:
        start_loads()
        ins = ins[2:]
        part, up_buf, dn_buf, total, up_send, up_recv, dn_send, dn_recv = scratch[:8]
        scratch = scratch[8:]
    if ag:
        full, outs = outs[0], outs[1:]
        own, ag_recv, ag_up, ag_dn, ag_here = scratch[:5]
        rows = own.shape[0]
    size = rows // chunks

    def cut(c, base=0):
        return pl.ds(pl.multiple_of(base + c * size, size), size)

    def slot(j, device, turned):
        return lax.rem(j - device + n, n) if turned else j

    def product(g):
        block = jnp.concatenate([left[pl.ds(pl.multiple_of(j * rows + g * tall, tall), tall)] for j in range(n)], axis=0)

        def tile(q, _):
            @pl.when(g == 0)
            def _():
                right_copy(q).wait()

            columns = pl.ds(pl.multiple_of(q * wide, wide), wide)
            found = lax.dot_general(block, right[columns], (((1,), (1,)), ((), ())), preferred_element_type=jnp.float32)
            for j in range(n):
                part[pl.ds(pl.multiple_of(j * rows + g * tall, tall), tall), columns] = found[
                    j * tall : (j + 1) * tall
                ].astype(part.dtype)
            return 0

        lax.fori_loop(0, right.shape[0] // wide, tile, 0)

    def send(src, dst, send_sem, recv_sem, to):
        return pltpu.make_async_remote_copy(
            src_ref=src,
            dst_ref=dst,
            send_sem=send_sem,
            recv_sem=recv_sem,
            device_id={AXIS: to},
            device_id_type=pl.DeviceIdType.MESH,
        )

    barrier = pltpu.get_barrier_semaphore()

    @pl.when(me > 0)
    def _():
        pl.semaphore_signal(barrier, inc=1, device_id={AXIS: me - 1}, device_id_type=pl.DeviceIdType.MESH)

    @pl.when(me < last)
    def _():
        pl.semaphore_signal(barrier, inc=1, device_id={AXIS: me + 1}, device_id_type=pl.DeviceIdType.MESH)

    greeted = greet(barrier)
    pl.semaphore_wait(barrier, jnp.where((me > 0) & (me < last), 2, 1) + greeted)

    def sum_copy(up, d, c):
        buf, s, r, to = (up_buf, up_send, up_recv, me + 1) if up else (dn_buf, dn_send, dn_recv, me - 1)
        ref = buf.at[d - up, cut(c)]
        return send(ref, ref, s.at[d, c], r.at[d, c], to)

    def sum_step(up, d, c):
        buf = up_buf if up else dn_buf
        first = 0 if up else last
        mine = part[cut(c, slot(d, me, rolled[0]) * rows)]

        @pl.when(me == first)
        def _():
            buf[d - up, cut(c)] = mine

        @pl.when(me != first)
        def _():
            sum_copy(up, d, c).wait_recv()
            buf[d - up, cut(c)] += mine

        sum_copy(up, d, c).start()

    def gather_copy(up, j, c, from_own=False):
        to = me + 1 if up else me - 1
        src = own.at[cut(c)] if from_own else full.at[cut(c, slot(j, me, rolled[1]) * rows)]
        dst = full.at[cut(c, slot(j, to, rolled[1]) * rows)]
        return send(src, dst, (ag_up if up else ag_dn).at[j, c], ag_recv.at[j, c], to)

    def here_copy(c):
        return pltpu.make_async_copy(own.at[cut(c)], full.at[cut(c, slot(me, me, rolled[1]) * rows)], ag_here.at[c])

    def step(s, _):
        if rs:
            for up in (True, False):
                c = s - me if up else s - (last - me)
                for d in range(last, 0, -1) if up else range(last):

                    @pl.when((c >= 0) & (c < chunks) & ((me < d) if up else (me > d)))
                    def _(up=up, c=c, d=d):
                        sum_step(up, d, c)

            if not early:
                pl.when(s == 0)(wait_soon)

            @pl.when(s == 1)
            def _():
                for i in others:
                    other_copy(i).wait()

        also(s + 1 if early else s)
        if rs:
            per_group = chunks // groups

            @pl.when((lax.rem(s, per_group) == 0) & (s + per_group < chunks))
            def _():
                product(s // per_group + 1)

        c_own = s - lag

        @pl.when((c_own >= 0) & (c_own < chunks))
        def _():
            c = c_own
            if rs:
                total[...] = part[cut(c, slot(me, me, rolled[0]) * rows)].astype(jnp.float32)

                @pl.when(me > 0)
                def _():
                    sum_copy(True, me, c).wait_recv()
                    total[...] += up_buf[me - 1, cut(c)].astype(jnp.float32)

                @pl.when(me < last)
                def _():
                    sum_copy(False, me, c).wait_recv()
                    total[...] += dn_buf[me, cut(c)].astype(jnp.float32)

                result = middle(cut(c), total[...], ins, outs)
            else:
                result = middle(cut(c), None, ins, outs)
            if ag:
                own[cut(c)] = result.astype(own.dtype)
                here_copy(c).start()

                @pl.when(me < last)
                def _():
                    gather_copy(True, me, c, True).start()

                @pl.when(me > 0)
                def _():
                    gather_copy(False, me, c, True).start()

        if ag:
            for t in range(1, last):
                c = s - lag - t
                for up in (True, False):
                    j = me - t if up else me + t

                    @pl.when((c >= 0) & (c < chunks) & (((j >= 0) & (me < last)) if up else ((j <= last) & (me > 0))))
                    def _(up=up, c=c, j=j):
                        gather_copy(up, j, c).wait_recv()
                        gather_copy(up, j, c).start()

        return 0

    if rs:
        for j in range(n):
            left_copy(0, j).wait()
        if early:
            wait_soon()
            also(0)
        product(0)
    lax.fori_loop(0, max(chunks + lag + (last - 1 if ag else 0), steps - early), step, 0)
    finish()

    def drain(c, _):
        if rs:
            for d in range(n):

                @pl.when(me < d)
                def _(d=d):
                    sum_copy(True, d, c).wait_send()

                @pl.when(me > d)
                def _(d=d):
                    sum_copy(False, d, c).wait_send()

        if ag:
            here_copy(c).wait()
            for j in range(n):

                @pl.when(((me == last) & (j < me)) | ((me == 0) & (j > me)))
                def _(j=j):
                    gather_copy(True, j, c).wait_recv()

                @pl.when((me < last) & (j <= me))
                def _(j=j):
                    gather_copy(True, j, c).wait_send()

                @pl.when((me > 0) & (j >= me))
                def _(j=j):
                    gather_copy(False, j, c).wait_send()

        return 0

    lax.fori_loop(0, chunks, drain, 0)


def line_pass(name, summed, extras, extra_outs, middle, ag, chunks, collective_id, rows, width, rolled=(False, False), square=None, square_ins=(), square_outs=(), square_scratch=()):
    n = lax.axis_size(AXIS)
    rs = summed is not None
    size = rows // chunks
    vmem = pl.BlockSpec(memory_space=pltpu.VMEM)
    operands = (list(summed) if rs else []) + list(extras) + list(square_ins)
    scratch = []
    sems = pltpu.SemaphoreType.DMA((n, chunks))
    if rs:
        depth = summed[0].shape[1]
        shapes = [(n * rows, depth), (width, depth)] + [operand.shape for operand in operands[2:]]
        scratch += [pltpu.VMEM(shape, operand.dtype) for shape, operand in zip(shapes, operands)]
        scratch += [
            pltpu.SemaphoreType.DMA((len(operands),)),
            pltpu.SemaphoreType.DMA((n * rows // TALL, n)),
            pltpu.SemaphoreType.DMA((width // min(COLUMNS, width),)),
            pltpu.VMEM((n * rows, width), jnp.bfloat16),
            pltpu.VMEM((n - 1, rows, width), jnp.bfloat16),
            pltpu.VMEM((n - 1, rows, width), jnp.bfloat16),
            pltpu.VMEM((size, width), jnp.float32),
            sems, sems, sems, sems,
        ]
    if ag:
        scratch += [pltpu.VMEM((rows, width), jnp.bfloat16), sems, sems, sems, pltpu.SemaphoreType.DMA((chunks,))]
    shapes = ([jax.ShapeDtypeStruct((n * rows, width), jnp.bfloat16)] if ag else []) + [
        jax.ShapeDtypeStruct((rows, width), kind) for kind in extra_outs
    ] + list(square_outs)
    specs = ([pl.BlockSpec(memory_space=pl.ANY)] if ag else []) + [vmem] * (len(extra_outs) + len(square_outs))
    if square is not None:
        square = (square, len(square_ins), len(square_outs), len(square_scratch))
    moved = rows * width * 2 * (n - 1)
    return pl.pallas_call(
        functools.partial(line_body, n, chunks, rs, ag, rolled, middle, square, len(operands), len(shapes)),
        out_shape=shapes,
        in_specs=[pl.BlockSpec(memory_space=pl.ANY) if rs else vmem] * len(operands),
        out_specs=specs,
        scratch_shapes=scratch + list(square_scratch),
        compiler_params=pltpu.CompilerParams(
            collective_id=collective_id, has_side_effects=True, vmem_limit_bytes=VMEM
        ),
        cost_estimate=pl.CostEstimate(
            flops=0, bytes_accessed=moved * 40, transcendentals=0, remote_bytes_transferred=moved
        ),
        name=name,
    )(*operands)


def flipped(index, bit):
    return index + (1 << bit) - 2 * (1 << bit) * lax.rem(index // (1 << bit), 2)


def square_parts(heads, left, ins, outs, scratch):
    turned, gain, weights, other_terms, other_gain = ins
    gain_sum, grads = outs[0], outs[1:]
    terms_one, sums, sums_in, sums_send, sums_recv, sent, *rest = scratch
    line = lax.axis_index(AXIS)
    line_bits = lax.axis_size(AXIS).bit_length() - 1
    size = lax.axis_size("dp")
    bits = size.bit_length() - 1
    arrived, sems = rest[:bits], rest[bits:]
    me = lax.axis_index("dp")
    rows, wide = sent.shape[-2:]
    half = wide // 2
    pairs = arrived[0].shape[0]
    orders = list(range(bits - 1)), list(range(bits - 1))[::-1]

    def greet(barrier):
        for bit in range(bits):
            pl.semaphore_signal(barrier, inc=1, device_id={"dp": flipped(me, bit)}, device_id_type=pl.DeviceIdType.MESH)
        for bit in range(line_bits):
            pl.semaphore_signal(barrier, inc=1, device_id={AXIS: flipped(line, bit)}, device_id_type=pl.DeviceIdType.MESH)
        return bits + line_bits

    def sums_copy(bit):
        return pltpu.make_async_remote_copy(
            src_ref=sums.at[bit],
            dst_ref=sums_in.at[bit],
            send_sem=sums_send.at[bit],
            recv_sem=sums_recv.at[bit],
            device_id={AXIS: flipped(line, bit)},
            device_id_type=pl.DeviceIdType.MESH,
        )

    def send(src, dst, send_sem, recv_sem, bit):
        return pltpu.make_async_remote_copy(
            src_ref=src,
            dst_ref=dst,
            send_sem=send_sem,
            recv_sem=recv_sem,
            device_id={"dp": flipped(me, bit)},
            device_id_type=pl.DeviceIdType.MESH,
        )

    def first_copy(p):
        return send(sent.at[lax.rem(p, 2)], arrived[0].at[p], sems[0].at[p], sems[1].at[p], 0)

    def places(side, stage, at):
        found = [slice(None)] * (bits - 1)
        for done in orders[side][: stage - 1]:
            found[done] = 0
        found[orders[side][stage - 1]] = at
        return tuple(found)

    def later_copy(p, side, stage):
        columns = (slice(None), pl.ds(side * half, half))
        return send(
            arrived[0].at[(p, *places(side, stage, 1), *columns)],
            arrived[stage].at[(p, *[slice(None)] * (bits - 1 - stage), *columns)],
            sems[2 * stage].at[p, side],
            sems[2 * stage + 1].at[p, side],
            orders[side][stage - 1] + 1,
        )

    def multiply(p, u, odd):
        owner = me
        for bit in range(bits):
            set_bit = odd if bit == 0 else u[bits - 1 - bit]
            if set_bit:
                owner = flipped(owner, bit)
        block = turned[pl.ds(pl.multiple_of(owner * rows, rows), rows)]
        columns = left[:, pl.ds(pl.multiple_of(p * wide, wide), wide)]
        return jnp.dot(block, columns, preferred_element_type=jnp.float32)

    blocks = [tuple(u >> bit & 1 for bit in range(bits - 1))[::-1] for u in range(size // 2)]

    def also(s):
        @pl.when(s < pairs)
        def _():
            p = s

            @pl.when(p >= 2)
            def _():
                first_copy(p - 2).wait_send()

            for u in blocks:
                sent[(lax.rem(p, 2), *u[::-1])] = multiply(p, u, 1).astype(sent.dtype)
            first_copy(p).start()

        for stage in range(1, bits + 1):

            @pl.when((s >= stage) & (s < pairs + stage))
            def _(stage=stage):
                p = s - stage
                if stage == 1:
                    first_copy(p).wait_recv()
                    for u in blocks:
                        at = (p, *u[::-1])
                        arrived[0][at] = (multiply(p, u, 0) + arrived[0][at].astype(jnp.float32)).astype(sent.dtype)
                for side in range(2):
                    columns = (slice(None), pl.ds(side * half, half))
                    if stage > 1:
                        later_copy(p, side, stage - 1).wait_recv()
                        at = (p, *places(side, stage - 1, 0), *columns)
                        came = (p, *[slice(None)] * (bits - stage), *columns)
                        if stage < bits:
                            arrived[0][at] += arrived[stage - 1][came]
                        else:
                            result(p, side, arrived[0][at].astype(jnp.float32) + arrived[stage - 1][came].astype(jnp.float32))
                    if stage < bits:
                        later_copy(p, side, stage).start()

        for bit in range(line_bits + 1):

            @pl.when(s == pairs + bits + bit)
            def _(bit=bit):
                if bit:
                    sums_copy(bit - 1).wait()
                    sums[bit] = sums[bit - 1] + sums_in[bit - 1]
                else:
                    sums[0, 0] = terms_one[...].T[: sums.shape[2]]
                    sums[0, 1] = other_terms[...].T[: sums.shape[2]]
                if bit < line_bits:
                    sums_copy(bit).start()
                else:
                    gain_sum[0] = sums[bit, 0] / as_row(gain)
                    gain_sum[1] = sums[bit, 1] / as_row(other_gain)

    def result(p, side, summed):
        at = pl.ds(pl.multiple_of(p * wide + side * half, half), half)
        terms = jnp.sum(summed * weights[:, at].astype(jnp.float32), axis=1, keepdims=True)
        terms = jnp.broadcast_to(terms, terms_one.shape)
        if side:
            terms_one[...] += terms
        else:

            @pl.when(p == 0)
            def _():
                terms_one[...] = terms

            @pl.when(p > 0)
            def _():
                terms_one[...] += terms

        summed = summed * as_column(as_row(gain))
        for found in range(pairs):
            head, kind = found // (pairs // heads), found % (pairs // heads)
            where = grads[side] if kind == 0 else grads[1 + kind]
            start = head * half if kind == 0 else head * wide + side * half

            @pl.when(p == found)
            def _(where=where, start=start):
                where[:, start : start + half] = summed

    def finish():
        for p in range(max(pairs - 2, 0), pairs):
            first_copy(p).wait_send()

        def drain(p, _):
            for side in range(2):
                for stage in range(1, bits):
                    later_copy(p, side, stage).wait_send()
            return 0

        lax.fori_loop(0, pairs, drain, 0)

    return greet, also, finish, pairs + bits + line_bits + 1, False


def square_shapes(rows, heads, columns):
    size = lax.axis_size("dp")
    bits = size.bit_length() - 1
    wide = 2 * KD
    pairs = columns // wide
    twos = [2] * (bits - 1)
    sums = [pltpu.VMEM((pairs, *twos[stage:], rows, wide), jnp.bfloat16) for stage in range(bits)]
    sems = [pltpu.SemaphoreType.DMA((pairs,))] * 2
    for _ in range(1, bits):
        sems += [pltpu.SemaphoreType.DMA((pairs, 2))] * 2
    outs = [jax.ShapeDtypeStruct((2, 8, rows), jnp.float32)]
    line_bits = lax.axis_size(AXIS).bit_length() - 1
    line_sems = pltpu.SemaphoreType.DMA((max(line_bits, 1),))
    line_scratch = [
        pltpu.VMEM((rows, 128), jnp.float32),
        pltpu.VMEM((line_bits + 1, 2, 8, rows), jnp.float32),
        pltpu.VMEM((max(line_bits, 1), 2, 8, rows), jnp.float32),
        line_sems,
        line_sems,
    ]
    outs += [jax.ShapeDtypeStruct((rows, heads * cols), jnp.float32) for cols in (KD, KD, VD, VD)]
    return outs, line_scratch + [pltpu.VMEM((2, *twos, rows, wide), jnp.bfloat16)] + sums + sems


def turn_parts(blocks, left, ins, outs, scratch):
    (rows_in,), (turned,) = ins, outs
    columns = rows_in.shape[1] // blocks

    def also(s):
        for block in range(blocks):

            @pl.when(s == block)
            def _(block=block):
                at = pl.ds(block * columns, columns)
                turned[at] = rows_in[:, at].T

    return lambda barrier: 0, also, lambda: None, blocks, False


HEADS = 8
KD = 256
VD = 512
ROWS = 256


EPS_NORM = 1e-06
EPS_GROUP = 1.0
CONTRACT_ROWS = (((0,), (0,)), ((), ()))
CONTRACT_COLUMNS = (((1,), (1,)), ((), ()))


def rotary_tables(length):
    positions = np.arange(length).astype(np.float32)[:, None]
    frequency = np.float32(10000.0) ** (-np.arange(KD // 2).astype(np.float32) * np.float32(2.0 / KD))
    angles = (positions * frequency[None, :]).astype(np.float32).astype(np.float64)
    return np.cos(angles).astype(np.float32), np.sin(angles).astype(np.float32)


def turn(rows, cosine, sine):
    low, high = rows[:, : KD // 2], rows[:, KD // 2 :]
    return jnp.concatenate([low * cosine - high * sine, high * cosine + low * sine], axis=1)


def dot(left, right, dims=(((1,), (0,)), ((), ()))):
    return lax.dot_general(left, right, dims, preferred_element_type=jnp.float32)


def head_decay(decay_ref, log_ref, heads, head, reach):
    ahead = lax.broadcasted_iota(jnp.int32, decay_ref.shape, 0) - lax.broadcasted_iota(jnp.int32, decay_ref.shape, 1)
    distance = ahead + reach
    mine = lax.axis_index(AXIS) * heads + head
    value = jnp.exp(log_ref[mine] * jnp.maximum(distance, 0).astype(jnp.float32))
    decay_ref[...] = jnp.where(distance >= 0, value, 0.0)


def normed_heads(heads_out):
    centred = heads_out - jnp.mean(heads_out, axis=-1, keepdims=True)
    inverse = lax.rsqrt(jnp.mean(centred * centred, axis=-1, keepdims=True) + EPS_GROUP)
    return centred * inverse, inverse


def retention_body(block, reach, log_ref, proj, cosine, sine, segments, *refs):
    *arrays, kept, mixed, joined, keys, vals, decay, seg_line = refs
    head, row = pl.program_id(0), pl.program_id(1)
    here = pl.ds(pl.multiple_of(reach + row * block, block), block)
    window = pl.ds(pl.multiple_of(row * block, block), reach + block)

    @pl.when((head == 0) & (row == 0))
    def _():
        joined_body([(i, 0, arrays[i].shape[1]) for i in range(len(arrays) - 1)], 1, *arrays, joined)

    @pl.when(row == 0)
    def _():
        head_decay(decay, log_ref, pl.num_programs(0), head, reach)
        keys[:reach] = jnp.zeros((reach, KD), keys.dtype)
        vals[:reach] = jnp.zeros((reach, VD), vals.dtype)
        seg_line[:, :reach] = jnp.full((1, reach), -1, jnp.int32)
        seg_line[:, reach:] = segments[...]

    query = turn(proj[:, :KD], cosine[...], sine[...]).astype(jnp.bfloat16)
    key = (turn(proj[:, KD : 2 * KD], cosine[...], sine[...]) * KD ** (-0.5)).astype(jnp.bfloat16)
    value = proj[:, 2 * KD : 2 * KD + VD].astype(jnp.bfloat16)
    keys[here] = key
    vals[here] = value
    kept[:, :KD] = query
    kept[:, KD : 2 * KD] = key
    kept[:, 2 * KD :] = value
    weight = jnp.where(as_column(seg_line[:, here]) == seg_line[:, window], decay[...], 0.0)
    probs = (dot(query, keys[window], CONTRACT_COLUMNS) * weight).astype(jnp.bfloat16)
    normed, _ = normed_heads(dot(probs, vals[window]))
    mixed[...] = (jax.nn.silu(proj[:, 2 * KD + VD :]) * normed).astype(jnp.bfloat16)


def retention_pull_body(
    block, reach, log_ref, kept, gate, d_branch, w_out, cosine, sine, segments, d_in, keys, vals, d_keys, d_vals, decay, seg_line
):
    head, row = pl.program_id(0), pl.num_programs(1) - 1 - pl.program_id(1)
    mine = pl.ds(pl.multiple_of(row * block, block), block)
    here = pl.ds(pl.multiple_of(reach + row * block, block), block)
    window = pl.ds(pl.multiple_of(row * block, block), reach + block)

    @pl.when(pl.program_id(1) == 0)
    def _():
        head_decay(decay, log_ref, pl.num_programs(0), head, reach)
        keys[:reach] = jnp.zeros((reach, KD), keys.dtype)
        vals[:reach] = jnp.zeros((reach, VD), vals.dtype)
        seg_line[:, :reach] = jnp.full((1, reach), -1, jnp.int32)
        seg_line[:, reach:] = segments[...]
        keys[reach:] = kept[:, KD : 2 * KD]
        vals[reach:] = kept[:, 2 * KD :]
        d_keys[...] = jnp.zeros_like(d_keys)
        d_vals[...] = jnp.zeros_like(d_vals)

    query = kept[mine, :KD]
    weight = jnp.where(as_column(seg_line[:, here]) == seg_line[:, window], decay[...], 0.0)
    probs = (dot(query, keys[window], CONTRACT_COLUMNS) * weight).astype(jnp.bfloat16)
    normed, inverse = normed_heads(dot(probs, vals[window]))
    gate_pre, upstream = gate[...], dot(d_branch[...], w_out[...])
    opened = jax.nn.sigmoid(gate_pre)
    silu = gate_pre * opened
    d_in[:, 2 * KD + VD :] = (upstream * normed * (opened + silu * (1.0 - opened))).astype(jnp.bfloat16)
    e = upstream * silu
    d_heads = e - jnp.mean(e, axis=-1, keepdims=True) - normed * jnp.mean(e * normed, axis=-1, keepdims=True)
    d_heads = (d_heads * inverse).astype(jnp.bfloat16)
    d_scores = (dot(d_heads, vals[window], CONTRACT_COLUMNS) * weight).astype(jnp.bfloat16)
    d_vals[window] += dot(probs, d_heads, CONTRACT_ROWS)
    d_keys[window] += dot(d_scores, query, CONTRACT_ROWS)
    d_query = dot(d_scores, keys[window])
    d_in[:, :KD] = turn(d_query, cosine[...], -sine[...]).astype(jnp.bfloat16)
    d_in[:, KD : 2 * KD] = (turn(d_keys[here], cosine[...], -sine[...]) * KD ** (-0.5)).astype(jnp.bfloat16)
    d_in[:, 2 * KD : 2 * KD + VD] = d_vals[here].astype(jnp.bfloat16)


def hop_valid(kind, t, device, up):
    last = lax.axis_size(AXIS) - 1
    passed = device if up else last - device
    inside = (passed >= 0) & (passed < last)
    return inside & ((passed >= t) if kind == "gather" else (passed <= t))


def hop_call(body, hop, collective_id, then=None, resident=(), *, grid, in_specs, out_specs, out_shape, scratch_shapes=(), cost, name):
    def params(**more):
        return pltpu.CompilerParams(vmem_limit_bytes=VMEM, **more)

    if hop is None:
        return pl.pallas_call(
            body,
            grid=grid,
            in_specs=in_specs,
            out_specs=out_specs,
            out_shape=out_shape,
            scratch_shapes=list(scratch_shapes),
            compiler_params=params(),
            cost_estimate=cost,
            name=name,
        )
    kind, t, *arrays = hop
    n = lax.axis_size(AXIS)
    n_in, n_out, n_sent = len(in_specs), len(out_specs), len(arrays)
    rows, width = arrays[0].shape[0] // (n if n_sent == 1 else 1), arrays[0].shape[1]
    shape = jax.ShapeDtypeStruct((rows, width), arrays[0].dtype)
    added = [] if then is None else list(then)
    n_got = 1 if len(added) == 2 else 2

    def with_hop(*refs):
        ins, sources, refs = refs[:n_in], refs[n_in : n_in + n_sent], refs[n_in + n_sent :]
        terms, outs, refs = refs[: len(added)], refs[len(added) : len(added) + n_out], refs[len(added) + n_out :]
        targets, (*scratch, send_sems, recv_sems, load_sems) = refs[:n_got], refs[n_got:]
        held, scratch = scratch[: len(resident)], scratch[len(resident) :]
        found = targets
        if added:
            *scratch, came, mine, mine_sems = scratch
            targets = [came.at[0], came.at[1]]
        if len(added) == 2:
            *scratch, kept, kept_sem = scratch
        me = lax.axis_index(AXIS)
        last = n - 1
        steps = [pl.program_id(i) for i in range(len(grid))]
        at_first = functools.reduce(jnp.logical_and, [step == 0 for step in steps])
        at_last = functools.reduce(jnp.logical_and, [step == size - 1 for step, size in zip(steps, grid)])

        def copy(way):
            source = sources[way] if n_sent == 2 else sources[0].at[pl.ds((1 if way else last) * rows, rows)]
            return pltpu.make_async_remote_copy(
                src_ref=source,
                dst_ref=targets[way],
                send_sem=send_sems.at[way],
                recv_sem=recv_sems.at[way],
                device_id={AXIS: me - 1 if way else me + 1},
                device_id_type=pl.DeviceIdType.MESH,
            )

        def term_copies():
            if not added:
                return []
            slots = [0] if len(added) == 2 else [last - t - 1, 2 + t]
            copies = [
                pltpu.make_async_copy(terms[0].at[pl.ds(slot * rows, rows)], mine.at[way], mine_sems.at[way])
                for way, slot in enumerate(slots)
            ]
            return copies + ([pltpu.make_async_copy(terms[1], kept, kept_sem)] if len(added) == 2 else [])

        @pl.when(at_first)
        def _():
            barrier = pltpu.get_barrier_semaphore()
            for way in range(2):

                @pl.when((me > 0) if way else (me < last))
                def _(way=way):
                    to = me - 1 if way else me + 1
                    pl.semaphore_signal(barrier, inc=1, device_id={AXIS: to}, device_id_type=pl.DeviceIdType.MESH)

            pl.semaphore_wait(barrier, jnp.where((me > 0) & (me < last), 2, 1))
            for way in range(2):

                @pl.when(hop_valid(kind, t, me, way == 0))
                def _(way=way):
                    copy(way).start()

            loads = [
                pltpu.make_async_copy(ins[i].at[:, pl.ds(column, ref.shape[1])], ref, load_sems.at[k])
                for k, (i, column, ref) in enumerate(zip(resident, columns, held))
            ]
            for load in loads:
                load.start()
            for term in term_copies():
                term.start()
            for load in loads:
                load.wait()

        inside = list(ins)
        for i, ref in zip(resident, held):
            inside[i] = ref
        body(*inside, *outs, *scratch)

        @pl.when(at_last)
        def _():
            for term in term_copies():
                term.wait()
            if len(added) == 1:
                for way in range(2):
                    found[way][...] = mine[way]
            if len(added) == 2:
                kept[...] += mine[0].astype(jnp.float32)
            for way in range(2):

                @pl.when(hop_valid(kind, t, me, way == 0))
                def _(way=way):
                    copy(way).wait_send()

                @pl.when(hop_valid(kind, t, me + 1 if way else me - 1, way == 0))
                def _(way=way):
                    copy(way).wait_recv()
                    if len(added) == 1:
                        found[way][...] += came[way]
                    if len(added) == 2:
                        kept[...] += came[way].astype(jnp.float32)

            if len(added) == 2:
                found[0][...] = kept[...].astype(shape.dtype)

    anywhere = pl.BlockSpec(memory_space=pl.ANY)
    blocks = [in_specs[i].block_shape for i in resident]
    columns = [in_specs[i].index_map(*[0] * len(grid))[1] * block[1] for i, block in zip(resident, blocks)]
    in_specs = [anywhere if i in resident else spec for i, spec in enumerate(in_specs)]
    got = pl.BlockSpec((rows, width), lambda *_: (0, 0)) if added else anywhere
    more = []
    if len(added) == 2:
        more += [pltpu.VMEM((rows, width), jnp.float32), pltpu.SemaphoreType.DMA]
    if added:
        more += [pltpu.VMEM((2, rows, width), shape.dtype)] * 2 + [pltpu.SemaphoreType.DMA((2,))]
    call = pl.pallas_call(
        with_hop,
        grid=grid,
        in_specs=[*in_specs, *[anywhere] * (n_sent + len(added))],
        out_specs=[*out_specs, *[got] * n_got],
        out_shape=[*out_shape, *[shape] * n_got],
        scratch_shapes=[
            *[pltpu.VMEM(block, jnp.bfloat16) for block in blocks],
            *scratch_shapes,
            *more,
            pltpu.SemaphoreType.DMA((2,)),
            pltpu.SemaphoreType.DMA((2,)),
            pltpu.SemaphoreType.DMA((max(len(blocks), 1),)),
        ],
        compiler_params=params(collective_id=collective_id, has_side_effects=True),
        cost_estimate=cost,
        name=name,
    )
    return lambda *operands: call(*operands, *arrays, *added)


def work(flops, moved):
    return pl.CostEstimate(flops=flops, bytes_accessed=moved, transcendentals=0)


def project_body(block, rows_in, weights, out):
    def part(q, _):
        at = pl.ds(pl.multiple_of(q * block, block), block)
        out[at] = dot(rows_in[at], weights[...])
        return 0

    lax.fori_loop(0, rows_in.shape[0] // block, part, 0)


def project(rows_in, weights, hop):
    length, depth = rows_in.shape
    columns = weights.shape[1]
    tile = min(512, columns)
    return hop_call(
        functools.partial(project_body, ROWS),
        hop,
        4,
        resident=(0,),
        grid=(columns // tile,),
        in_specs=[pl.BlockSpec((length, depth), lambda c: (0, 0)), pl.BlockSpec((depth, tile), lambda c: (0, c))],
        out_specs=[pl.BlockSpec((length, tile), lambda c: (0, c))],
        out_shape=[jax.ShapeDtypeStruct((length, columns), jnp.float32)],
        cost=work(2 * length * weights.size, 2 * rows_in.size + 2 * weights.size + 4 * length * columns),
        name="project",
    )(rows_in, weights)


def hidden_body(rows_in, w_pair, w_down, both, hidden, part):
    found = dot(rows_in[...], w_pair[...])
    both[...] = found
    columns = hidden.shape[1]
    hidden[...] = (jax.nn.gelu(found[:, :columns], approximate=True) * found[:, columns:]).astype(hidden.dtype)
    part[...] = dot(hidden[...], w_down[...], CONTRACT_COLUMNS).astype(part.dtype)


def hidden_layer(rows_in, mlp_full, hop):
    length, width = rows_in.shape
    columns = mlp_full.shape[1] // 3
    once = pl.Buffered(1)
    return hop_call(
        hidden_body,
        hop,
        6,
        resident=(1, 2),
        grid=(length // ROWS,),
        in_specs=[
            pl.BlockSpec((ROWS, width), lambda r: (r, 0)),
            pl.BlockSpec((width, 2 * columns), lambda r: (0, 0), pipeline_mode=once),
            pl.BlockSpec((width, columns), lambda r: (0, 2), pipeline_mode=once),
        ],
        out_specs=[
            pl.BlockSpec((ROWS, 2 * columns), lambda r: (r, 0)),
            pl.BlockSpec((ROWS, columns), lambda r: (r, 0)),
            pl.BlockSpec((ROWS, width), lambda r: (r, 0)),
        ],
        out_shape=[
            jax.ShapeDtypeStruct((length, 2 * columns), jnp.float32),
            jax.ShapeDtypeStruct((length, columns), jnp.bfloat16),
            jax.ShapeDtypeStruct((length, width), jnp.bfloat16),
        ],
        cost=work(6 * length * width * columns, 2 * mlp_full.size + 14 * length * columns),
        name="hidden_layer",
    )(rows_in, mlp_full, mlp_full)


def turned_body(*refs):
    *pairs, out = refs
    at = 0
    for left, right in zip(pairs[::2], pairs[1::2]):
        columns = right.shape[1]
        out[:, at : at + columns] = dot(left[...], right[...], CONTRACT_ROWS).astype(out.dtype)
        at += columns


def turned_dots(pairs, hop, collective_id, then, name):
    length, width = pairs[0][0].shape
    columns = sum(right.shape[1] for _, right in pairs)
    specs = []
    for _, right in pairs:
        specs.append(pl.BlockSpec((length, ROWS), lambda r: (0, r)))
        specs.append(pl.BlockSpec(right.shape, lambda r: (0, 0), pipeline_mode=pl.Buffered(1)))
    return hop_call(
        turned_body,
        hop,
        collective_id,
        then,
        tuple(range(1, 2 * len(pairs), 2)),
        grid=(width // ROWS,),
        in_specs=specs,
        out_specs=[pl.BlockSpec((ROWS, columns), lambda r: (r, 0))],
        out_shape=[jax.ShapeDtypeStruct((width, columns), jnp.bfloat16)],
        cost=work(2 * length * width * columns, 2 * (len(pairs) * length * width + length * columns + width * columns)),
        name=name,
    )(*[array for pair in pairs for array in pair])


def retention_inputs(segments):
    length = segments.shape[1]
    block = min(ROWS, length // 2)
    reach = length // 2
    log_decay = np.log(1.0 - 2.0 ** (-5.0 - np.arange(HEADS))).astype(np.float32)
    return block, reach, log_decay


def retention(projected, segments, heads, hop, to_join):
    length = projected.shape[0]
    block, reach, log_decay = retention_inputs(segments)
    cosine, sine = rotary_tables(length)
    per_head = projected.shape[1] // heads
    joined = (to_join[0].shape[0], sum(array.shape[1] for array in to_join[:-1]))
    table = pl.BlockSpec((block, KD // 2), lambda h, r: (r, 0))
    return hop_call(
        functools.partial(retention_body, block, reach),
        hop,
        5,
        resident=tuple(range(5, 4 + len(to_join))),
        grid=(heads, length // block),
        in_specs=[
            pl.BlockSpec(memory_space=pltpu.SMEM),
            pl.BlockSpec((block, per_head), lambda h, r: (r, h)),
            table,
            table,
            pl.BlockSpec(segments.shape, lambda h, r: (0, 0)),
            *[pl.BlockSpec(array.shape, lambda h, r: (0, 0)) for array in to_join[:-1]],
            pl.BlockSpec(to_join[-1].shape, lambda h, r: (0,)),
        ],
        out_specs=[
            pl.BlockSpec((block, 2 * KD + VD), lambda h, r: (r, h)),
            pl.BlockSpec((block, VD), lambda h, r: (r, h)),
            pl.BlockSpec(joined, lambda h, r: (0, 0)),
        ],
        out_shape=[
            jax.ShapeDtypeStruct((length, heads * (2 * KD + VD)), jnp.bfloat16),
            jax.ShapeDtypeStruct((length, heads * VD), jnp.bfloat16),
            jax.ShapeDtypeStruct(joined, jnp.bfloat16),
        ],
        scratch_shapes=[
            pltpu.VMEM((reach + length, KD), jnp.bfloat16),
            pltpu.VMEM((reach + length, VD), jnp.bfloat16),
            pltpu.VMEM((block, reach + block), jnp.float32),
            pltpu.VMEM((1, reach + length), jnp.int32),
        ],
        cost=work(2 * heads * length * (reach + block) * (KD + VD), projected.size * 6),
        name="retention",
    )(log_decay, projected, cosine, sine, segments, *to_join)


def retention_pull(kept, projected, d_branch, w_out, segments, heads, hop, then):
    length = kept.shape[0]
    block, reach, log_decay = retention_inputs(segments)
    cosine, sine = rotary_tables(length)
    per_head = projected.shape[1] // heads
    last = length // block - 1
    gate_block = per_head // VD
    table = pl.BlockSpec((block, KD // 2), lambda h, r: (last - r, 0))
    return hop_call(
        functools.partial(retention_pull_body, block, reach),
        hop,
        9,
        then,
        grid=(heads, last + 1),
        in_specs=[
            pl.BlockSpec(memory_space=pltpu.SMEM),
            pl.BlockSpec((length, 2 * KD + VD), lambda h, r: (0, h)),
            pl.BlockSpec((block, VD), lambda h, r: (last - r, gate_block * h + gate_block - 1)),
            pl.BlockSpec((block, d_branch.shape[1]), lambda h, r: (last - r, 0)),
            pl.BlockSpec((w_out.shape[0], VD), lambda h, r: (0, h)),
            table,
            table,
            pl.BlockSpec(segments.shape, lambda h, r: (0, 0)),
        ],
        out_specs=[pl.BlockSpec((block, per_head), lambda h, r: (last - r, h))],
        out_shape=[jax.ShapeDtypeStruct(projected.shape, jnp.bfloat16)],
        scratch_shapes=[
            pltpu.VMEM((reach + length, KD), jnp.bfloat16),
            pltpu.VMEM((reach + length, VD), jnp.bfloat16),
            pltpu.VMEM((reach + length, KD), jnp.float32),
            pltpu.VMEM((reach + length, VD), jnp.float32),
            pltpu.VMEM((block, reach + block), jnp.float32),
            pltpu.VMEM((1, reach + length), jnp.int32),
        ],
        cost=work(2 * heads * length * ((reach + block) * 3 * (KD + VD) + d_branch.shape[1] * VD), projected.size * 8),
        name="retention_pull",
    )(log_decay, kept, projected, d_branch, w_out, cosine, sine, segments)


def inverse_rms(rows):
    return lax.rsqrt(jnp.mean(rows * rows, axis=-1, keepdims=True) + EPS_NORM)


def norm_pull(unit, inverse, d_unit):
    return inverse * (d_unit - unit * jnp.mean(d_unit * unit, axis=-1, keepdims=True))


def unit_step(cut, summed, ins, outs):
    inputs = ins[0][cut].astype(jnp.float32)
    return inputs * inverse_rms(inputs)


def residual_step(cut, summed, ins, outs):
    residual = ins[0][cut].astype(jnp.float32) + summed
    outs[0][cut] = residual
    return residual * inverse_rms(residual)


def d_residual_step(cut, summed, ins, outs):
    residual = ins[0][cut]
    inverse = inverse_rms(residual)
    d_residual = ins[1][cut].astype(jnp.float32) + norm_pull(residual * inverse, inverse, summed)
    outs[0][cut] = d_residual
    return d_residual


def tokens_step(cut, summed, ins, outs):
    inputs = ins[0][cut].astype(jnp.float32)
    inverse = inverse_rms(inputs)
    grad = ins[1][cut] + norm_pull(inputs * inverse, inverse, summed)
    outs[0][cut] = grad.astype(outs[0].dtype)


def hops(up):
    n = lax.axis_size(AXIS)
    return [(i, i + 1) if up else (i + 1, i) for i in range(n - 1)]


def as_row(ref):
    return ref[...].astype(jnp.float32).reshape(1, -1)


def as_column(row):
    return jnp.broadcast_to(row, (128, row.shape[1])).T[:, :1]


def joined_body(parts, plain, *refs):
    *arrays, gain_row, out = refs
    gain = as_column(as_row(gain_row))
    at = 0
    for array, index, columns in parts:
        found = arrays[array][:, index * columns : (index + 1) * columns]
        if array < len(arrays) - plain:
            found = (found.astype(jnp.float32) * gain).astype(out.dtype)
        out[:, at : at + columns] = found
        at += columns


def joined(name, arrays, gain, parts, plain=0):
    columns = sum(part[2] for part in parts)
    return pl.pallas_call(
        functools.partial(joined_body, parts, plain),
        out_shape=jax.ShapeDtypeStruct((gain.shape[0], columns), arrays[0].dtype),
        compiler_params=pltpu.CompilerParams(vmem_limit_bytes=VMEM),
        name=name,
    )(*arrays, gain)


def mlp_pull_body(count, n, *refs):
    pieces, refs = refs[: 2 * n - 1], refs[2 * n - 1 :]
    w_down, both, hidden, unit, d_pair_out, grads, cotangent, d_pair, sems = refs
    ups, downs = pieces[:1] + pieces[1::2], pieces[:1] + pieces[2::2]
    step, me = pl.program_id(0), lax.axis_index(AXIS)
    columns = w_down.shape[1]
    rows = cotangent.shape[0] // n

    def load(k, source):
        return pltpu.make_async_copy(source, cotangent.at[pl.ds(k * rows, rows)], sems.at[k])

    @pl.when(step == 0)
    def _():
        load(0, ups[0]).start()
        for k in range(1, n):

            @pl.when(me + k < n)
            def _(k=k):
                load(k, downs[k]).start()

            @pl.when(me + k >= n)
            def _(k=k):
                load(k, ups[n - k]).start()

    for k in range(n):

        @pl.when(step == k * rows // ROWS)
        def _(k=k):
            load(k, ups[0]).wait()

    @pl.when(step < count)
    def _():
        mine = pl.ds(pl.multiple_of(step * ROWS, ROWS), ROWS)
        d_hidden = dot(cotangent[mine], w_down[...])
        gate, up = both[:, :columns], both[:, columns:]
        slope = math.sqrt(2.0 / math.pi)
        cubed = 0.044715 * gate * gate
        bent = jnp.tanh(slope * gate * (1.0 + cubed))
        half = 0.5 + 0.5 * bent
        d_gelu = half + 0.5 * gate * (1.0 - bent * bent) * slope * (1.0 + 3.0 * cubed)
        d_gate = (d_hidden * up * d_gelu).astype(d_pair.dtype)
        d_up = (d_hidden * gate * half).astype(d_pair.dtype)
        for out in (d_pair_out, d_pair.at[mine]):
            out[:, :columns] = d_gate
            out[:, columns:] = d_up

    @pl.when(step >= count)
    def _():
        at = pl.ds(pl.multiple_of((step - count) * ROWS, ROWS), ROWS)
        grads[:, : 2 * columns] = dot(unit[...], d_pair[...], CONTRACT_ROWS).astype(grads.dtype)
        grads[:, 2 * columns :] = dot(cotangent[:, at], hidden[...], CONTRACT_ROWS).astype(grads.dtype)


def mlp_pull(pieces, mlp_full, both, hidden, unit, hop, then):
    n = lax.axis_size(AXIS)
    length, width = unit.shape
    columns = hidden.shape[1]
    count = length // ROWS
    once = pl.Buffered(1)
    return hop_call(
        functools.partial(mlp_pull_body, count, n),
        hop,
        7,
        then,
        (len(pieces), len(pieces) + 2),
        grid=(count + width // ROWS,),
        in_specs=[pl.BlockSpec(memory_space=pl.ANY)] * len(pieces)
        + [
            pl.BlockSpec((width, columns), lambda i: (0, 2), pipeline_mode=once),
            pl.BlockSpec((ROWS, 2 * columns), lambda i: (jnp.minimum(i, count - 1), 0)),
            pl.BlockSpec((length, columns), lambda i: (0, 0), pipeline_mode=once),
            pl.BlockSpec((length, ROWS), lambda i: (0, jnp.maximum(i - count, 0))),
        ],
        out_specs=[
            pl.BlockSpec((ROWS, 2 * columns), lambda i: (jnp.minimum(i, count - 1), 0)),
            pl.BlockSpec((ROWS, 3 * columns), lambda i: (jnp.maximum(i - count, 0), 0)),
        ],
        out_shape=[
            jax.ShapeDtypeStruct((length, 2 * columns), jnp.bfloat16),
            jax.ShapeDtypeStruct((width, 3 * columns), jnp.bfloat16),
        ],
        scratch_shapes=[
            pltpu.VMEM((length, width), jnp.bfloat16),
            pltpu.VMEM((length, 2 * columns), jnp.bfloat16),
            pltpu.SemaphoreType.DMA((n,)),
        ],
        cost=work(8 * length * width * columns, 2 * (3 * length * width + 4 * width * columns + 8 * length * columns)),
        name="mlp_pull",
    )(*pieces, mlp_full, both, hidden, unit)


def steps_of(part, parts):
    n = lax.axis_size(AXIS)
    return range((n - 1) * part // parts, (n - 1) * (part + 1) // parts)


def gather_hop(state, steps):
    for _ in steps[:-1]:
        up, down = state[-2:]
        state = [*state, lax.ppermute(up, AXIS, hops(True)), lax.ppermute(down, AXIS, hops(False))]
    return state, ("gather", steps[-1], *state[-2:]) if len(steps) else None


def scatter_hop(part, steps, sums=None):
    n, me = lax.axis_size(AXIS), lax.axis_index(AXIS)
    rows = part.shape[0] // n
    if sums is None:
        sums = [part[k * rows : (k + 1) * rows] for k in (n - 1, 1)] if len(steps) > 1 else [part]
    for t in steps[:-1]:
        came = [lax.ppermute(rows_out, AXIS, hops(way)) for rows_out, way in zip(sums, (True, False))]
        sums = [part[k * rows : (k + 1) * rows] + rows_in for k, rows_in in zip((n - 2 - t, 2 + t), came)]
    return ("scatter", steps[-1], *sums)


def shards(tokens,
    segment_ids,
    attn_gain,
    w_query,
    w_key,
    w_value,
    w_gate,
    w_out,
    mlp_gain,
    w_mlp_gate,
    w_mlp_up,
    w_down,
    cotangent,
):
    local_rows, width = tokens.shape
    heads = HEADS // lax.axis_size(AXIS)
    hidden_cols = w_mlp_gate.shape[1]
    after = lax.optimization_barrier

    def gather(own):
        return lax.all_gather(own, "dp", axis=0, tiled=True)

    def scatter(grad):
        return lax.psum_scatter(grad, "dp", scatter_dimension=0, tiled=True)

    def gain_terms(weights, grads):
        return jnp.sum(weights.astype(jnp.float32) * grads.astype(jnp.float32), axis=1)

    in_parts = [(array, head, columns) for head in range(heads) for array, columns in enumerate((KD, KD, VD, VD))]
    w_in_own = joined("join_in", [w_query, w_key, w_value, w_gate], attn_gain, in_parts)
    w_in = gather(w_in_own)
    (unit_one,) = line_pass("gather_one", None, [tokens], [], unit_step, True, 4, 0, local_rows, width)
    w_in, unit_one, w_out, cot_own = after((w_in, unit_one, w_out, cotangent))
    out_full = gather(w_out)
    cot, hop = gather_hop([cot_own, cot_own], steps_of(0, 3))
    projected, *came = project(unit_one, w_in, hop)
    cot, hop = gather_hop([*cot, *came], steps_of(1, 3))
    kept, mixed, mlp_own, *came = retention(
        projected, segment_ids, heads, hop, [w_mlp_gate, w_mlp_up, w_down, mlp_gain]
    )
    cot = [*cot, *came]
    mixed, out_full, mlp_send, *cot = after((mixed, out_full, mlp_own, *cot))
    mlp_full = gather(mlp_send)
    unit_two, residual, unit_turned = line_pass(
        "residual",
        (mixed, out_full),
        [tokens],
        [jnp.float32],
        residual_step,
        True,
        16,
        1,
        local_rows,
        width,
        (False, True),
        square=functools.partial(turn_parts, 8),
        square_ins=[unit_one],
        square_outs=[jax.ShapeDtypeStruct(unit_one.shape[::-1], unit_one.dtype)],
    )
    unit_two, mlp_full, *cot = after((unit_two, mlp_full, *cot))
    cot, hop = gather_hop(cot, steps_of(2, 3))
    both_hidden, hidden, part_down, *came = hidden_layer(unit_two, mlp_full, hop)
    hop = scatter_hop(part_down, steps_of(0, 3))
    d_pair, grad_mlp, *sums = mlp_pull([*cot, *came][1:], mlp_full, both_hidden, hidden, unit_two, hop, (part_down,))
    mlp_grad = scatter(grad_mlp)
    d_branch_one, d_residual = line_pass(
        "d_residual",
        (d_pair, mlp_full),
        [residual, cotangent],
        [jnp.float32],
        d_residual_step,
        True,
        16,
        2,
        local_rows,
        width,
        (True, False),
    )
    d_branch_one, d_residual, mlp_grad = after((d_branch_one, d_residual, mlp_grad))
    hop = scatter_hop(part_down, steps_of(1, 3), sums)
    grad_out, *sums = turned_dots([(d_branch_one, mixed)], hop, 10, (part_down,), "out_grads")
    out_grad = scatter(grad_out)
    hop = scatter_hop(part_down, steps_of(2, 3), sums)
    d_in, result = retention_pull(
        kept, projected, d_branch_one, out_full, segment_ids, heads, hop, (part_down, residual)
    )
    pair_grad, down_grad = mlp_grad[:, : 2 * hidden_cols], mlp_grad[:, 2 * hidden_cols :].astype(jnp.float32)
    terms_two = gain_terms(mlp_own[:, : 2 * hidden_cols], pair_grad)
    terms_two = jnp.broadcast_to(terms_two[:, None], (terms_two.shape[0], 128))
    pair_grad = pair_grad.astype(jnp.float32) * mlp_gain.astype(jnp.float32)[:, None]
    gate_grad, up_grad = pair_grad[:, :hidden_cols], pair_grad[:, hidden_cols:]
    d_in, result, gate_grad, up_grad, down_grad = after((d_in, result, gate_grad, up_grad, down_grad))
    square_outs, square_scratch = square_shapes(attn_gain.shape[0], heads, w_in.shape[1])
    tokens_grad, gain_sums, *in_grads = line_pass(
        "tokens_grad",
        (d_in, w_in),
        [tokens, d_residual],
        [jnp.bfloat16],
        tokens_step,
        False,
        8,
        3,
        local_rows,
        width,
        square=functools.partial(square_parts, heads),
        square_ins=[unit_turned, attn_gain, w_in_own, terms_two, mlp_gain],
        square_outs=square_outs,
        square_scratch=square_scratch,
    )
    gain_sum_one, gain_sum_two = gain_sums[0, 0], gain_sums[1, 0]
    return (
        result,
        tokens_grad,
        gain_sum_one,
        *in_grads,
        out_grad.astype(jnp.float32),
        gain_sum_two,
        gate_grad,
        up_grad,
        down_grad,
    )


def solution(mesh):
    return jax.shard_map(
        shards,
        mesh=mesh,
        in_specs=(
            P(("dp", "tensor"), None),
            P("dp", None),
            P("dp"),
            P("dp", "tensor"),
            P("dp", "tensor"),
            P("dp", "tensor"),
            P("dp", "tensor"),
            P("dp", "tensor"),
            P("dp"),
            P("dp", "tensor"),
            P("dp", "tensor"),
            P("dp", "tensor"),
            P(("dp", "tensor"), None),
        ),
        out_specs=(
            P(("dp", "tensor"), None),
            P(("dp", "tensor"), None),
            P("dp"),
            P("dp", "tensor"),
            P("dp", "tensor"),
            P("dp", "tensor"),
            P("dp", "tensor"),
            P("dp", "tensor"),
            P("dp"),
            P("dp", "tensor"),
            P("dp", "tensor"),
            P("dp", "tensor"),
        ),
        check_vma=False,
    )
```

```python
import functools
import math
import jax
import jax.numpy as jnp
import numpy as np
from jax import lax
from jax.experimental import pallas as pl
from jax.experimental.pallas import tpu as pltpu
from jax.sharding import PartitionSpec as P

AXIS = "tensor"
TALL = 256
COLUMNS = 1024
VMEM = 62 * 1024 * 1024


def line_body(n, chunks, rs, ag, rolled, middle, square, n_in, n_out, *refs):
    ins, outs, scratch = refs[:n_in], refs[n_in : n_in + n_out], list(refs[n_in + n_out :])
    me = lax.axis_index(AXIS)
    last = n - 1
    lag = last if rs else 0
    greet, also, finish, steps, early = lambda barrier: 0, lambda s: None, lambda: None, 0, False
    if rs:
        here, load_sems, left_sems, right_sems = scratch[:n_in], *scratch[n_in : n_in + 3]
        scratch = scratch[n_in + 3 :]
        outside, (left, right) = ins, here[:2]
        groups = left.shape[0] // TALL
        rows, tall, wide = left.shape[0] // n, left.shape[0] // n // groups, min(COLUMNS, right.shape[0])

        def left_copy(g, j):
            at = pl.ds(j * rows + g * tall, tall)
            return pltpu.make_async_copy(outside[0].at[at], left.at[at], left_sems.at[g, j])

        def right_copy(q):
            at = pl.ds(pl.multiple_of(q * wide, wide), wide)
            return pltpu.make_async_copy(outside[1].at[at, pl.ds(0, right.shape[1])], right.at[at], right_sems.at[q])

        def other_copy(i):
            return pltpu.make_async_copy(outside[i], here[i], load_sems.at[i])

        soon = n_in - square[1] if square is not None else n_in
        others = [i for i in range(2, n_in) if i != soon]

        def start_loads():
            starts = [left_copy(0, j) for j in range(n)]
            later = [left_copy(g, j) for g in range(1, groups) for j in range(n)]
            later += [other_copy(soon)] if soon < n_in else []
            tiles = [right_copy(q) for q in range(right.shape[0] // wide)]
            for copy in starts + (later + tiles if early else tiles + later) + [other_copy(i) for i in others]:
                copy.start()

        def wait_soon():
            for g in range(1, groups):
                for j in range(n):
                    left_copy(g, j).wait()
            if soon < n_in:
                other_copy(soon).wait()

        ins = here
    if square is not None:
        counts = square[1:]
        square_refs = ins[n_in - counts[0] :], outs[n_out - counts[1] :], scratch[len(scratch) - counts[2] :]
        ins, outs, scratch = ins[: n_in - counts[0]], outs[: n_out - counts[1]], scratch[: len(scratch) - counts[2]]
        greet, also, finish, steps, early = square[0](ins[0], *square_refs)
    if rs:
        start_loads()
        ins = ins[2:]
        part, up_buf, dn_buf, total, up_send, up_recv, dn_send, dn_recv = scratch[:8]
        scratch = scratch[8:]
    if ag:
        full, outs = outs[0], outs[1:]
        own, ag_recv, ag_up, ag_dn, ag_here = scratch[:5]
        rows = own.shape[0]
    size = rows // chunks

    def cut(c, base=0):
        return pl.ds(pl.multiple_of(base + c * size, size), size)

    def slot(j, device, turned):
        return lax.rem(j - device + n, n) if turned else j

    def product(g):
        block = jnp.concatenate([left[pl.ds(pl.multiple_of(j * rows + g * tall, tall), tall)] for j in range(n)], axis=0)

        def tile(q, _):
            @pl.when(g == 0)
            def _():
                right_copy(q).wait()

            columns = pl.ds(pl.multiple_of(q * wide, wide), wide)
            found = lax.dot_general(block, right[columns], (((1,), (1,)), ((), ())), preferred_element_type=jnp.float32)
            for j in range(n):
                part[pl.ds(pl.multiple_of(j * rows + g * tall, tall), tall), columns] = found[
                    j * tall : (j + 1) * tall
                ].astype(part.dtype)
            return 0

        lax.fori_loop(0, right.shape[0] // wide, tile, 0)

    def send(src, dst, send_sem, recv_sem, to):
        return pltpu.make_async_remote_copy(
            src_ref=src,
            dst_ref=dst,
            send_sem=send_sem,
            recv_sem=recv_sem,
            device_id={AXIS: to},
            device_id_type=pl.DeviceIdType.MESH,
        )

    barrier = pltpu.get_barrier_semaphore()

    @pl.when(me > 0)
    def _():
        pl.semaphore_signal(barrier, inc=1, device_id={AXIS: me - 1}, device_id_type=pl.DeviceIdType.MESH)

    @pl.when(me < last)
    def _():
        pl.semaphore_signal(barrier, inc=1, device_id={AXIS: me + 1}, device_id_type=pl.DeviceIdType.MESH)

    greeted = greet(barrier)
    pl.semaphore_wait(barrier, jnp.where((me > 0) & (me < last), 2, 1) + greeted)

    def sum_copy(up, d, c):
        buf, s, r, to = (up_buf, up_send, up_recv, me + 1) if up else (dn_buf, dn_send, dn_recv, me - 1)
        ref = buf.at[d - up, cut(c)]
        return send(ref, ref, s.at[d, c], r.at[d, c], to)

    def sum_step(up, d, c):
        buf = up_buf if up else dn_buf
        first = 0 if up else last
        mine = part[cut(c, slot(d, me, rolled[0]) * rows)]

        @pl.when(me == first)
        def _():
            buf[d - up, cut(c)] = mine

        @pl.when(me != first)
        def _():
            sum_copy(up, d, c).wait_recv()
            buf[d - up, cut(c)] += mine

        sum_copy(up, d, c).start()

    def gather_copy(up, j, c, from_own=False):
        to = me + 1 if up else me - 1
        src = own.at[cut(c)] if from_own else full.at[cut(c, slot(j, me, rolled[1]) * rows)]
        dst = full.at[cut(c, slot(j, to, rolled[1]) * rows)]
        return send(src, dst, (ag_up if up else ag_dn).at[j, c], ag_recv.at[j, c], to)

    def here_copy(c):
        return pltpu.make_async_copy(own.at[cut(c)], full.at[cut(c, slot(me, me, rolled[1]) * rows)], ag_here.at[c])

    def step(s, _):
        if rs:
            for up in (True, False):
                c = s - me if up else s - (last - me)
                for d in range(last, 0, -1) if up else range(last):

                    @pl.when((c >= 0) & (c < chunks) & ((me < d) if up else (me > d)))
                    def _(up=up, c=c, d=d):
                        sum_step(up, d, c)

            if not early:
                pl.when(s == 0)(wait_soon)

            @pl.when(s == 1)
            def _():
                for i in others:
                    other_copy(i).wait()

        also(s + 1 if early else s)
        if rs:
            per_group = chunks // groups

            @pl.when((lax.rem(s, per_group) == 0) & (s + per_group < chunks))
            def _():
                product(s // per_group + 1)

        c_own = s - lag

        @pl.when((c_own >= 0) & (c_own < chunks))
        def _():
            c = c_own
            if rs:
                total[...] = part[cut(c, slot(me, me, rolled[0]) * rows)].astype(jnp.float32)

                @pl.when(me > 0)
                def _():
                    sum_copy(True, me, c).wait_recv()
                    total[...] += up_buf[me - 1, cut(c)].astype(jnp.float32)

                @pl.when(me < last)
                def _():
                    sum_copy(False, me, c).wait_recv()
                    total[...] += dn_buf[me, cut(c)].astype(jnp.float32)

                result = middle(cut(c), total[...], ins, outs)
            else:
                result = middle(cut(c), None, ins, outs)
            if ag:
                own[cut(c)] = result.astype(own.dtype)
                here_copy(c).start()

                @pl.when(me < last)
                def _():
                    gather_copy(True, me, c, True).start()

                @pl.when(me > 0)
                def _():
                    gather_copy(False, me, c, True).start()

        if ag:
            for t in range(1, last):
                c = s - lag - t
                for up in (True, False):
                    j = me - t if up else me + t

                    @pl.when((c >= 0) & (c < chunks) & (((j >= 0) & (me < last)) if up else ((j <= last) & (me > 0))))
                    def _(up=up, c=c, j=j):
                        gather_copy(up, j, c).wait_recv()
                        gather_copy(up, j, c).start()

        return 0

    if rs:
        for j in range(n):
            left_copy(0, j).wait()
        if early:
            wait_soon()
            also(0)
        product(0)
    lax.fori_loop(0, max(chunks + lag + (last - 1 if ag else 0), steps - early), step, 0)
    finish()

    def drain(c, _):
        if rs:
            for d in range(1, n):

                @pl.when(me < d)
                def _(d=d):
                    sum_copy(True, d, c).wait_send()

            for d in range(last):

                @pl.when(me > d)
                def _(d=d):
                    sum_copy(False, d, c).wait_send()

        if ag:
            here_copy(c).wait()
            for j in range(n):

                @pl.when(((me == last) & (j < me)) | ((me == 0) & (j > me)))
                def _(j=j):
                    gather_copy(True, j, c).wait_recv()

                @pl.when((me < last) & (j <= me))
                def _(j=j):
                    gather_copy(True, j, c).wait_send()

                @pl.when((me > 0) & (j >= me))
                def _(j=j):
                    gather_copy(False, j, c).wait_send()

        return 0

    lax.fori_loop(0, chunks, drain, 0)


def line_pass(name, summed, extras, extra_outs, middle, ag, chunks, collective_id, rows, width, rolled=(False, False), square=None, square_ins=(), square_outs=(), square_scratch=()):
    n = lax.axis_size(AXIS)
    rs = summed is not None
    size = rows // chunks
    vmem = pl.BlockSpec(memory_space=pltpu.VMEM)
    operands = (list(summed) if rs else []) + list(extras) + list(square_ins)
    scratch = []
    sems = pltpu.SemaphoreType.DMA((n, chunks))
    if rs:
        depth = summed[0].shape[1]
        shapes = [(n * rows, depth), (width, depth)] + [operand.shape for operand in operands[2:]]
        scratch += [pltpu.VMEM(shape, operand.dtype) for shape, operand in zip(shapes, operands)]
        scratch += [
            pltpu.SemaphoreType.DMA((len(operands),)),
            pltpu.SemaphoreType.DMA((n * rows // TALL, n)),
            pltpu.SemaphoreType.DMA((width // min(COLUMNS, width),)),
            pltpu.VMEM((n * rows, width), jnp.bfloat16),
            pltpu.VMEM((n - 1, rows, width), jnp.bfloat16),
            pltpu.VMEM((n - 1, rows, width), jnp.bfloat16),
            pltpu.VMEM((size, width), jnp.float32),
            sems, sems, sems, sems,
        ]
    if ag:
        scratch += [pltpu.VMEM((rows, width), jnp.bfloat16), sems, sems, sems, pltpu.SemaphoreType.DMA((chunks,))]
    shapes = ([jax.ShapeDtypeStruct((n * rows, width), jnp.bfloat16)] if ag else []) + [
        jax.ShapeDtypeStruct((rows, width), kind) for kind in extra_outs
    ] + list(square_outs)
    specs = ([pl.BlockSpec(memory_space=pl.ANY)] if ag else []) + [vmem] * (len(extra_outs) + len(square_outs))
    if square is not None:
        square = (square, len(square_ins), len(square_outs), len(square_scratch))
    moved = rows * width * 2 * (n - 1)
    return pl.pallas_call(
        functools.partial(line_body, n, chunks, rs, ag, rolled, middle, square, len(operands), len(shapes)),
        out_shape=shapes,
        in_specs=[pl.BlockSpec(memory_space=pl.ANY) if rs else vmem] * len(operands),
        out_specs=specs,
        scratch_shapes=scratch + list(square_scratch),
        compiler_params=pltpu.CompilerParams(
            collective_id=collective_id, has_side_effects=True, vmem_limit_bytes=VMEM
        ),
        cost_estimate=pl.CostEstimate(
            flops=0, bytes_accessed=moved * 40, transcendentals=0, remote_bytes_transferred=moved
        ),
        name=name,
    )(*operands)


def flipped(index, bit):
    return index + (1 << bit) - 2 * (1 << bit) * lax.rem(index // (1 << bit), 2)


def square_parts(heads, left, ins, outs, scratch):
    turned, gain, weights, other_terms, other_gain = ins
    gain_sum, grads = outs[0], outs[1:]
    terms_one, sums, sums_in, sums_send, sums_recv, sent, *rest = scratch
    line = lax.axis_index(AXIS)
    line_bits = lax.axis_size(AXIS).bit_length() - 1
    size = lax.axis_size("dp")
    bits = size.bit_length() - 1
    arrived, sems = rest[:bits], rest[bits:]
    me = lax.axis_index("dp")
    rows, wide = sent.shape[-2:]
    half = wide // 2
    pairs = arrived[0].shape[0]
    orders = list(range(bits - 1)), list(range(bits - 1))[::-1]

    def greet(barrier):
        for bit in range(bits):
            pl.semaphore_signal(barrier, inc=1, device_id={"dp": flipped(me, bit)}, device_id_type=pl.DeviceIdType.MESH)
        for bit in range(line_bits):
            pl.semaphore_signal(barrier, inc=1, device_id={AXIS: flipped(line, bit)}, device_id_type=pl.DeviceIdType.MESH)
        return bits + line_bits

    def sums_copy(bit):
        return pltpu.make_async_remote_copy(
            src_ref=sums.at[bit],
            dst_ref=sums_in.at[bit],
            send_sem=sums_send.at[bit],
            recv_sem=sums_recv.at[bit],
            device_id={AXIS: flipped(line, bit)},
            device_id_type=pl.DeviceIdType.MESH,
        )

    def send(src, dst, send_sem, recv_sem, bit):
        return pltpu.make_async_remote_copy(
            src_ref=src,
            dst_ref=dst,
            send_sem=send_sem,
            recv_sem=recv_sem,
            device_id={"dp": flipped(me, bit)},
            device_id_type=pl.DeviceIdType.MESH,
        )

    def first_copy(p):
        return send(sent.at[lax.rem(p, 2)], arrived[0].at[p], sems[0].at[p], sems[1].at[p], 0)

    def places(side, stage, at):
        found = [slice(None)] * (bits - 1)
        for done in orders[side][: stage - 1]:
            found[done] = 0
        found[orders[side][stage - 1]] = at
        return tuple(found)

    def later_copy(p, side, stage):
        columns = (slice(None), pl.ds(side * half, half))
        return send(
            arrived[0].at[(p, *places(side, stage, 1), *columns)],
            arrived[stage].at[(p, *[slice(None)] * (bits - 1 - stage), *columns)],
            sems[2 * stage].at[p, side],
            sems[2 * stage + 1].at[p, side],
            orders[side][stage - 1] + 1,
        )

    def multiply(p, u, odd):
        owner = me
        for bit in range(bits):
            set_bit = odd if bit == 0 else u[bits - 1 - bit]
            if set_bit:
                owner = flipped(owner, bit)
        block = turned[pl.ds(pl.multiple_of(owner * rows, rows), rows)]
        columns = left[:, pl.ds(pl.multiple_of(p * wide, wide), wide)]
        return jnp.dot(block, columns, preferred_element_type=jnp.float32)

    blocks = [tuple(u >> bit & 1 for bit in range(bits - 1))[::-1] for u in range(size // 2)]

    def also(s):
        @pl.when(s < pairs)
        def _():
            p = s

            @pl.when(p >= 2)
            def _():
                first_copy(p - 2).wait_send()

            for u in blocks:
                sent[(lax.rem(p, 2), *u[::-1])] = multiply(p, u, 1).astype(sent.dtype)
            first_copy(p).start()

        for stage in range(1, bits + 1):

            @pl.when((s >= stage) & (s < pairs + stage))
            def _(stage=stage):
                p = s - stage
                if stage == 1:
                    first_copy(p).wait_recv()
                    for u in blocks:
                        at = (p, *u[::-1])
                        arrived[0][at] = (multiply(p, u, 0) + arrived[0][at].astype(jnp.float32)).astype(sent.dtype)
                for side in range(2):
                    columns = (slice(None), pl.ds(side * half, half))
                    if stage > 1:
                        later_copy(p, side, stage - 1).wait_recv()
                        at = (p, *places(side, stage - 1, 0), *columns)
                        came = (p, *[slice(None)] * (bits - stage), *columns)
                        if stage < bits:
                            arrived[0][at] += arrived[stage - 1][came]
                        else:
                            result(p, side, arrived[0][at].astype(jnp.float32) + arrived[stage - 1][came].astype(jnp.float32))
                    if stage < bits:
                        later_copy(p, side, stage).start()

        for bit in range(line_bits + 1):

            @pl.when(s == pairs + bits + bit)
            def _(bit=bit):
                if bit:
                    sums_copy(bit - 1).wait()
                    sums[bit] = sums[bit - 1] + sums_in[bit - 1]
                else:
                    sums[0, 0] = terms_one[...].T[: sums.shape[2]]
                    sums[0, 1] = other_terms[...].T[: sums.shape[2]]
                if bit < line_bits:
                    sums_copy(bit).start()
                else:
                    gain_sum[0] = sums[bit, 0] / as_row(gain)
                    gain_sum[1] = sums[bit, 1] / as_row(other_gain)

    def result(p, side, summed):
        at = pl.ds(pl.multiple_of(p * wide + side * half, half), half)
        terms = jnp.sum(summed * weights[:, at].astype(jnp.float32), axis=1, keepdims=True)
        terms = jnp.broadcast_to(terms, terms_one.shape)
        if side:
            terms_one[...] += terms
        else:

            @pl.when(p == 0)
            def _():
                terms_one[...] = terms

            @pl.when(p > 0)
            def _():
                terms_one[...] += terms

        summed = summed * as_column(as_row(gain))
        for found in range(pairs):
            head, kind = found // (pairs // heads), found % (pairs // heads)
            where = grads[side] if kind == 0 else grads[1 + kind]
            start = head * half if kind == 0 else head * wide + side * half

            @pl.when(p == found)
            def _(where=where, start=start):
                where[:, start : start + half] = summed

    def finish():
        for p in range(max(pairs - 2, 0), pairs):
            first_copy(p).wait_send()

        def drain(p, _):
            for side in range(2):
                for stage in range(1, bits):
                    later_copy(p, side, stage).wait_send()
            return 0

        lax.fori_loop(0, pairs, drain, 0)

    return greet, also, finish, pairs + bits + line_bits + 1, False


def square_shapes(rows, heads, columns):
    size = lax.axis_size("dp")
    bits = size.bit_length() - 1
    wide = 2 * KD
    pairs = columns // wide
    twos = [2] * (bits - 1)
    sums = [pltpu.VMEM((pairs, *twos[stage:], rows, wide), jnp.bfloat16) for stage in range(bits)]
    sems = [pltpu.SemaphoreType.DMA((pairs,))] * 2
    for _ in range(1, bits):
        sems += [pltpu.SemaphoreType.DMA((pairs, 2))] * 2
    outs = [jax.ShapeDtypeStruct((2, 8, rows), jnp.float32)]
    line_bits = lax.axis_size(AXIS).bit_length() - 1
    line_sems = pltpu.SemaphoreType.DMA((max(line_bits, 1),))
    line_scratch = [
        pltpu.VMEM((rows, 128), jnp.float32),
        pltpu.VMEM((line_bits + 1, 2, 8, rows), jnp.float32),
        pltpu.VMEM((max(line_bits, 1), 2, 8, rows), jnp.float32),
        line_sems,
        line_sems,
    ]
    outs += [jax.ShapeDtypeStruct((rows, heads * cols), jnp.float32) for cols in (KD, KD, VD, VD)]
    return outs, line_scratch + [pltpu.VMEM((2, *twos, rows, wide), jnp.bfloat16)] + sums + sems


def turn_parts(blocks, left, ins, outs, scratch):
    (rows_in,), (turned,) = ins, outs
    columns = rows_in.shape[1] // blocks

    def also(s):
        for block in range(blocks):

            @pl.when(s == block)
            def _(block=block):
                at = pl.ds(block * columns, columns)
                turned[at] = rows_in[:, at].T

    return lambda barrier: 0, also, lambda: None, blocks, False


HEADS = 8
KD = 256
VD = 512
ROWS = 256


EPS_NORM = 1e-06
EPS_GROUP = 1.0
CONTRACT_ROWS = (((0,), (0,)), ((), ()))
CONTRACT_COLUMNS = (((1,), (1,)), ((), ()))


def rotary_tables(length):
    positions = np.arange(length).astype(np.float32)[:, None]
    frequency = np.float32(10000.0) ** (-np.arange(KD // 2).astype(np.float32) * np.float32(2.0 / KD))
    angles = (positions * frequency[None, :]).astype(np.float32).astype(np.float64)
    return np.cos(angles).astype(np.float32), np.sin(angles).astype(np.float32)


def turn(rows, cosine, sine):
    low, high = rows[:, : KD // 2], rows[:, KD // 2 :]
    return jnp.concatenate([low * cosine - high * sine, high * cosine + low * sine], axis=1)


def dot(left, right, dims=(((1,), (0,)), ((), ()))):
    return lax.dot_general(left, right, dims, preferred_element_type=jnp.float32)


def head_decay(decay_ref, log_ref, heads, head, reach):
    ahead = lax.broadcasted_iota(jnp.int32, decay_ref.shape, 0) - lax.broadcasted_iota(jnp.int32, decay_ref.shape, 1)
    distance = ahead + reach
    mine = lax.axis_index(AXIS) * heads + head
    value = jnp.exp(log_ref[mine] * jnp.maximum(distance, 0).astype(jnp.float32))
    decay_ref[...] = jnp.where(distance >= 0, value, 0.0)


def normed_heads(heads_out):
    centred = heads_out - jnp.mean(heads_out, axis=-1, keepdims=True)
    inverse = lax.rsqrt(jnp.mean(centred * centred, axis=-1, keepdims=True) + EPS_GROUP)
    return centred * inverse, inverse


def retention_body(block, reach, log_ref, proj, cosine, sine, segments, *refs):
    *arrays, kept, mixed, joined, keys, vals, decay, seg_line = refs
    head, row = pl.program_id(0), pl.program_id(1)
    here = pl.ds(pl.multiple_of(reach + row * block, block), block)
    window = pl.ds(pl.multiple_of(row * block, block), reach + block)

    @pl.when((head == 0) & (row == 0))
    def _():
        joined_body([(i, 0, arrays[i].shape[1]) for i in range(len(arrays) - 1)], 1, *arrays, joined)

    @pl.when(row == 0)
    def _():
        head_decay(decay, log_ref, pl.num_programs(0), head, reach)
        keys[:reach] = jnp.zeros((reach, KD), keys.dtype)
        vals[:reach] = jnp.zeros((reach, VD), vals.dtype)
        seg_line[:, :reach] = jnp.full((1, reach), -1, jnp.int32)
        seg_line[:, reach:] = segments[...]

    query = turn(proj[:, :KD], cosine[...], sine[...]).astype(jnp.bfloat16)
    key = (turn(proj[:, KD : 2 * KD], cosine[...], sine[...]) * KD ** (-0.5)).astype(jnp.bfloat16)
    value = proj[:, 2 * KD : 2 * KD + VD].astype(jnp.bfloat16)
    keys[here] = key
    vals[here] = value
    kept[:, :KD] = query
    kept[:, KD : 2 * KD] = key
    kept[:, 2 * KD :] = value
    weight = jnp.where(as_column(seg_line[:, here]) == seg_line[:, window], decay[...], 0.0)
    probs = (dot(query, keys[window], CONTRACT_COLUMNS) * weight).astype(jnp.bfloat16)
    normed, _ = normed_heads(dot(probs, vals[window]))
    mixed[...] = (jax.nn.silu(proj[:, 2 * KD + VD :]) * normed).astype(jnp.bfloat16)


def retention_pull_body(
    block, reach, log_ref, kept, gate, d_branch, w_out, cosine, sine, segments, d_in, keys, vals, d_keys, d_vals, decay, seg_line
):
    head, row = pl.program_id(0), pl.num_programs(1) - 1 - pl.program_id(1)
    mine = pl.ds(pl.multiple_of(row * block, block), block)
    here = pl.ds(pl.multiple_of(reach + row * block, block), block)
    window = pl.ds(pl.multiple_of(row * block, block), reach + block)

    @pl.when(pl.program_id(1) == 0)
    def _():
        head_decay(decay, log_ref, pl.num_programs(0), head, reach)
        keys[:reach] = jnp.zeros((reach, KD), keys.dtype)
        vals[:reach] = jnp.zeros((reach, VD), vals.dtype)
        seg_line[:, :reach] = jnp.full((1, reach), -1, jnp.int32)
        seg_line[:, reach:] = segments[...]
        keys[reach:] = kept[:, KD : 2 * KD]
        vals[reach:] = kept[:, 2 * KD :]
        d_keys[...] = jnp.zeros_like(d_keys)
        d_vals[...] = jnp.zeros_like(d_vals)

    query = kept[mine, :KD]
    weight = jnp.where(as_column(seg_line[:, here]) == seg_line[:, window], decay[...], 0.0)
    probs = (dot(query, keys[window], CONTRACT_COLUMNS) * weight).astype(jnp.bfloat16)
    normed, inverse = normed_heads(dot(probs, vals[window]))
    gate_pre, upstream = gate[...], dot(d_branch[...], w_out[...])
    opened = jax.nn.sigmoid(gate_pre)
    silu = gate_pre * opened
    d_in[:, 2 * KD + VD :] = (upstream * normed * (opened + silu * (1.0 - opened))).astype(jnp.bfloat16)
    e = upstream * silu
    d_heads = e - jnp.mean(e, axis=-1, keepdims=True) - normed * jnp.mean(e * normed, axis=-1, keepdims=True)
    d_heads = (d_heads * inverse).astype(jnp.bfloat16)
    d_scores = (dot(d_heads, vals[window], CONTRACT_COLUMNS) * weight).astype(jnp.bfloat16)
    d_vals[window] += dot(probs, d_heads, CONTRACT_ROWS)
    d_keys[window] += dot(d_scores, query, CONTRACT_ROWS)
    d_query = dot(d_scores, keys[window])
    d_in[:, :KD] = turn(d_query, cosine[...], -sine[...]).astype(jnp.bfloat16)
    d_in[:, KD : 2 * KD] = (turn(d_keys[here], cosine[...], -sine[...]) * KD ** (-0.5)).astype(jnp.bfloat16)
    d_in[:, 2 * KD : 2 * KD + VD] = d_vals[here].astype(jnp.bfloat16)


def hop_valid(kind, t, device, up):
    last = lax.axis_size(AXIS) - 1
    passed = device if up else last - device
    inside = (passed >= 0) & (passed < last)
    return inside & ((passed >= t) if kind == "gather" else (passed <= t))


def hop_call(body, hop, collective_id, then=None, resident=(), *, grid, in_specs, out_specs, out_shape, scratch_shapes=(), cost, name):
    def params(**more):
        return pltpu.CompilerParams(vmem_limit_bytes=VMEM, **more)

    if hop is None:
        return pl.pallas_call(
            body,
            grid=grid,
            in_specs=in_specs,
            out_specs=out_specs,
            out_shape=out_shape,
            scratch_shapes=list(scratch_shapes),
            compiler_params=params(),
            cost_estimate=cost,
            name=name,
        )
    kind, t, *arrays = hop
    n = lax.axis_size(AXIS)
    n_in, n_out, n_sent = len(in_specs), len(out_specs), len(arrays)
    rows, width = arrays[0].shape[0] // (n if n_sent == 1 else 1), arrays[0].shape[1]
    shape = jax.ShapeDtypeStruct((rows, width), arrays[0].dtype)
    added = [] if then is None else list(then)
    n_got = 1 if len(added) == 2 else 2

    def with_hop(*refs):
        ins, sources, refs = refs[:n_in], refs[n_in : n_in + n_sent], refs[n_in + n_sent :]
        terms, outs, refs = refs[: len(added)], refs[len(added) : len(added) + n_out], refs[len(added) + n_out :]
        targets, (*scratch, send_sems, recv_sems, load_sems) = refs[:n_got], refs[n_got:]
        held, scratch = scratch[: len(resident)], scratch[len(resident) :]
        found = targets
        if added:
            *scratch, came, mine, mine_sems = scratch
            targets = [came.at[0], came.at[1]]
        if len(added) == 2:
            *scratch, kept, kept_sem = scratch
        me = lax.axis_index(AXIS)
        last = n - 1
        steps = [pl.program_id(i) for i in range(len(grid))]
        at_first = functools.reduce(jnp.logical_and, [step == 0 for step in steps])
        at_last = functools.reduce(jnp.logical_and, [step == size - 1 for step, size in zip(steps, grid)])

        def copy(way):
            source = sources[way] if n_sent == 2 else sources[0].at[pl.ds((1 if way else last) * rows, rows)]
            return pltpu.make_async_remote_copy(
                src_ref=source,
                dst_ref=targets[way],
                send_sem=send_sems.at[way],
                recv_sem=recv_sems.at[way],
                device_id={AXIS: me - 1 if way else me + 1},
                device_id_type=pl.DeviceIdType.MESH,
            )

        def term_copies():
            if not added:
                return []
            slots = [0] if len(added) == 2 else [last - t - 1, 2 + t]
            copies = [
                pltpu.make_async_copy(terms[0].at[pl.ds(slot * rows, rows)], mine.at[way], mine_sems.at[way])
                for way, slot in enumerate(slots)
            ]
            return copies + ([pltpu.make_async_copy(terms[1], kept, kept_sem)] if len(added) == 2 else [])

        @pl.when(at_first)
        def _():
            barrier = pltpu.get_barrier_semaphore()
            for way in range(2):

                @pl.when((me > 0) if way else (me < last))
                def _(way=way):
                    to = me - 1 if way else me + 1
                    pl.semaphore_signal(barrier, inc=1, device_id={AXIS: to}, device_id_type=pl.DeviceIdType.MESH)

            pl.semaphore_wait(barrier, jnp.where((me > 0) & (me < last), 2, 1))
            for way in range(2):

                @pl.when(hop_valid(kind, t, me, way == 0))
                def _(way=way):
                    copy(way).start()

            loads = [
                pltpu.make_async_copy(ins[i].at[:, pl.ds(column, ref.shape[1])], ref, load_sems.at[k])
                for k, (i, column, ref) in enumerate(zip(resident, columns, held))
            ]
            for load in loads:
                load.start()
            for term in term_copies():
                term.start()
            for load in loads:
                load.wait()

        inside = list(ins)
        for i, ref in zip(resident, held):
            inside[i] = ref
        body(*inside, *outs, *scratch)

        @pl.when(at_last)
        def _():
            for term in term_copies():
                term.wait()
            if len(added) == 1:
                for way in range(2):
                    found[way][...] = mine[way]
            if len(added) == 2:
                kept[...] += mine[0].astype(jnp.float32)
            for way in range(2):

                @pl.when(hop_valid(kind, t, me, way == 0))
                def _(way=way):
                    copy(way).wait_send()

                @pl.when(hop_valid(kind, t, me + 1 if way else me - 1, way == 0))
                def _(way=way):
                    copy(way).wait_recv()
                    if len(added) == 1:
                        found[way][...] += came[way]
                    if len(added) == 2:
                        kept[...] += came[way].astype(jnp.float32)

            if len(added) == 2:
                found[0][...] = kept[...].astype(shape.dtype)

    anywhere = pl.BlockSpec(memory_space=pl.ANY)
    blocks = [in_specs[i].block_shape for i in resident]
    columns = [in_specs[i].index_map(*[0] * len(grid))[1] * block[1] for i, block in zip(resident, blocks)]
    in_specs = [anywhere if i in resident else spec for i, spec in enumerate(in_specs)]
    got = pl.BlockSpec((rows, width), lambda *_: (0, 0)) if added else anywhere
    more = []
    if len(added) == 2:
        more += [pltpu.VMEM((rows, width), jnp.float32), pltpu.SemaphoreType.DMA]
    if added:
        more += [pltpu.VMEM((2, rows, width), shape.dtype)] * 2 + [pltpu.SemaphoreType.DMA((2,))]
    call = pl.pallas_call(
        with_hop,
        grid=grid,
        in_specs=[*in_specs, *[anywhere] * (n_sent + len(added))],
        out_specs=[*out_specs, *[got] * n_got],
        out_shape=[*out_shape, *[shape] * n_got],
        scratch_shapes=[
            *[pltpu.VMEM(block, jnp.bfloat16) for block in blocks],
            *scratch_shapes,
            *more,
            pltpu.SemaphoreType.DMA((2,)),
            pltpu.SemaphoreType.DMA((2,)),
            pltpu.SemaphoreType.DMA((max(len(blocks), 1),)),
        ],
        compiler_params=params(collective_id=collective_id, has_side_effects=True),
        cost_estimate=cost,
        name=name,
    )
    return lambda *operands: call(*operands, *arrays, *added)


def work(flops, moved):
    return pl.CostEstimate(flops=flops, bytes_accessed=moved, transcendentals=0)


def project_body(block, rows_in, weights, out):
    def part(q, _):
        at = pl.ds(pl.multiple_of(q * block, block), block)
        out[at] = dot(rows_in[at], weights[...])
        return 0

    lax.fori_loop(0, rows_in.shape[0] // block, part, 0)


def project(rows_in, weights, hop):
    length, depth = rows_in.shape
    columns = weights.shape[1]
    tile = min(512, columns)
    return hop_call(
        functools.partial(project_body, ROWS),
        hop,
        4,
        resident=(0,),
        grid=(columns // tile,),
        in_specs=[pl.BlockSpec((length, depth), lambda c: (0, 0)), pl.BlockSpec((depth, tile), lambda c: (0, c))],
        out_specs=[pl.BlockSpec((length, tile), lambda c: (0, c))],
        out_shape=[jax.ShapeDtypeStruct((length, columns), jnp.float32)],
        cost=work(2 * length * weights.size, 2 * rows_in.size + 2 * weights.size + 4 * length * columns),
        name="project",
    )(rows_in, weights)


def hidden_body(rows_in, w_pair, w_down, both, hidden, part):
    found = dot(rows_in[...], w_pair[...])
    both[...] = found
    columns = hidden.shape[1]
    hidden[...] = (jax.nn.gelu(found[:, :columns], approximate=True) * found[:, columns:]).astype(hidden.dtype)
    part[...] = dot(hidden[...], w_down[...], CONTRACT_COLUMNS).astype(part.dtype)


def hidden_layer(rows_in, mlp_full, hop):
    length, width = rows_in.shape
    columns = mlp_full.shape[1] // 3
    once = pl.Buffered(1)
    return hop_call(
        hidden_body,
        hop,
        6,
        resident=(1, 2),
        grid=(length // ROWS,),
        in_specs=[
            pl.BlockSpec((ROWS, width), lambda r: (r, 0)),
            pl.BlockSpec((width, 2 * columns), lambda r: (0, 0), pipeline_mode=once),
            pl.BlockSpec((width, columns), lambda r: (0, 2), pipeline_mode=once),
        ],
        out_specs=[
            pl.BlockSpec((ROWS, 2 * columns), lambda r: (r, 0)),
            pl.BlockSpec((ROWS, columns), lambda r: (r, 0)),
            pl.BlockSpec((ROWS, width), lambda r: (r, 0)),
        ],
        out_shape=[
            jax.ShapeDtypeStruct((length, 2 * columns), jnp.float32),
            jax.ShapeDtypeStruct((length, columns), jnp.bfloat16),
            jax.ShapeDtypeStruct((length, width), jnp.bfloat16),
        ],
        cost=work(6 * length * width * columns, 2 * mlp_full.size + 14 * length * columns),
        name="hidden_layer",
    )(rows_in, mlp_full, mlp_full)


def turned_body(*refs):
    *pairs, out = refs
    at = 0
    for left, right in zip(pairs[::2], pairs[1::2]):
        columns = right.shape[1]
        out[:, at : at + columns] = dot(left[...], right[...], CONTRACT_ROWS).astype(out.dtype)
        at += columns


def turned_dots(pairs, hop, collective_id, then, name):
    length, width = pairs[0][0].shape
    columns = sum(right.shape[1] for _, right in pairs)
    specs = []
    for _, right in pairs:
        specs.append(pl.BlockSpec((length, ROWS), lambda r: (0, r)))
        specs.append(pl.BlockSpec(right.shape, lambda r: (0, 0), pipeline_mode=pl.Buffered(1)))
    return hop_call(
        turned_body,
        hop,
        collective_id,
        then,
        tuple(range(1, 2 * len(pairs), 2)),
        grid=(width // ROWS,),
        in_specs=specs,
        out_specs=[pl.BlockSpec((ROWS, columns), lambda r: (r, 0))],
        out_shape=[jax.ShapeDtypeStruct((width, columns), jnp.bfloat16)],
        cost=work(2 * length * width * columns, 2 * (len(pairs) * length * width + length * columns + width * columns)),
        name=name,
    )(*[array for pair in pairs for array in pair])


def retention_inputs(segments):
    length = segments.shape[1]
    block = min(ROWS, length // 2)
    reach = length // 2
    log_decay = np.log(1.0 - 2.0 ** (-5.0 - np.arange(HEADS))).astype(np.float32)
    return block, reach, log_decay


def retention(projected, segments, heads, hop, to_join):
    length = projected.shape[0]
    block, reach, log_decay = retention_inputs(segments)
    cosine, sine = rotary_tables(length)
    per_head = projected.shape[1] // heads
    joined = (to_join[0].shape[0], sum(array.shape[1] for array in to_join[:-1]))
    table = pl.BlockSpec((block, KD // 2), lambda h, r: (r, 0))
    return hop_call(
        functools.partial(retention_body, block, reach),
        hop,
        5,
        resident=tuple(range(5, 4 + len(to_join))),
        grid=(heads, length // block),
        in_specs=[
            pl.BlockSpec(memory_space=pltpu.SMEM),
            pl.BlockSpec((block, per_head), lambda h, r: (r, h)),
            table,
            table,
            pl.BlockSpec(segments.shape, lambda h, r: (0, 0)),
            *[pl.BlockSpec(array.shape, lambda h, r: (0, 0)) for array in to_join[:-1]],
            pl.BlockSpec(to_join[-1].shape, lambda h, r: (0,)),
        ],
        out_specs=[
            pl.BlockSpec((block, 2 * KD + VD), lambda h, r: (r, h)),
            pl.BlockSpec((block, VD), lambda h, r: (r, h)),
            pl.BlockSpec(joined, lambda h, r: (0, 0)),
        ],
        out_shape=[
            jax.ShapeDtypeStruct((length, heads * (2 * KD + VD)), jnp.bfloat16),
            jax.ShapeDtypeStruct((length, heads * VD), jnp.bfloat16),
            jax.ShapeDtypeStruct(joined, jnp.bfloat16),
        ],
        scratch_shapes=[
            pltpu.VMEM((reach + length, KD), jnp.bfloat16),
            pltpu.VMEM((reach + length, VD), jnp.bfloat16),
            pltpu.VMEM((block, reach + block), jnp.float32),
            pltpu.VMEM((1, reach + length), jnp.int32),
        ],
        cost=work(2 * heads * length * (reach + block) * (KD + VD), projected.size * 6),
        name="retention",
    )(log_decay, projected, cosine, sine, segments, *to_join)


def retention_pull(kept, projected, d_branch, w_out, segments, heads, hop, then):
    length = kept.shape[0]
    block, reach, log_decay = retention_inputs(segments)
    cosine, sine = rotary_tables(length)
    per_head = projected.shape[1] // heads
    last = length // block - 1
    gate_block = per_head // VD
    table = pl.BlockSpec((block, KD // 2), lambda h, r: (last - r, 0))
    return hop_call(
        functools.partial(retention_pull_body, block, reach),
        hop,
        9,
        then,
        grid=(heads, last + 1),
        in_specs=[
            pl.BlockSpec(memory_space=pltpu.SMEM),
            pl.BlockSpec((length, 2 * KD + VD), lambda h, r: (0, h)),
            pl.BlockSpec((block, VD), lambda h, r: (last - r, gate_block * h + gate_block - 1)),
            pl.BlockSpec((block, d_branch.shape[1]), lambda h, r: (last - r, 0)),
            pl.BlockSpec((w_out.shape[0], VD), lambda h, r: (0, h)),
            table,
            table,
            pl.BlockSpec(segments.shape, lambda h, r: (0, 0)),
        ],
        out_specs=[pl.BlockSpec((block, per_head), lambda h, r: (last - r, h))],
        out_shape=[jax.ShapeDtypeStruct(projected.shape, jnp.bfloat16)],
        scratch_shapes=[
            pltpu.VMEM((reach + length, KD), jnp.bfloat16),
            pltpu.VMEM((reach + length, VD), jnp.bfloat16),
            pltpu.VMEM((reach + length, KD), jnp.float32),
            pltpu.VMEM((reach + length, VD), jnp.float32),
            pltpu.VMEM((block, reach + block), jnp.float32),
            pltpu.VMEM((1, reach + length), jnp.int32),
        ],
        cost=work(2 * heads * length * ((reach + block) * 3 * (KD + VD) + d_branch.shape[1] * VD), projected.size * 8),
        name="retention_pull",
    )(log_decay, kept, projected, d_branch, w_out, cosine, sine, segments)


def inverse_rms(rows):
    return lax.rsqrt(jnp.mean(rows * rows, axis=-1, keepdims=True) + EPS_NORM)


def norm_pull(unit, inverse, d_unit):
    return inverse * (d_unit - unit * jnp.mean(d_unit * unit, axis=-1, keepdims=True))


def unit_step(cut, summed, ins, outs):
    inputs = ins[0][cut].astype(jnp.float32)
    return inputs * inverse_rms(inputs)


def residual_step(cut, summed, ins, outs):
    residual = ins[0][cut].astype(jnp.float32) + summed
    outs[0][cut] = residual
    return residual * inverse_rms(residual)


def d_residual_step(cut, summed, ins, outs):
    residual = ins[0][cut]
    inverse = inverse_rms(residual)
    d_residual = ins[1][cut].astype(jnp.float32) + norm_pull(residual * inverse, inverse, summed)
    outs[0][cut] = d_residual
    return d_residual


def tokens_step(cut, summed, ins, outs):
    inputs = ins[0][cut].astype(jnp.float32)
    inverse = inverse_rms(inputs)
    grad = ins[1][cut] + norm_pull(inputs * inverse, inverse, summed)
    outs[0][cut] = grad.astype(outs[0].dtype)


def hops(up):
    n = lax.axis_size(AXIS)
    return [(i, i + 1) if up else (i + 1, i) for i in range(n - 1)]


def as_row(ref):
    return ref[...].astype(jnp.float32).reshape(1, -1)


def as_column(row):
    return jnp.broadcast_to(row, (128, row.shape[1])).T[:, :1]


def joined_body(parts, plain, *refs):
    *arrays, gain_row, out = refs
    gain = as_column(as_row(gain_row))
    at = 0
    for array, index, columns in parts:
        found = arrays[array][:, index * columns : (index + 1) * columns]
        if array < len(arrays) - plain:
            found = (found.astype(jnp.float32) * gain).astype(out.dtype)
        out[:, at : at + columns] = found
        at += columns


def joined(name, arrays, gain, parts, plain=0):
    columns = sum(part[2] for part in parts)
    return pl.pallas_call(
        functools.partial(joined_body, parts, plain),
        out_shape=jax.ShapeDtypeStruct((gain.shape[0], columns), arrays[0].dtype),
        compiler_params=pltpu.CompilerParams(vmem_limit_bytes=VMEM),
        name=name,
    )(*arrays, gain)


def mlp_pull_body(count, n, *refs):
    pieces, refs = refs[: 2 * n - 1], refs[2 * n - 1 :]
    w_down, both, hidden, unit, d_pair_out, grads, cotangent, d_pair, sems = refs
    ups, downs = pieces[:1] + pieces[1::2], pieces[:1] + pieces[2::2]
    step, me = pl.program_id(0), lax.axis_index(AXIS)
    columns = w_down.shape[1]
    rows = cotangent.shape[0] // n

    def load(k, source):
        return pltpu.make_async_copy(source, cotangent.at[pl.ds(k * rows, rows)], sems.at[k])

    @pl.when(step == 0)
    def _():
        load(0, ups[0]).start()
        for k in range(1, n):

            @pl.when(me + k < n)
            def _(k=k):
                load(k, downs[k]).start()

            @pl.when(me + k >= n)
            def _(k=k):
                load(k, ups[n - k]).start()

    for k in range(n):

        @pl.when(step == k * rows // ROWS)
        def _(k=k):
            load(k, ups[0]).wait()

    @pl.when(step < count)
    def _():
        mine = pl.ds(pl.multiple_of(step * ROWS, ROWS), ROWS)
        d_hidden = dot(cotangent[mine], w_down[...])
        gate, up = both[:, :columns], both[:, columns:]
        slope = math.sqrt(2.0 / math.pi)
        cubed = 0.044715 * gate * gate
        bent = jnp.tanh(slope * gate * (1.0 + cubed))
        half = 0.5 + 0.5 * bent
        d_gelu = half + 0.5 * gate * (1.0 - bent * bent) * slope * (1.0 + 3.0 * cubed)
        d_gate = (d_hidden * up * d_gelu).astype(d_pair.dtype)
        d_up = (d_hidden * gate * half).astype(d_pair.dtype)
        for out in (d_pair_out, d_pair.at[mine]):
            out[:, :columns] = d_gate
            out[:, columns:] = d_up

    @pl.when(step >= count)
    def _():
        at = pl.ds(pl.multiple_of((step - count) * ROWS, ROWS), ROWS)
        grads[:, : 2 * columns] = dot(unit[...], d_pair[...], CONTRACT_ROWS).astype(grads.dtype)
        grads[:, 2 * columns :] = dot(cotangent[:, at], hidden[...], CONTRACT_ROWS).astype(grads.dtype)


def mlp_pull(pieces, mlp_full, both, hidden, unit, hop, then):
    n = lax.axis_size(AXIS)
    length, width = unit.shape
    columns = hidden.shape[1]
    count = length // ROWS
    once = pl.Buffered(1)
    return hop_call(
        functools.partial(mlp_pull_body, count, n),
        hop,
        7,
        then,
        (len(pieces), len(pieces) + 2),
        grid=(count + width // ROWS,),
        in_specs=[pl.BlockSpec(memory_space=pl.ANY)] * len(pieces)
        + [
            pl.BlockSpec((width, columns), lambda i: (0, 2), pipeline_mode=once),
            pl.BlockSpec((ROWS, 2 * columns), lambda i: (jnp.minimum(i, count - 1), 0)),
            pl.BlockSpec((length, columns), lambda i: (0, 0), pipeline_mode=once),
            pl.BlockSpec((length, ROWS), lambda i: (0, jnp.maximum(i - count, 0))),
        ],
        out_specs=[
            pl.BlockSpec((ROWS, 2 * columns), lambda i: (jnp.minimum(i, count - 1), 0)),
            pl.BlockSpec((ROWS, 3 * columns), lambda i: (jnp.maximum(i - count, 0), 0)),
        ],
        out_shape=[
            jax.ShapeDtypeStruct((length, 2 * columns), jnp.bfloat16),
            jax.ShapeDtypeStruct((width, 3 * columns), jnp.bfloat16),
        ],
        scratch_shapes=[
            pltpu.VMEM((length, width), jnp.bfloat16),
            pltpu.VMEM((length, 2 * columns), jnp.bfloat16),
            pltpu.SemaphoreType.DMA((n,)),
        ],
        cost=work(8 * length * width * columns, 2 * (3 * length * width + 4 * width * columns + 8 * length * columns)),
        name="mlp_pull",
    )(*pieces, mlp_full, both, hidden, unit)


def steps_of(part, parts):
    n = lax.axis_size(AXIS)
    return range((n - 1) * part // parts, (n - 1) * (part + 1) // parts)


def gather_hop(state, steps):
    for _ in steps[:-1]:
        up, down = state[-2:]
        state = [*state, lax.ppermute(up, AXIS, hops(True)), lax.ppermute(down, AXIS, hops(False))]
    return state, ("gather", steps[-1], *state[-2:]) if len(steps) else None


def scatter_hop(part, steps, sums=None):
    n, me = lax.axis_size(AXIS), lax.axis_index(AXIS)
    rows = part.shape[0] // n
    if sums is None:
        sums = [part[k * rows : (k + 1) * rows] for k in (n - 1, 1)] if len(steps) > 1 else [part]
    for t in steps[:-1]:
        came = [lax.ppermute(rows_out, AXIS, hops(way)) for rows_out, way in zip(sums, (True, False))]
        sums = [part[k * rows : (k + 1) * rows] + rows_in for k, rows_in in zip((n - 2 - t, 2 + t), came)]
    return ("scatter", steps[-1], *sums)


def shards(tokens,
    segment_ids,
    attn_gain,
    w_query,
    w_key,
    w_value,
    w_gate,
    w_out,
    mlp_gain,
    w_mlp_gate,
    w_mlp_up,
    w_down,
    cotangent,
):
    local_rows, width = tokens.shape
    heads = HEADS // lax.axis_size(AXIS)
    hidden_cols = w_mlp_gate.shape[1]
    after = lax.optimization_barrier

    def gather(own):
        return lax.all_gather(own, "dp", axis=0, tiled=True)

    def scatter(grad):
        return lax.psum_scatter(grad, "dp", scatter_dimension=0, tiled=True)

    def gain_terms(weights, grads):
        return jnp.sum(weights.astype(jnp.float32) * grads.astype(jnp.float32), axis=1)

    in_parts = [(array, head, columns) for head in range(heads) for array, columns in enumerate((KD, KD, VD, VD))]
    w_in_own = joined("join_in", [w_query, w_key, w_value, w_gate], attn_gain, in_parts)
    w_in = gather(w_in_own)
    (unit_one,) = line_pass("gather_one", None, [tokens], [], unit_step, True, 4, 0, local_rows, width)
    w_in, unit_one, w_out, cot_own = after((w_in, unit_one, w_out, cotangent))
    out_full = gather(w_out)
    cot, hop = gather_hop([cot_own, cot_own], steps_of(0, 3))
    projected, *came = project(unit_one, w_in, hop)
    cot, hop = gather_hop([*cot, *came], steps_of(1, 3))
    kept, mixed, mlp_own, *came = retention(
        projected, segment_ids, heads, hop, [w_mlp_gate, w_mlp_up, w_down, mlp_gain]
    )
    cot = [*cot, *came]
    mixed, out_full, mlp_send, *cot = after((mixed, out_full, mlp_own, *cot))
    mlp_full = gather(mlp_send)
    unit_two, residual, unit_turned = line_pass(
        "residual",
        (mixed, out_full),
        [tokens],
        [jnp.float32],
        residual_step,
        True,
        16,
        1,
        local_rows,
        width,
        (False, True),
        square=functools.partial(turn_parts, 8),
        square_ins=[unit_one],
        square_outs=[jax.ShapeDtypeStruct(unit_one.shape[::-1], unit_one.dtype)],
    )
    unit_two, mlp_full, *cot = after((unit_two, mlp_full, *cot))
    cot, hop = gather_hop(cot, steps_of(2, 3))
    both_hidden, hidden, part_down, *came = hidden_layer(unit_two, mlp_full, hop)
    hop = scatter_hop(part_down, steps_of(0, 3))
    d_pair, grad_mlp, *sums = mlp_pull([*cot, *came][1:], mlp_full, both_hidden, hidden, unit_two, hop, (part_down,))
    mlp_grad = scatter(grad_mlp)
    d_branch_one, d_residual = line_pass(
        "d_residual",
        (d_pair, mlp_full),
        [residual, cotangent],
        [jnp.float32],
        d_residual_step,
        True,
        16,
        2,
        local_rows,
        width,
        (True, False),
    )
    d_branch_one, d_residual, mlp_grad = after((d_branch_one, d_residual, mlp_grad))
    hop = scatter_hop(part_down, steps_of(1, 3), sums)
    grad_out, *sums = turned_dots([(d_branch_one, mixed)], hop, 10, (part_down,), "out_grads")
    out_grad = scatter(grad_out)
    hop = scatter_hop(part_down, steps_of(2, 3), sums)
    d_in, result = retention_pull(
        kept, projected, d_branch_one, out_full, segment_ids, heads, hop, (part_down, residual)
    )
    pair_grad, down_grad = mlp_grad[:, : 2 * hidden_cols], mlp_grad[:, 2 * hidden_cols :].astype(jnp.float32)
    terms_two = gain_terms(mlp_own[:, : 2 * hidden_cols], pair_grad)
    terms_two = jnp.broadcast_to(terms_two[:, None], (terms_two.shape[0], 128))
    pair_grad = pair_grad.astype(jnp.float32) * mlp_gain.astype(jnp.float32)[:, None]
    gate_grad, up_grad = pair_grad[:, :hidden_cols], pair_grad[:, hidden_cols:]
    d_in, result, gate_grad, up_grad, down_grad = after((d_in, result, gate_grad, up_grad, down_grad))
    square_outs, square_scratch = square_shapes(attn_gain.shape[0], heads, w_in.shape[1])
    tokens_grad, gain_sums, *in_grads = line_pass(
        "tokens_grad",
        (d_in, w_in),
        [tokens, d_residual],
        [jnp.bfloat16],
        tokens_step,
        False,
        8,
        3,
        local_rows,
        width,
        square=functools.partial(square_parts, heads),
        square_ins=[unit_turned, attn_gain, w_in_own, terms_two, mlp_gain],
        square_outs=square_outs,
        square_scratch=square_scratch,
    )
    gain_sum_one, gain_sum_two = gain_sums[0, 0], gain_sums[1, 0]
    return (
        result,
        tokens_grad,
        gain_sum_one,
        *in_grads,
        out_grad.astype(jnp.float32),
        gain_sum_two,
        gate_grad,
        up_grad,
        down_grad,
    )


def solution(mesh):
    return jax.shard_map(
        shards,
        mesh=mesh,
        in_specs=(
            P(("dp", "tensor"), None),
            P("dp", None),
            P("dp"),
            P("dp", "tensor"),
            P("dp", "tensor"),
            P("dp", "tensor"),
            P("dp", "tensor"),
            P("dp", "tensor"),
            P("dp"),
            P("dp", "tensor"),
            P("dp", "tensor"),
            P("dp", "tensor"),
            P(("dp", "tensor"), None),
        ),
        out_specs=(
            P(("dp", "tensor"), None),
            P(("dp", "tensor"), None),
            P("dp"),
            P("dp", "tensor"),
            P("dp", "tensor"),
            P("dp", "tensor"),
            P("dp", "tensor"),
            P("dp", "tensor"),
            P("dp"),
            P("dp", "tensor"),
            P("dp", "tensor"),
            P("dp", "tensor"),
        ),
        check_vma=False,
    )
```

```python
import functools
import math
import jax
import jax.numpy as jnp
import numpy as np
from jax import lax
from jax.experimental import pallas as pl
from jax.experimental.pallas import tpu as pltpu
from jax.sharding import PartitionSpec as P

AXIS = "tensor"
TALL = 256
COLUMNS = 1024
VMEM = 62 * 1024 * 1024


def line_body(n, chunks, rs, ag, rolled, middle, square, n_in, n_out, *refs):
    ins, outs, scratch = refs[:n_in], refs[n_in : n_in + n_out], list(refs[n_in + n_out :])
    me = lax.axis_index(AXIS)
    last = n - 1
    lag = last if rs else 0
    greet, also, finish, steps, early = lambda barrier: 0, lambda s: None, lambda: None, 0, False
    if rs:
        here, load_sems, left_sems, right_sems = scratch[:n_in], *scratch[n_in : n_in + 3]
        scratch = scratch[n_in + 3 :]
        outside, (left, right) = ins, here[:2]
        groups = left.shape[0] // TALL
        rows, tall, wide = left.shape[0] // n, left.shape[0] // n // groups, min(COLUMNS, right.shape[0])

        def left_copy(g, j):
            at = pl.ds(j * rows + g * tall, tall)
            return pltpu.make_async_copy(outside[0].at[at], left.at[at], left_sems.at[g, j])

        def right_copy(q):
            at = pl.ds(pl.multiple_of(q * wide, wide), wide)
            return pltpu.make_async_copy(outside[1].at[at, pl.ds(0, right.shape[1])], right.at[at], right_sems.at[q])

        def other_copy(i):
            return pltpu.make_async_copy(outside[i], here[i], load_sems.at[i])

        soon = n_in - square[1] if square is not None else n_in
        others = [i for i in range(2, n_in) if i != soon]

        def start_loads():
            starts = [left_copy(0, j) for j in range(n)]
            later = [left_copy(g, j) for g in range(1, groups) for j in range(n)]
            later += [other_copy(soon)] if soon < n_in else []
            tiles = [right_copy(q) for q in range(right.shape[0] // wide)]
            for copy in starts + (later + tiles if early else tiles + later) + [other_copy(i) for i in others]:
                copy.start()

        def wait_soon():
            for g in range(1, groups):
                for j in range(n):
                    left_copy(g, j).wait()
            if soon < n_in:
                other_copy(soon).wait()

        ins = here
    if square is not None:
        counts = square[1:]
        square_refs = ins[n_in - counts[0] :], outs[n_out - counts[1] :], scratch[len(scratch) - counts[2] :]
        ins, outs, scratch = ins[: n_in - counts[0]], outs[: n_out - counts[1]], scratch[: len(scratch) - counts[2]]
        greet, also, finish, steps, early = square[0](ins[0], *square_refs)
    if rs:
        start_loads()
        ins = ins[2:]
        part, up_buf, dn_buf, total, up_send, up_recv, dn_send, dn_recv = scratch[:8]
        scratch = scratch[8:]
    if ag:
        full, outs = outs[0], outs[1:]
        own, ag_recv, ag_up, ag_dn, ag_here = scratch[:5]
        rows = own.shape[0]
    size = rows // chunks

    def cut(c, base=0):
        return pl.ds(pl.multiple_of(base + c * size, size), size)

    def slot(j, device, turned):
        return lax.rem(j - device + n, n) if turned else j

    def product(g):
        block = jnp.concatenate([left[pl.ds(pl.multiple_of(j * rows + g * tall, tall), tall)] for j in range(n)], axis=0)

        def tile(q, _):
            @pl.when(g == 0)
            def _():
                right_copy(q).wait()

            columns = pl.ds(pl.multiple_of(q * wide, wide), wide)
            found = lax.dot_general(block, right[columns], (((1,), (1,)), ((), ())), preferred_element_type=jnp.float32)
            for j in range(n):
                part[pl.ds(pl.multiple_of(j * rows + g * tall, tall), tall), columns] = found[
                    j * tall : (j + 1) * tall
                ].astype(part.dtype)
            return 0

        lax.fori_loop(0, right.shape[0] // wide, tile, 0)

    def send(src, dst, send_sem, recv_sem, to):
        return pltpu.make_async_remote_copy(
            src_ref=src,
            dst_ref=dst,
            send_sem=send_sem,
            recv_sem=recv_sem,
            device_id={AXIS: to},
            device_id_type=pl.DeviceIdType.MESH,
        )

    barrier = pltpu.get_barrier_semaphore()

    @pl.when(me > 0)
    def _():
        pl.semaphore_signal(barrier, inc=1, device_id={AXIS: me - 1}, device_id_type=pl.DeviceIdType.MESH)

    @pl.when(me < last)
    def _():
        pl.semaphore_signal(barrier, inc=1, device_id={AXIS: me + 1}, device_id_type=pl.DeviceIdType.MESH)

    greeted = greet(barrier)
    pl.semaphore_wait(barrier, jnp.where((me > 0) & (me < last), 2, 1) + greeted)

    def sum_copy(up, d, c):
        buf, s, r, to = (up_buf, up_send, up_recv, me + 1) if up else (dn_buf, dn_send, dn_recv, me - 1)
        ref = buf.at[d - up, cut(c)]
        return send(ref, ref, s.at[d, c], r.at[d, c], to)

    def sum_step(up, d, c):
        buf = up_buf if up else dn_buf
        first = 0 if up else last
        mine = part[cut(c, slot(d, me, rolled[0]) * rows)]

        @pl.when(me == first)
        def _():
            buf[d - up, cut(c)] = mine

        @pl.when(me != first)
        def _():
            sum_copy(up, d, c).wait_recv()
            buf[d - up, cut(c)] += mine

        sum_copy(up, d, c).start()

    def gather_copy(up, j, c, from_own=False):
        to = me + 1 if up else me - 1
        src = own.at[cut(c)] if from_own else full.at[cut(c, slot(j, me, rolled[1]) * rows)]
        dst = full.at[cut(c, slot(j, to, rolled[1]) * rows)]
        return send(src, dst, (ag_up if up else ag_dn).at[j, c], ag_recv.at[j, c], to)

    def here_copy(c):
        return pltpu.make_async_copy(own.at[cut(c)], full.at[cut(c, slot(me, me, rolled[1]) * rows)], ag_here.at[c])

    def step(s, _):
        if rs:
            for up in (True, False):
                c = s - me if up else s - (last - me)
                for d in range(last, 0, -1) if up else range(last):

                    @pl.when((c >= 0) & (c < chunks) & ((me < d) if up else (me > d)))
                    def _(up=up, c=c, d=d):
                        sum_step(up, d, c)

            if not early:
                pl.when(s == 0)(wait_soon)

            @pl.when(s == 1)
            def _():
                for i in others:
                    other_copy(i).wait()

        also(s + 1 if early else s)
        if rs:
            per_group = chunks // groups

            @pl.when((lax.rem(s, per_group) == 0) & (s + per_group < chunks))
            def _():
                product(s // per_group + 1)

        c_own = s - lag

        @pl.when((c_own >= 0) & (c_own < chunks))
        def _():
            c = c_own
            if rs:
                total[...] = part[cut(c, slot(me, me, rolled[0]) * rows)].astype(jnp.float32)

                @pl.when(me > 0)
                def _():
                    sum_copy(True, me, c).wait_recv()
                    total[...] += up_buf[me - 1, cut(c)].astype(jnp.float32)

                @pl.when(me < last)
                def _():
                    sum_copy(False, me, c).wait_recv()
                    total[...] += dn_buf[me, cut(c)].astype(jnp.float32)

                result = middle(cut(c), total[...], ins, outs)
            else:
                result = middle(cut(c), None, ins, outs)
            if ag:
                own[cut(c)] = result.astype(own.dtype)
                here_copy(c).start()

                @pl.when(me < last)
                def _():
                    gather_copy(True, me, c, True).start()

                @pl.when(me > 0)
                def _():
                    gather_copy(False, me, c, True).start()

        if ag:
            for t in range(1, last):
                c = s - lag - t
                for up in (True, False):
                    j = me - t if up else me + t

                    @pl.when((c >= 0) & (c < chunks) & (((j >= 0) & (me < last)) if up else ((j <= last) & (me > 0))))
                    def _(up=up, c=c, j=j):
                        gather_copy(up, j, c).wait_recv()
                        gather_copy(up, j, c).start()

        return 0

    if rs:
        for j in range(n):
            left_copy(0, j).wait()
        if early:
            wait_soon()
            also(0)
        product(0)
    lax.fori_loop(0, max(chunks + lag + (last - 1 if ag else 0), steps - early), step, 0)
    finish()

    def drain(c, _):
        if rs:
            for d in range(1, n):

                @pl.when(me < d)
                def _(d=d):
                    sum_copy(True, d, c).wait_send()

            for d in range(last):

                @pl.when(me > d)
                def _(d=d):
                    sum_copy(False, d, c).wait_send()

        if ag:
            here_copy(c).wait()
            for j in range(n):

                @pl.when(((me == last) & (j < me)) | ((me == 0) & (j > me)))
                def _(j=j):
                    gather_copy(True, j, c).wait_recv()

                @pl.when((me < last) & (j <= me))
                def _(j=j):
                    gather_copy(True, j, c).wait_send()

                @pl.when((me > 0) & (j >= me))
                def _(j=j):
                    gather_copy(False, j, c).wait_send()

        return 0

    lax.fori_loop(0, chunks, drain, 0)


def line_pass(name, summed, extras, extra_outs, middle, ag, chunks, collective_id, rows, width, rolled=(False, False), square=None, square_ins=(), square_outs=(), square_scratch=()):
    n = lax.axis_size(AXIS)
    rs = summed is not None
    size = rows // chunks
    vmem = pl.BlockSpec(memory_space=pltpu.VMEM)
    operands = (list(summed) if rs else []) + list(extras) + list(square_ins)
    scratch = []
    sems = pltpu.SemaphoreType.DMA((n, chunks))
    if rs:
        depth = summed[0].shape[1]
        shapes = [(n * rows, depth), (width, depth)] + [operand.shape for operand in operands[2:]]
        scratch += [pltpu.VMEM(shape, operand.dtype) for shape, operand in zip(shapes, operands)]
        scratch += [
            pltpu.SemaphoreType.DMA((len(operands),)),
            pltpu.SemaphoreType.DMA((n * rows // TALL, n)),
            pltpu.SemaphoreType.DMA((width // min(COLUMNS, width),)),
            pltpu.VMEM((n * rows, width), jnp.bfloat16),
            pltpu.VMEM((n - 1, rows, width), jnp.bfloat16),
            pltpu.VMEM((n - 1, rows, width), jnp.bfloat16),
            pltpu.VMEM((size, width), jnp.float32),
            sems, sems, sems, sems,
        ]
    if ag:
        scratch += [pltpu.VMEM((rows, width), jnp.bfloat16), sems, sems, sems, pltpu.SemaphoreType.DMA((chunks,))]
    shapes = ([jax.ShapeDtypeStruct((n * rows, width), jnp.bfloat16)] if ag else []) + [
        jax.ShapeDtypeStruct((rows, width), kind) for kind in extra_outs
    ] + list(square_outs)
    specs = ([pl.BlockSpec(memory_space=pl.ANY)] if ag else []) + [vmem] * (len(extra_outs) + len(square_outs))
    if square is not None:
        square = (square, len(square_ins), len(square_outs), len(square_scratch))
    moved = rows * width * 2 * (n - 1)
    return pl.pallas_call(
        functools.partial(line_body, n, chunks, rs, ag, rolled, middle, square, len(operands), len(shapes)),
        out_shape=shapes,
        in_specs=[pl.BlockSpec(memory_space=pl.ANY) if rs else vmem] * len(operands),
        out_specs=specs,
        scratch_shapes=scratch + list(square_scratch),
        compiler_params=pltpu.CompilerParams(
            collective_id=collective_id, has_side_effects=True, vmem_limit_bytes=VMEM
        ),
        cost_estimate=pl.CostEstimate(
            flops=0, bytes_accessed=moved * 40, transcendentals=0, remote_bytes_transferred=moved
        ),
        name=name,
    )(*operands)


def flipped(index, bit):
    return index + (1 << bit) - 2 * (1 << bit) * lax.rem(index // (1 << bit), 2)


def square_parts(heads, left, ins, outs, scratch):
    turned, gain, weights, other_terms, other_gain = ins
    gain_sum, grads = outs[0], outs[1:]
    terms_one, sums, sums_in, sums_send, sums_recv, sent, *rest = scratch
    line = lax.axis_index(AXIS)
    line_bits = lax.axis_size(AXIS).bit_length() - 1
    size = lax.axis_size("dp")
    bits = size.bit_length() - 1
    arrived, sems = rest[:bits], rest[bits:]
    me = lax.axis_index("dp")
    rows, wide = sent.shape[-2:]
    half = wide // 2
    pairs = arrived[0].shape[0]
    orders = list(range(bits - 1)), list(range(bits - 1))[::-1]

    def greet(barrier):
        for bit in range(bits):
            pl.semaphore_signal(barrier, inc=1, device_id={"dp": flipped(me, bit)}, device_id_type=pl.DeviceIdType.MESH)
        for bit in range(line_bits):
            pl.semaphore_signal(barrier, inc=1, device_id={AXIS: flipped(line, bit)}, device_id_type=pl.DeviceIdType.MESH)
        return bits + line_bits

    def sums_copy(bit):
        return pltpu.make_async_remote_copy(
            src_ref=sums.at[bit],
            dst_ref=sums_in.at[bit],
            send_sem=sums_send.at[bit],
            recv_sem=sums_recv.at[bit],
            device_id={AXIS: flipped(line, bit)},
            device_id_type=pl.DeviceIdType.MESH,
        )

    def send(src, dst, send_sem, recv_sem, bit):
        return pltpu.make_async_remote_copy(
            src_ref=src,
            dst_ref=dst,
            send_sem=send_sem,
            recv_sem=recv_sem,
            device_id={"dp": flipped(me, bit)},
            device_id_type=pl.DeviceIdType.MESH,
        )

    def first_copy(p):
        return send(sent.at[lax.rem(p, 2)], arrived[0].at[p], sems[0].at[p], sems[1].at[p], 0)

    def places(side, stage, at):
        found = [slice(None)] * (bits - 1)
        for done in orders[side][: stage - 1]:
            found[done] = 0
        found[orders[side][stage - 1]] = at
        return tuple(found)

    def later_copy(p, side, stage):
        columns = (slice(None), pl.ds(side * half, half))
        return send(
            arrived[0].at[(p, *places(side, stage, 1), *columns)],
            arrived[stage].at[(p, *[slice(None)] * (bits - 1 - stage), *columns)],
            sems[2 * stage].at[p, side],
            sems[2 * stage + 1].at[p, side],
            orders[side][stage - 1] + 1,
        )

    def multiply(p, u, odd):
        owner = me
        for bit in range(bits):
            set_bit = odd if bit == 0 else u[bits - 1 - bit]
            if set_bit:
                owner = flipped(owner, bit)
        block = turned[pl.ds(pl.multiple_of(owner * rows, rows), rows)]
        columns = left[:, pl.ds(pl.multiple_of(p * wide, wide), wide)]
        return jnp.dot(block, columns, preferred_element_type=jnp.float32)

    blocks = [tuple(u >> bit & 1 for bit in range(bits - 1))[::-1] for u in range(size // 2)]

    def also(s):
        @pl.when(s < pairs)
        def _():
            p = s

            @pl.when(p >= 2)
            def _():
                first_copy(p - 2).wait_send()

            for u in blocks:
                sent[(lax.rem(p, 2), *u[::-1])] = multiply(p, u, 1).astype(sent.dtype)
            first_copy(p).start()

        for stage in range(1, bits + 1):

            @pl.when((s >= stage) & (s < pairs + stage))
            def _(stage=stage):
                p = s - stage
                if stage == 1:
                    first_copy(p).wait_recv()
                    for u in blocks:
                        at = (p, *u[::-1])
                        arrived[0][at] = (multiply(p, u, 0) + arrived[0][at].astype(jnp.float32)).astype(sent.dtype)
                for side in range(2):
                    columns = (slice(None), pl.ds(side * half, half))
                    if stage > 1:
                        later_copy(p, side, stage - 1).wait_recv()
                        at = (p, *places(side, stage - 1, 0), *columns)
                        came = (p, *[slice(None)] * (bits - stage), *columns)
                        if stage < bits:
                            arrived[0][at] += arrived[stage - 1][came]
                        else:
                            result(p, side, arrived[0][at].astype(jnp.float32) + arrived[stage - 1][came].astype(jnp.float32))
                    if stage < bits:
                        later_copy(p, side, stage).start()

        for bit in range(line_bits + 1):

            @pl.when(s == pairs + bits + bit)
            def _(bit=bit):
                if bit:
                    sums_copy(bit - 1).wait()
                    sums[bit] = sums[bit - 1] + sums_in[bit - 1]
                else:
                    sums[0, 0] = terms_one[...].T[: sums.shape[2]]
                    sums[0, 1] = jnp.broadcast_to(as_row(other_terms), sums.shape[2:])
                if bit < line_bits:
                    sums_copy(bit).start()
                else:
                    gain_sum[0] = sums[bit, 0] / as_row(gain)
                    gain_sum[1] = sums[bit, 1] / as_row(other_gain)

    def result(p, side, summed):
        at = pl.ds(pl.multiple_of(p * wide + side * half, half), half)
        terms = jnp.sum(summed * weights[:, at].astype(jnp.float32), axis=1, keepdims=True)
        terms = jnp.broadcast_to(terms, terms_one.shape)
        if side:
            terms_one[...] += terms
        else:

            @pl.when(p == 0)
            def _():
                terms_one[...] = terms

            @pl.when(p > 0)
            def _():
                terms_one[...] += terms

        summed = summed * as_column(as_row(gain))
        for found in range(pairs):
            head, kind = found // (pairs // heads), found % (pairs // heads)
            where = grads[side] if kind == 0 else grads[1 + kind]
            start = head * half if kind == 0 else head * wide + side * half

            @pl.when(p == found)
            def _(where=where, start=start):
                where[:, start : start + half] = summed

    def finish():
        for p in range(max(pairs - 2, 0), pairs):
            first_copy(p).wait_send()

        def drain(p, _):
            for side in range(2):
                for stage in range(1, bits):
                    later_copy(p, side, stage).wait_send()
            return 0

        lax.fori_loop(0, pairs, drain, 0)

    return greet, also, finish, pairs + bits + line_bits + 1, False


def square_shapes(rows, heads, columns):
    size = lax.axis_size("dp")
    bits = size.bit_length() - 1
    wide = 2 * KD
    pairs = columns // wide
    twos = [2] * (bits - 1)
    sums = [pltpu.VMEM((pairs, *twos[stage:], rows, wide), jnp.bfloat16) for stage in range(bits)]
    sems = [pltpu.SemaphoreType.DMA((pairs,))] * 2
    for _ in range(1, bits):
        sems += [pltpu.SemaphoreType.DMA((pairs, 2))] * 2
    outs = [jax.ShapeDtypeStruct((2, 8, rows), jnp.float32)]
    line_bits = lax.axis_size(AXIS).bit_length() - 1
    line_sems = pltpu.SemaphoreType.DMA((max(line_bits, 1),))
    line_scratch = [
        pltpu.VMEM((rows, 128), jnp.float32),
        pltpu.VMEM((line_bits + 1, 2, 8, rows), jnp.float32),
        pltpu.VMEM((max(line_bits, 1), 2, 8, rows), jnp.float32),
        line_sems,
        line_sems,
    ]
    outs += [jax.ShapeDtypeStruct((rows, heads * cols), jnp.float32) for cols in (KD, KD, VD, VD)]
    return outs, line_scratch + [pltpu.VMEM((2, *twos, rows, wide), jnp.bfloat16)] + sums + sems


def turn_parts(blocks, left, ins, outs, scratch):
    (rows_in,), (turned,) = ins, outs
    columns = rows_in.shape[1] // blocks

    def also(s):
        for block in range(blocks):

            @pl.when(s == block)
            def _(block=block):
                at = pl.ds(block * columns, columns)
                turned[at] = rows_in[:, at].T

    return lambda barrier: 0, also, lambda: None, blocks, False


HEADS = 8
KD = 256
VD = 512
ROWS = 256


EPS_NORM = 1e-06
EPS_GROUP = 1.0
CONTRACT_ROWS = (((0,), (0,)), ((), ()))
CONTRACT_COLUMNS = (((1,), (1,)), ((), ()))


def rotary_tables(length):
    positions = np.arange(length).astype(np.float32)[:, None]
    frequency = np.float32(10000.0) ** (-np.arange(KD // 2).astype(np.float32) * np.float32(2.0 / KD))
    angles = (positions * frequency[None, :]).astype(np.float32).astype(np.float64)
    return np.cos(angles).astype(np.float32), np.sin(angles).astype(np.float32)


def turn(rows, cosine, sine):
    low, high = rows[:, : KD // 2], rows[:, KD // 2 :]
    return jnp.concatenate([low * cosine - high * sine, high * cosine + low * sine], axis=1)


def dot(left, right, dims=(((1,), (0,)), ((), ()))):
    return lax.dot_general(left, right, dims, preferred_element_type=jnp.float32)


def head_decay(decay_ref, log_ref, heads, head, reach):
    ahead = lax.broadcasted_iota(jnp.int32, decay_ref.shape, 0) - lax.broadcasted_iota(jnp.int32, decay_ref.shape, 1)
    distance = ahead + reach
    mine = lax.axis_index(AXIS) * heads + head
    value = jnp.exp(log_ref[mine] * jnp.maximum(distance, 0).astype(jnp.float32))
    decay_ref[...] = jnp.where(distance >= 0, value, 0.0)


def normed_heads(heads_out):
    centred = heads_out - jnp.mean(heads_out, axis=-1, keepdims=True)
    inverse = lax.rsqrt(jnp.mean(centred * centred, axis=-1, keepdims=True) + EPS_GROUP)
    return centred * inverse, inverse


def retention_body(block, reach, log_ref, proj, cosine, sine, segments, *refs):
    *arrays, kept, mixed, joined, keys, vals, decay, seg_line = refs
    head, row = pl.program_id(0), pl.program_id(1)
    here = pl.ds(pl.multiple_of(reach + row * block, block), block)
    window = pl.ds(pl.multiple_of(row * block, block), reach + block)

    @pl.when((head == 0) & (row == 0))
    def _():
        joined_body([(i, 0, arrays[i].shape[1]) for i in range(len(arrays) - 1)], 1, *arrays, joined)

    @pl.when(row == 0)
    def _():
        head_decay(decay, log_ref, pl.num_programs(0), head, reach)
        keys[:reach] = jnp.zeros((reach, KD), keys.dtype)
        vals[:reach] = jnp.zeros((reach, VD), vals.dtype)
        seg_line[:, :reach] = jnp.full((1, reach), -1, jnp.int32)
        seg_line[:, reach:] = segments[...]

    query = turn(proj[:, :KD], cosine[...], sine[...]).astype(jnp.bfloat16)
    key = (turn(proj[:, KD : 2 * KD], cosine[...], sine[...]) * KD ** (-0.5)).astype(jnp.bfloat16)
    value = proj[:, 2 * KD : 2 * KD + VD].astype(jnp.bfloat16)
    keys[here] = key
    vals[here] = value
    kept[:, :KD] = query
    kept[:, KD : 2 * KD] = key
    kept[:, 2 * KD :] = value
    weight = jnp.where(as_column(seg_line[:, here]) == seg_line[:, window], decay[...], 0.0)
    probs = (dot(query, keys[window], CONTRACT_COLUMNS) * weight).astype(jnp.bfloat16)
    normed, _ = normed_heads(dot(probs, vals[window]))
    mixed[...] = (jax.nn.silu(proj[:, 2 * KD + VD :]) * normed).astype(jnp.bfloat16)


def retention_pull_body(
    block, reach, log_ref, kept, gate, d_branch, w_out, cosine, sine, segments, d_in, keys, vals, d_keys, d_vals, decay, seg_line
):
    head, row = pl.program_id(0), pl.num_programs(1) - 1 - pl.program_id(1)
    mine = pl.ds(pl.multiple_of(row * block, block), block)
    here = pl.ds(pl.multiple_of(reach + row * block, block), block)
    window = pl.ds(pl.multiple_of(row * block, block), reach + block)

    @pl.when(pl.program_id(1) == 0)
    def _():
        head_decay(decay, log_ref, pl.num_programs(0), head, reach)
        keys[:reach] = jnp.zeros((reach, KD), keys.dtype)
        vals[:reach] = jnp.zeros((reach, VD), vals.dtype)
        seg_line[:, :reach] = jnp.full((1, reach), -1, jnp.int32)
        seg_line[:, reach:] = segments[...]
        keys[reach:] = kept[:, KD : 2 * KD]
        vals[reach:] = kept[:, 2 * KD :]
        d_keys[...] = jnp.zeros_like(d_keys)
        d_vals[...] = jnp.zeros_like(d_vals)

    query = kept[mine, :KD]
    weight = jnp.where(as_column(seg_line[:, here]) == seg_line[:, window], decay[...], 0.0)
    probs = (dot(query, keys[window], CONTRACT_COLUMNS) * weight).astype(jnp.bfloat16)
    normed, inverse = normed_heads(dot(probs, vals[window]))
    gate_pre, upstream = gate[...], dot(d_branch[...], w_out[...])
    opened = jax.nn.sigmoid(gate_pre)
    silu = gate_pre * opened
    d_in[:, 2 * KD + VD :] = (upstream * normed * (opened + silu * (1.0 - opened))).astype(jnp.bfloat16)
    e = upstream * silu
    d_heads = e - jnp.mean(e, axis=-1, keepdims=True) - normed * jnp.mean(e * normed, axis=-1, keepdims=True)
    d_heads = (d_heads * inverse).astype(jnp.bfloat16)
    d_scores = (dot(d_heads, vals[window], CONTRACT_COLUMNS) * weight).astype(jnp.bfloat16)
    d_vals[window] += dot(probs, d_heads, CONTRACT_ROWS)
    d_keys[window] += dot(d_scores, query, CONTRACT_ROWS)
    d_query = dot(d_scores, keys[window])
    d_in[:, :KD] = turn(d_query, cosine[...], -sine[...]).astype(jnp.bfloat16)
    d_in[:, KD : 2 * KD] = (turn(d_keys[here], cosine[...], -sine[...]) * KD ** (-0.5)).astype(jnp.bfloat16)
    d_in[:, 2 * KD : 2 * KD + VD] = d_vals[here].astype(jnp.bfloat16)


def hop_valid(kind, t, device, up):
    last = lax.axis_size(AXIS) - 1
    passed = device if up else last - device
    inside = (passed >= 0) & (passed < last)
    return inside & ((passed >= t) if kind == "gather" else (passed <= t))


def hop_call(body, hop, collective_id, then=None, resident=(), *, grid, in_specs, out_specs, out_shape, scratch_shapes=(), cost, name):
    def params(**more):
        return pltpu.CompilerParams(vmem_limit_bytes=VMEM, **more)

    if hop is None:
        return pl.pallas_call(
            body,
            grid=grid,
            in_specs=in_specs,
            out_specs=out_specs,
            out_shape=out_shape,
            scratch_shapes=list(scratch_shapes),
            compiler_params=params(),
            cost_estimate=cost,
            name=name,
        )
    kind, t, *arrays = hop
    n = lax.axis_size(AXIS)
    n_in, n_out, n_sent = len(in_specs), len(out_specs), len(arrays)
    rows, width = arrays[0].shape[0] // (n if n_sent == 1 else 1), arrays[0].shape[1]
    shape = jax.ShapeDtypeStruct((rows, width), arrays[0].dtype)
    added = [] if then is None else list(then)
    n_got = 1 if len(added) == 2 else 2

    def with_hop(*refs):
        ins, sources, refs = refs[:n_in], refs[n_in : n_in + n_sent], refs[n_in + n_sent :]
        terms, outs, refs = refs[: len(added)], refs[len(added) : len(added) + n_out], refs[len(added) + n_out :]
        targets, (*scratch, send_sems, recv_sems, load_sems) = refs[:n_got], refs[n_got:]
        held, scratch = scratch[: len(resident)], scratch[len(resident) :]
        found = targets
        if added:
            *scratch, came, mine, mine_sems = scratch
            targets = [came.at[0], came.at[1]]
        if len(added) == 2:
            *scratch, kept, kept_sem = scratch
        me = lax.axis_index(AXIS)
        last = n - 1
        steps = [pl.program_id(i) for i in range(len(grid))]
        at_first = functools.reduce(jnp.logical_and, [step == 0 for step in steps])
        at_last = functools.reduce(jnp.logical_and, [step == size - 1 for step, size in zip(steps, grid)])

        def copy(way):
            source = sources[way] if n_sent == 2 else sources[0].at[pl.ds((1 if way else last) * rows, rows)]
            return pltpu.make_async_remote_copy(
                src_ref=source,
                dst_ref=targets[way],
                send_sem=send_sems.at[way],
                recv_sem=recv_sems.at[way],
                device_id={AXIS: me - 1 if way else me + 1},
                device_id_type=pl.DeviceIdType.MESH,
            )

        def term_copies():
            if not added:
                return []
            slots = [0] if len(added) == 2 else [last - t - 1, 2 + t]
            copies = [
                pltpu.make_async_copy(terms[0].at[pl.ds(slot * rows, rows)], mine.at[way], mine_sems.at[way])
                for way, slot in enumerate(slots)
            ]
            return copies + ([pltpu.make_async_copy(terms[1], kept, kept_sem)] if len(added) == 2 else [])

        @pl.when(at_first)
        def _():
            barrier = pltpu.get_barrier_semaphore()
            for way in range(2):

                @pl.when((me > 0) if way else (me < last))
                def _(way=way):
                    to = me - 1 if way else me + 1
                    pl.semaphore_signal(barrier, inc=1, device_id={AXIS: to}, device_id_type=pl.DeviceIdType.MESH)

            pl.semaphore_wait(barrier, jnp.where((me > 0) & (me < last), 2, 1))
            for way in range(2):

                @pl.when(hop_valid(kind, t, me, way == 0))
                def _(way=way):
                    copy(way).start()

            loads = [
                pltpu.make_async_copy(ins[i].at[:, pl.ds(column, ref.shape[1])], ref, load_sems.at[k])
                for k, (i, column, ref) in enumerate(zip(resident, columns, held))
            ]
            for load in loads:
                load.start()
            for term in term_copies():
                term.start()
            for load in loads:
                load.wait()

        inside = list(ins)
        for i, ref in zip(resident, held):
            inside[i] = ref
        body(*inside, *outs, *scratch)

        @pl.when(at_last)
        def _():
            for term in term_copies():
                term.wait()
            if len(added) == 1:
                for way in range(2):
                    found[way][...] = mine[way]
            if len(added) == 2:
                kept[...] += mine[0].astype(jnp.float32)
            for way in range(2):

                @pl.when(hop_valid(kind, t, me, way == 0))
                def _(way=way):
                    copy(way).wait_send()

                @pl.when(hop_valid(kind, t, me + 1 if way else me - 1, way == 0))
                def _(way=way):
                    copy(way).wait_recv()
                    if len(added) == 1:
                        found[way][...] += came[way]
                    if len(added) == 2:
                        kept[...] += came[way].astype(jnp.float32)

            if len(added) == 2:
                found[0][...] = kept[...].astype(shape.dtype)

    anywhere = pl.BlockSpec(memory_space=pl.ANY)
    blocks = [in_specs[i].block_shape for i in resident]
    columns = [in_specs[i].index_map(*[0] * len(grid))[1] * block[1] for i, block in zip(resident, blocks)]
    in_specs = [anywhere if i in resident else spec for i, spec in enumerate(in_specs)]
    got = pl.BlockSpec((rows, width), lambda *_: (0, 0)) if added else anywhere
    more = []
    if len(added) == 2:
        more += [pltpu.VMEM((rows, width), jnp.float32), pltpu.SemaphoreType.DMA]
    if added:
        more += [pltpu.VMEM((2, rows, width), shape.dtype)] * 2 + [pltpu.SemaphoreType.DMA((2,))]
    call = pl.pallas_call(
        with_hop,
        grid=grid,
        in_specs=[*in_specs, *[anywhere] * (n_sent + len(added))],
        out_specs=[*out_specs, *[got] * n_got],
        out_shape=[*out_shape, *[shape] * n_got],
        scratch_shapes=[
            *[pltpu.VMEM(block, jnp.bfloat16) for block in blocks],
            *scratch_shapes,
            *more,
            pltpu.SemaphoreType.DMA((2,)),
            pltpu.SemaphoreType.DMA((2,)),
            pltpu.SemaphoreType.DMA((max(len(blocks), 1),)),
        ],
        compiler_params=params(collective_id=collective_id, has_side_effects=True),
        cost_estimate=cost,
        name=name,
    )
    return lambda *operands: call(*operands, *arrays, *added)


def work(flops, moved):
    return pl.CostEstimate(flops=flops, bytes_accessed=moved, transcendentals=0)


def project_body(block, rows_in, weights, out):
    def part(q, _):
        at = pl.ds(pl.multiple_of(q * block, block), block)
        out[at] = dot(rows_in[at], weights[...])
        return 0

    lax.fori_loop(0, rows_in.shape[0] // block, part, 0)


def project(rows_in, weights, hop):
    length, depth = rows_in.shape
    columns = weights.shape[1]
    tile = min(512, columns)
    return hop_call(
        functools.partial(project_body, ROWS),
        hop,
        4,
        resident=(0,),
        grid=(columns // tile,),
        in_specs=[pl.BlockSpec((length, depth), lambda c: (0, 0)), pl.BlockSpec((depth, tile), lambda c: (0, c))],
        out_specs=[pl.BlockSpec((length, tile), lambda c: (0, c))],
        out_shape=[jax.ShapeDtypeStruct((length, columns), jnp.float32)],
        cost=work(2 * length * weights.size, 2 * rows_in.size + 2 * weights.size + 4 * length * columns),
        name="project",
    )(rows_in, weights)


def hidden_body(rows_in, w_pair, w_down, both, hidden, part):
    found = dot(rows_in[...], w_pair[...])
    both[...] = found
    columns = hidden.shape[1]
    hidden[...] = (jax.nn.gelu(found[:, :columns], approximate=True) * found[:, columns:]).astype(hidden.dtype)
    part[...] = dot(hidden[...], w_down[...], CONTRACT_COLUMNS).astype(part.dtype)


def hidden_layer(rows_in, mlp_full, hop):
    length, width = rows_in.shape
    columns = mlp_full.shape[1] // 3
    once = pl.Buffered(1)
    return hop_call(
        hidden_body,
        hop,
        6,
        resident=(1, 2),
        grid=(length // ROWS,),
        in_specs=[
            pl.BlockSpec((ROWS, width), lambda r: (r, 0)),
            pl.BlockSpec((width, 2 * columns), lambda r: (0, 0), pipeline_mode=once),
            pl.BlockSpec((width, columns), lambda r: (0, 2), pipeline_mode=once),
        ],
        out_specs=[
            pl.BlockSpec((ROWS, 2 * columns), lambda r: (r, 0)),
            pl.BlockSpec((ROWS, columns), lambda r: (r, 0)),
            pl.BlockSpec((ROWS, width), lambda r: (r, 0)),
        ],
        out_shape=[
            jax.ShapeDtypeStruct((length, 2 * columns), jnp.float32),
            jax.ShapeDtypeStruct((length, columns), jnp.bfloat16),
            jax.ShapeDtypeStruct((length, width), jnp.bfloat16),
        ],
        cost=work(6 * length * width * columns, 2 * mlp_full.size + 14 * length * columns),
        name="hidden_layer",
    )(rows_in, mlp_full, mlp_full)


def turned_body(*refs):
    *pairs, out = refs
    at = 0
    for left, right in zip(pairs[::2], pairs[1::2]):
        columns = right.shape[1]
        out[:, at : at + columns] = dot(left[...], right[...], CONTRACT_ROWS).astype(out.dtype)
        at += columns


def turned_dots(pairs, hop, collective_id, then, name):
    length, width = pairs[0][0].shape
    columns = sum(right.shape[1] for _, right in pairs)
    specs = []
    for _, right in pairs:
        specs.append(pl.BlockSpec((length, ROWS), lambda r: (0, r)))
        specs.append(pl.BlockSpec(right.shape, lambda r: (0, 0), pipeline_mode=pl.Buffered(1)))
    return hop_call(
        turned_body,
        hop,
        collective_id,
        then,
        tuple(range(1, 2 * len(pairs), 2)),
        grid=(width // ROWS,),
        in_specs=specs,
        out_specs=[pl.BlockSpec((ROWS, columns), lambda r: (r, 0))],
        out_shape=[jax.ShapeDtypeStruct((width, columns), jnp.bfloat16)],
        cost=work(2 * length * width * columns, 2 * (len(pairs) * length * width + length * columns + width * columns)),
        name=name,
    )(*[array for pair in pairs for array in pair])


def retention_inputs(segments):
    length = segments.shape[1]
    block = min(ROWS, length // 2)
    reach = length // 2
    log_decay = np.log(1.0 - 2.0 ** (-5.0 - np.arange(HEADS))).astype(np.float32)
    return block, reach, log_decay


def retention(projected, segments, heads, hop, to_join):
    length = projected.shape[0]
    block, reach, log_decay = retention_inputs(segments)
    cosine, sine = rotary_tables(length)
    per_head = projected.shape[1] // heads
    joined = (to_join[0].shape[0], sum(array.shape[1] for array in to_join[:-1]))
    table = pl.BlockSpec((block, KD // 2), lambda h, r: (r, 0))
    return hop_call(
        functools.partial(retention_body, block, reach),
        hop,
        5,
        resident=tuple(range(5, 4 + len(to_join))),
        grid=(heads, length // block),
        in_specs=[
            pl.BlockSpec(memory_space=pltpu.SMEM),
            pl.BlockSpec((block, per_head), lambda h, r: (r, h)),
            table,
            table,
            pl.BlockSpec(segments.shape, lambda h, r: (0, 0)),
            *[pl.BlockSpec(array.shape, lambda h, r: (0, 0)) for array in to_join[:-1]],
            pl.BlockSpec(to_join[-1].shape, lambda h, r: (0,)),
        ],
        out_specs=[
            pl.BlockSpec((block, 2 * KD + VD), lambda h, r: (r, h)),
            pl.BlockSpec((block, VD), lambda h, r: (r, h)),
            pl.BlockSpec(joined, lambda h, r: (0, 0)),
        ],
        out_shape=[
            jax.ShapeDtypeStruct((length, heads * (2 * KD + VD)), jnp.bfloat16),
            jax.ShapeDtypeStruct((length, heads * VD), jnp.bfloat16),
            jax.ShapeDtypeStruct(joined, jnp.bfloat16),
        ],
        scratch_shapes=[
            pltpu.VMEM((reach + length, KD), jnp.bfloat16),
            pltpu.VMEM((reach + length, VD), jnp.bfloat16),
            pltpu.VMEM((block, reach + block), jnp.float32),
            pltpu.VMEM((1, reach + length), jnp.int32),
        ],
        cost=work(2 * heads * length * (reach + block) * (KD + VD), projected.size * 6),
        name="retention",
    )(log_decay, projected, cosine, sine, segments, *to_join)


def retention_pull(kept, projected, d_branch, w_out, segments, heads, hop, then):
    length = kept.shape[0]
    block, reach, log_decay = retention_inputs(segments)
    cosine, sine = rotary_tables(length)
    per_head = projected.shape[1] // heads
    last = length // block - 1
    gate_block = per_head // VD
    table = pl.BlockSpec((block, KD // 2), lambda h, r: (last - r, 0))
    return hop_call(
        functools.partial(retention_pull_body, block, reach),
        hop,
        9,
        then,
        grid=(heads, last + 1),
        in_specs=[
            pl.BlockSpec(memory_space=pltpu.SMEM),
            pl.BlockSpec((length, 2 * KD + VD), lambda h, r: (0, h)),
            pl.BlockSpec((block, VD), lambda h, r: (last - r, gate_block * h + gate_block - 1)),
            pl.BlockSpec((block, d_branch.shape[1]), lambda h, r: (last - r, 0)),
            pl.BlockSpec((w_out.shape[0], VD), lambda h, r: (0, h)),
            table,
            table,
            pl.BlockSpec(segments.shape, lambda h, r: (0, 0)),
        ],
        out_specs=[pl.BlockSpec((block, per_head), lambda h, r: (last - r, h))],
        out_shape=[jax.ShapeDtypeStruct(projected.shape, jnp.bfloat16)],
        scratch_shapes=[
            pltpu.VMEM((reach + length, KD), jnp.bfloat16),
            pltpu.VMEM((reach + length, VD), jnp.bfloat16),
            pltpu.VMEM((reach + length, KD), jnp.float32),
            pltpu.VMEM((reach + length, VD), jnp.float32),
            pltpu.VMEM((block, reach + block), jnp.float32),
            pltpu.VMEM((1, reach + length), jnp.int32),
        ],
        cost=work(2 * heads * length * ((reach + block) * 3 * (KD + VD) + d_branch.shape[1] * VD), projected.size * 8),
        name="retention_pull",
    )(log_decay, kept, projected, d_branch, w_out, cosine, sine, segments)


def inverse_rms(rows):
    return lax.rsqrt(jnp.mean(rows * rows, axis=-1, keepdims=True) + EPS_NORM)


def norm_pull(unit, inverse, d_unit):
    return inverse * (d_unit - unit * jnp.mean(d_unit * unit, axis=-1, keepdims=True))


def unit_step(cut, summed, ins, outs):
    inputs = ins[0][cut].astype(jnp.float32)
    return inputs * inverse_rms(inputs)


def residual_step(cut, summed, ins, outs):
    residual = ins[0][cut].astype(jnp.float32) + summed
    outs[0][cut] = residual
    return residual * inverse_rms(residual)


def d_residual_step(cut, summed, ins, outs):
    residual = ins[0][cut]
    inverse = inverse_rms(residual)
    d_residual = ins[1][cut].astype(jnp.float32) + norm_pull(residual * inverse, inverse, summed)
    outs[0][cut] = d_residual
    return d_residual


def tokens_step(cut, summed, ins, outs):
    inputs = ins[0][cut].astype(jnp.float32)
    inverse = inverse_rms(inputs)
    grad = ins[1][cut] + norm_pull(inputs * inverse, inverse, summed)
    outs[0][cut] = grad.astype(outs[0].dtype)


def hops(up):
    n = lax.axis_size(AXIS)
    return [(i, i + 1) if up else (i + 1, i) for i in range(n - 1)]


def as_row(ref):
    return ref[...].astype(jnp.float32).reshape(1, -1)


def as_column(row):
    return jnp.broadcast_to(row, (128, row.shape[1])).T[:, :1]


def joined_body(parts, plain, *refs):
    *arrays, gain_row, out = refs
    gain = as_column(as_row(gain_row))
    at = 0
    for array, index, columns in parts:
        found = arrays[array][:, index * columns : (index + 1) * columns]
        if array < len(arrays) - plain:
            found = (found.astype(jnp.float32) * gain).astype(out.dtype)
        out[:, at : at + columns] = found
        at += columns


def joined(name, arrays, gain, parts, plain=0):
    columns = sum(part[2] for part in parts)
    return pl.pallas_call(
        functools.partial(joined_body, parts, plain),
        out_shape=jax.ShapeDtypeStruct((gain.shape[0], columns), arrays[0].dtype),
        compiler_params=pltpu.CompilerParams(vmem_limit_bytes=VMEM),
        name=name,
    )(*arrays, gain)


def mlp_pull_body(count, n, *refs):
    pieces, refs = refs[: 2 * n - 1], refs[2 * n - 1 :]
    w_down, both, hidden, unit, d_pair_out, grads, cotangent, d_pair, sems = refs
    ups, downs = pieces[:1] + pieces[1::2], pieces[:1] + pieces[2::2]
    step, me = pl.program_id(0), lax.axis_index(AXIS)
    columns = w_down.shape[1]
    rows = cotangent.shape[0] // n

    def load(k, source):
        return pltpu.make_async_copy(source, cotangent.at[pl.ds(k * rows, rows)], sems.at[k])

    @pl.when(step == 0)
    def _():
        load(0, ups[0]).start()
        for k in range(1, n):

            @pl.when(me + k < n)
            def _(k=k):
                load(k, downs[k]).start()

            @pl.when(me + k >= n)
            def _(k=k):
                load(k, ups[n - k]).start()

    for k in range(n):

        @pl.when(step == k * rows // ROWS)
        def _(k=k):
            load(k, ups[0]).wait()

    @pl.when(step < count)
    def _():
        mine = pl.ds(pl.multiple_of(step * ROWS, ROWS), ROWS)
        d_hidden = dot(cotangent[mine], w_down[...])
        gate, up = both[:, :columns], both[:, columns:]
        slope = math.sqrt(2.0 / math.pi)
        cubed = 0.044715 * gate * gate
        bent = jnp.tanh(slope * gate * (1.0 + cubed))
        half = 0.5 + 0.5 * bent
        d_gelu = half + 0.5 * gate * (1.0 - bent * bent) * slope * (1.0 + 3.0 * cubed)
        d_gate = (d_hidden * up * d_gelu).astype(d_pair.dtype)
        d_up = (d_hidden * gate * half).astype(d_pair.dtype)
        for out in (d_pair_out, d_pair.at[mine]):
            out[:, :columns] = d_gate
            out[:, columns:] = d_up

    @pl.when(step >= count)
    def _():
        at = pl.ds(pl.multiple_of((step - count) * ROWS, ROWS), ROWS)
        grads[:, : 2 * columns] = dot(unit[...], d_pair[...], CONTRACT_ROWS).astype(grads.dtype)
        grads[:, 2 * columns :] = dot(cotangent[:, at], hidden[...], CONTRACT_ROWS).astype(grads.dtype)


def mlp_pull(pieces, mlp_full, both, hidden, unit, hop, then):
    n = lax.axis_size(AXIS)
    length, width = unit.shape
    columns = hidden.shape[1]
    count = length // ROWS
    once = pl.Buffered(1)
    return hop_call(
        functools.partial(mlp_pull_body, count, n),
        hop,
        7,
        then,
        (len(pieces), len(pieces) + 2),
        grid=(count + width // ROWS,),
        in_specs=[pl.BlockSpec(memory_space=pl.ANY)] * len(pieces)
        + [
            pl.BlockSpec((width, columns), lambda i: (0, 2), pipeline_mode=once),
            pl.BlockSpec((ROWS, 2 * columns), lambda i: (jnp.minimum(i, count - 1), 0)),
            pl.BlockSpec((length, columns), lambda i: (0, 0), pipeline_mode=once),
            pl.BlockSpec((length, ROWS), lambda i: (0, jnp.maximum(i - count, 0))),
        ],
        out_specs=[
            pl.BlockSpec((ROWS, 2 * columns), lambda i: (jnp.minimum(i, count - 1), 0)),
            pl.BlockSpec((ROWS, 3 * columns), lambda i: (jnp.maximum(i - count, 0), 0)),
        ],
        out_shape=[
            jax.ShapeDtypeStruct((length, 2 * columns), jnp.bfloat16),
            jax.ShapeDtypeStruct((width, 3 * columns), jnp.bfloat16),
        ],
        scratch_shapes=[
            pltpu.VMEM((length, width), jnp.bfloat16),
            pltpu.VMEM((length, 2 * columns), jnp.bfloat16),
            pltpu.SemaphoreType.DMA((n,)),
        ],
        cost=work(8 * length * width * columns, 2 * (3 * length * width + 4 * width * columns + 8 * length * columns)),
        name="mlp_pull",
    )(*pieces, mlp_full, both, hidden, unit)


def steps_of(part, parts):
    n = lax.axis_size(AXIS)
    return range((n - 1) * part // parts, (n - 1) * (part + 1) // parts)


def gather_hop(state, steps):
    for _ in steps[:-1]:
        up, down = state[-2:]
        state = [*state, lax.ppermute(up, AXIS, hops(True)), lax.ppermute(down, AXIS, hops(False))]
    return state, ("gather", steps[-1], *state[-2:]) if len(steps) else None


def scatter_hop(part, steps, sums=None):
    n, me = lax.axis_size(AXIS), lax.axis_index(AXIS)
    rows = part.shape[0] // n
    if sums is None:
        sums = [part[k * rows : (k + 1) * rows] for k in (n - 1, 1)] if len(steps) > 1 else [part]
    for t in steps[:-1]:
        came = [lax.ppermute(rows_out, AXIS, hops(way)) for rows_out, way in zip(sums, (True, False))]
        sums = [part[k * rows : (k + 1) * rows] + rows_in for k, rows_in in zip((n - 2 - t, 2 + t), came)]
    return ("scatter", steps[-1], *sums)


def shards(tokens,
    segment_ids,
    attn_gain,
    w_query,
    w_key,
    w_value,
    w_gate,
    w_out,
    mlp_gain,
    w_mlp_gate,
    w_mlp_up,
    w_down,
    cotangent,
):
    local_rows, width = tokens.shape
    heads = HEADS // lax.axis_size(AXIS)
    hidden_cols = w_mlp_gate.shape[1]
    after = lax.optimization_barrier

    def gather(own):
        return lax.all_gather(own, "dp", axis=0, tiled=True)

    def scatter(grad):
        return lax.psum_scatter(grad, "dp", scatter_dimension=0, tiled=True)

    def gain_terms(weights, grads):
        return jnp.sum(weights.astype(jnp.float32) * grads.astype(jnp.float32), axis=1)

    in_parts = [(array, head, columns) for head in range(heads) for array, columns in enumerate((KD, KD, VD, VD))]
    w_in_own = joined("join_in", [w_query, w_key, w_value, w_gate], attn_gain, in_parts)
    w_in = gather(w_in_own)
    (unit_one,) = line_pass("gather_one", None, [tokens], [], unit_step, True, 4, 0, local_rows, width)
    w_in, unit_one, w_out, cot_own = after((w_in, unit_one, w_out, cotangent))
    out_full = gather(w_out)
    cot, hop = gather_hop([cot_own, cot_own], steps_of(0, 3))
    projected, *came = project(unit_one, w_in, hop)
    cot, hop = gather_hop([*cot, *came], steps_of(1, 3))
    kept, mixed, mlp_own, *came = retention(
        projected, segment_ids, heads, hop, [w_mlp_gate, w_mlp_up, w_down, mlp_gain]
    )
    cot = [*cot, *came]
    mixed, out_full, mlp_send, *cot = after((mixed, out_full, mlp_own, *cot))
    mlp_full = gather(mlp_send)
    unit_two, residual, unit_turned = line_pass(
        "residual",
        (mixed, out_full),
        [tokens],
        [jnp.float32],
        residual_step,
        True,
        16,
        1,
        local_rows,
        width,
        (False, True),
        square=functools.partial(turn_parts, 8),
        square_ins=[unit_one],
        square_outs=[jax.ShapeDtypeStruct(unit_one.shape[::-1], unit_one.dtype)],
    )
    unit_two, mlp_full, *cot = after((unit_two, mlp_full, *cot))
    cot, hop = gather_hop(cot, steps_of(2, 3))
    both_hidden, hidden, part_down, *came = hidden_layer(unit_two, mlp_full, hop)
    hop = scatter_hop(part_down, steps_of(0, 3))
    d_pair, grad_mlp, *sums = mlp_pull([*cot, *came][1:], mlp_full, both_hidden, hidden, unit_two, hop, (part_down,))
    mlp_grad = scatter(grad_mlp)
    d_branch_one, d_residual = line_pass(
        "d_residual",
        (d_pair, mlp_full),
        [residual, cotangent],
        [jnp.float32],
        d_residual_step,
        True,
        16,
        2,
        local_rows,
        width,
        (True, False),
    )
    d_branch_one, d_residual, mlp_grad = after((d_branch_one, d_residual, mlp_grad))
    hop = scatter_hop(part_down, steps_of(1, 3), sums)
    grad_out, *sums = turned_dots([(d_branch_one, mixed)], hop, 10, (part_down,), "out_grads")
    out_grad = scatter(grad_out)
    hop = scatter_hop(part_down, steps_of(2, 3), sums)
    d_in, result = retention_pull(
        kept, projected, d_branch_one, out_full, segment_ids, heads, hop, (part_down, residual)
    )
    pair_grad, down_grad = mlp_grad[:, : 2 * hidden_cols], mlp_grad[:, 2 * hidden_cols :].astype(jnp.float32)
    terms_two = gain_terms(mlp_own[:, : 2 * hidden_cols], pair_grad)
    pair_grad = pair_grad.astype(jnp.float32) * mlp_gain.astype(jnp.float32)[:, None]
    gate_grad, up_grad = pair_grad[:, :hidden_cols], pair_grad[:, hidden_cols:]
    d_in, result, gate_grad, up_grad, down_grad = after((d_in, result, gate_grad, up_grad, down_grad))
    square_outs, square_scratch = square_shapes(attn_gain.shape[0], heads, w_in.shape[1])
    tokens_grad, gain_sums, *in_grads = line_pass(
        "tokens_grad",
        (d_in, w_in),
        [tokens, d_residual],
        [jnp.bfloat16],
        tokens_step,
        False,
        8,
        3,
        local_rows,
        width,
        square=functools.partial(square_parts, heads),
        square_ins=[unit_turned, attn_gain, w_in_own, terms_two, mlp_gain],
        square_outs=square_outs,
        square_scratch=square_scratch,
    )
    gain_sum_one, gain_sum_two = gain_sums[0, 0], gain_sums[1, 0]
    return (
        result,
        tokens_grad,
        gain_sum_one,
        *in_grads,
        out_grad.astype(jnp.float32),
        gain_sum_two,
        gate_grad,
        up_grad,
        down_grad,
    )


def solution(mesh):
    return jax.shard_map(
        shards,
        mesh=mesh,
        in_specs=(
            P(("dp", "tensor"), None),
            P("dp", None),
            P("dp"),
            P("dp", "tensor"),
            P("dp", "tensor"),
            P("dp", "tensor"),
            P("dp", "tensor"),
            P("dp", "tensor"),
            P("dp"),
            P("dp", "tensor"),
            P("dp", "tensor"),
            P("dp", "tensor"),
            P(("dp", "tensor"), None),
        ),
        out_specs=(
            P(("dp", "tensor"), None),
            P(("dp", "tensor"), None),
            P("dp"),
            P("dp", "tensor"),
            P("dp", "tensor"),
            P("dp", "tensor"),
            P("dp", "tensor"),
            P("dp", "tensor"),
            P("dp"),
            P("dp", "tensor"),
            P("dp", "tensor"),
            P("dp", "tensor"),
        ),
        check_vma=False,
    )
```
